128 devices in a mesh: row: 4 (over x), col: 32 (over z, y, core).
Axes of the slice: x: 4, y: 4, z: 4, core: 2. Of those that a mesh axis runs over, the one named last changes fastest.
Arguments:
- shot_dose: float32 [4096, 128], P(('row', 'col')), may hold values from 0.5 to 1.5
- shot_frac: float32 [2, 4096, 128], P(None, ('row', 'col')), may hold values from 0 to 1
- shot_pos: int32 [4096, 128], P(('row', 'col')), may hold values from 0 to 262143
- block_count: int32 [4096], P(('row', 'col')), may hold values from 32 to 128, as said below
- shot_tile: int32 [4096, 1], P(('row', 'col')), may hold values from 0 to 31; in each aligned block of 32 rows (0 to 31, 32 to 63, ...) at most 2 rows name the same one
- zone: int32 [16, 512], P('row', 'col'), may hold values from 0 to 7
- zone_weights: float32 [8, 3], replicated, may hold values from 0.2 to 2
- target: float32 [1024, 32768], P('row', 'col'), may hold values from -0.6 to 0.6
Outputs:
- exposure: float32 [1024, 32768], P('row', 'col')
- shot_grad: float32 [4096, 128], P(('row', 'col'))
The draws below stay inside these ranges and needn't reach their ends.
Inputs may be any that keep to these rules, and one draw needn't show every extreme that they name: block_count reaches 128 in at least one block of every device. `shot_tile`: within the 32 blocks of one device no tile column is named more than 2 times.
All inputs are finite; a program needn't handle non-finite values.
Results may differ from the reference program's by a relative error of at most 0.0001.
Values sent between devices are 32-bit elements; how exact they have to be, the bound alone decides.
A program may use at most 64 MiB of HBM per device.

```python
import math
import jax
import jax.numpy as jnp
import numpy as np
from jax import lax

TILE_R = 256
TILE_C = 1024
NB_DEV = 32
BS = 128
HALO = 64
ZONES = 8
CAP = 2
BLOCKS = 4096
NX = 1024
NY = 32768
N_COL = 32


def draw_block_count(key, part):
    first_key, second_key = jax.random.split(jax.random.fold_in(key, 11))
    groups = BLOCKS // NB_DEV
    counts = jax.random.randint(first_key, (groups, NB_DEV), BS // 4, BS + 1)
    chosen = jax.random.randint(second_key, (groups, 1), 0, NB_DEV)
    filled = jnp.where(jnp.arange(NB_DEV)[None, :] == chosen, BS, counts)
    return filled.reshape(BLOCKS).astype(jnp.int32)


def place_ends(result, stream_key, smallest, top_value):
    longest = result.shape.index(max(result.shape))
    spots = []
    for shift in (0, 1):
        where = [jax.random.randint(jax.random.fold_in(stream_key, axis), (), 0, length) for axis, length in enumerate(result.shape)]
        where[longest] = (where[longest] + shift) % result.shape[longest]
        spots.append(tuple(where))
    return result.at[spots[0]].set(smallest).at[spots[1]].set(top_value)


def level_of(stream_key, dims, cuts, smallest, top_value):
    def one(dim, parts):
        draws = jax.random.uniform(jax.random.fold_in(jax.random.fold_in(stream_key, 6), dim), (parts,), jnp.float32, smallest / len(cuts), top_value / len(cuts))
        return jnp.repeat(jnp.exp(draws), dims[dim] // parts).reshape((-1,) + (1,) * (len(dims) - dim - 1))

    factor_of = one(*cuts[0])
    for cut in cuts[1:]:
        factor_of = factor_of * one(*cut)
    return factor_of


def assign_block(rng, own, number, rows, number_of, top, reach, lean):
    ranking = jax.random.permutation(rng, number_of)
    packed, ordinary = load_shares(number_of, rows * top, reach, lean, True), load_shares(number_of, rows * top, reach, lean, False)
    places = jnp.arange(number_of)

    def named(tallies, turn):
        used = int((tallies > 0).sum())
        fixed = max(1, used // 4)
        passed = fixed + (places - fixed + turn * (used - fixed)) % max(1, number_of - fixed)
        return jnp.zeros((number_of,), jnp.int32).at[ranking[jnp.where(places < fixed, places, passed)]].set(jnp.asarray(tallies, jnp.int32))

    tallies = jnp.where(number % 4 == 0, named(packed, number // 4), named(ordinary, number - number // 4 - 1))
    mixed = jax.random.permutation(jax.random.fold_in(own, 3), number_of)
    donor, receiver = mixed[0:number_of // 2 * 2:2], mixed[1:number_of // 2 * 2:2]
    margin = jnp.minimum(tallies[donor] - 1, reach - tallies[receiver]) // 2
    margin = jnp.where((donor == ranking[0]) | (receiver == ranking[0]) | (tallies[receiver] == 0), 0, jnp.maximum(margin, 0))
    passed = jax.random.randint(jax.random.fold_in(own, 4), (number_of // 2,), 0, 1 << 20) % (margin + 1)
    tallies = tallies.at[donor].add(-passed).at[receiver].add(passed)
    labels = jnp.searchsorted(jnp.cumsum(tallies), jnp.arange(rows * top), side="right").astype(jnp.int32)
    grid = labels.reshape(top, rows).T
    grid = grid[jax.random.permutation(jax.random.fold_in(own, 1), rows)]
    turn = jax.random.randint(jax.random.fold_in(own, 2), (rows, 1), 0, top)
    return jnp.take_along_axis(grid, (jnp.arange(top)[None, :] + turn) % top, axis=1)


def load_shares(count, total, bound, slope, full):
    loads = [(1 << 20) // math.isqrt(grade ** slope) + 1 for grade in range(1, count + 1)]
    largest = bound if full else min(bound, max(-(-total // count), total * loads[0] // sum(loads)))
    least = 1 if total - largest >= count - 1 else 0
    given, spare = [largest] + [least] * (count - 1), total - largest - least * (count - 1)
    while spare > 0:
        candidates = [i for i in range(1, count) if given[i] < largest] or [i for i in range(1, count) if given[i] < bound]
        whole, budget = sum([loads[i] for i in candidates]), spare
        for i in candidates:
            extra = min(bound - given[i], max(1, budget * loads[i] // whole), spare)
            given[i] = given[i] + extra
            spare = spare - extra
    return np.array(given)


def gaussian(stream_key, extent, scale, most, pieces=(), held_as=jnp.bfloat16):
    entries = jax.random.normal(stream_key, extent, jnp.float32) * scale
    if len(pieces) > 0:
        entries = level_of(stream_key, extent, pieces, -0.22, 0.18) * entries
    return jnp.clip(entries, min=-most, max=most).astype(held_as)


def setup_inputs(seed: int = 0) -> dict:
    seeds = jax.random.split(jax.random.key(seed), 9)
    shot_dose = jnp.clip(0.5 + 1.0 * jax.random.uniform(seeds[0], (BLOCKS, BS), jnp.float32) ** level_of(seeds[0], (BLOCKS, BS), ((0, 128),), -0.2, 0.2), 0.5, 1.5)
    shot_frac = jnp.clip(1.0 * jax.random.uniform(seeds[1], (2, BLOCKS, BS), jnp.float32) ** level_of(seeds[1], (2, BLOCKS, BS), ((1, 128),), -0.2, 0.2), 0.0, 1.0)
    shot_pos = place_ends(jax.random.randint(seeds[2], (BLOCKS, BS), 0, TILE_R * TILE_C), jax.random.fold_in(seeds[2], 1), 0, (TILE_R * TILE_C) - 1).astype(jnp.int32)
    block_count = draw_block_count(jax.random.fold_in(seeds[8], 71), 0)
    shot_tile_keys = jax.random.split(jax.random.fold_in(seeds[4], 1), BLOCKS // NB_DEV)
    shot_tile_turns = jax.random.permutation(jax.random.fold_in(seeds[4], 3), BLOCKS // NB_DEV)
    shot_tile = jax.vmap(lambda own, number: assign_block(jax.random.fold_in(seeds[4], 2), own, number, NB_DEV, N_COL, 1, CAP, 2))(shot_tile_keys, shot_tile_turns).reshape((BLOCKS, 1))
    zone = place_ends(jax.random.randint(seeds[5], (NX // HALO, NY // HALO), 0, ZONES), jax.random.fold_in(seeds[5], 1), 0, ZONES - 1).astype(jnp.int32)
    zone_weights = jnp.clip(jnp.exp(jax.random.uniform(seeds[6], (ZONES, 3), jnp.float32, math.log(0.2), math.log(2.0))), 0.2, 2.0)
    target = gaussian(seeds[7], (NX, NY), 0.1, 0.6, ((0, 4), (1, 32)), jnp.float32)
    return {"shot_dose": shot_dose, "shot_frac": shot_frac, "shot_pos": shot_pos, "block_count": block_count, "shot_tile": shot_tile, "zone": zone, "zone_weights": zone_weights, "target": target}


sigma_parts = (0.125, 0.25, 0.5)


def kernel_taps(sigma):
    offsets = jnp.arange(-HALO, HALO + 1).astype(jnp.float32)
    values = jnp.exp(-offsets * offsets / (2.0 * sigma * sigma))
    return values / jnp.sum(values)


def blur_field(field, sigma):
    taps = kernel_taps(sigma)
    along_rows = lax.conv_general_dilated(field[None, None], taps[None, None, :, None], (1, 1), [(HALO, HALO), (0, 0)], precision=lax.Precision.HIGHEST)
    along_cols = lax.conv_general_dilated(along_rows, taps[None, None, None, :], (1, 1), [(0, 0), (HALO, HALO)], precision=lax.Precision.HIGHEST)
    return along_cols[0, 0]


def reference(shot_dose, shot_frac, shot_pos, block_count, shot_tile, zone, zone_weights, target):
    block_ids = jnp.arange(BLOCKS).astype(jnp.int32)
    tile_row = (block_ids // NB_DEV) // N_COL
    slots = jnp.arange(BS).astype(jnp.int32)
    live = (slots[None, :] < block_count[:, None]).astype(jnp.float32)
    local_row = jnp.minimum(shot_pos // TILE_C, TILE_R - 2)
    local_col = jnp.minimum(shot_pos % TILE_C, TILE_C - 2)
    rows_pix = (tile_row[:, None] * TILE_R + local_row).astype(jnp.int32)
    cols_pix = (shot_tile[:, 0:1] * TILE_C + local_col).astype(jnp.int32)
    frac_row = shot_frac[0]
    frac_col = shot_frac[1]
    amount = shot_dose * live
    dose_map = jnp.zeros((NX, NY), jnp.float32)
    dose_map = dose_map.at[rows_pix, cols_pix].add(amount * (1.0 - frac_row) * (1.0 - frac_col))
    dose_map = dose_map.at[rows_pix + 1, cols_pix].add(amount * frac_row * (1.0 - frac_col))
    dose_map = dose_map.at[rows_pix, cols_pix + 1].add(amount * (1.0 - frac_row) * frac_col)
    dose_map = dose_map.at[rows_pix + 1, cols_pix + 1].add(amount * frac_row * frac_col)
    table = jnp.transpose(zone_weights[zone], (2, 0, 1))
    weights = jnp.repeat(jnp.repeat(table, HALO, axis=1), HALO, axis=2)
    exposure = jnp.zeros((NX, NY), jnp.float32)
    for kernel in range(3):
        exposure = exposure + weights[kernel] * blur_field(dose_map, HALO * sigma_parts[kernel])
    error = exposure - target
    pixel_grad = jnp.zeros((NX, NY), jnp.float32)
    for kernel in range(3):
        pixel_grad = pixel_grad + blur_field(weights[kernel] * error, HALO * sigma_parts[kernel])
    shot_grad = (1.0 - frac_row) * (1.0 - frac_col) * pixel_grad[rows_pix, cols_pix]
    shot_grad = shot_grad + frac_row * (1.0 - frac_col) * pixel_grad[rows_pix + 1, cols_pix]
    shot_grad = shot_grad + (1.0 - frac_row) * frac_col * pixel_grad[rows_pix, cols_pix + 1]
    shot_grad = shot_grad + frac_row * frac_col * pixel_grad[rows_pix + 1, cols_pix + 1]
    return exposure, shot_grad * live
```

```python
import functools
import math

import jax
import jax.numpy as jnp
import numpy as np
from jax import lax
from jax.experimental import pallas as pl
from jax.experimental.pallas import tpu as pltpu
from jax.sharding import PartitionSpec as P

HALO = 64
ZONES = 8
LANES = 128
CHUNK = 256
SIDE = 128
SIGMAS = (0.125 * HALO, 0.25 * HALO, 0.5 * HALO)
MESH = pl.DeviceIdType.MESH
F32, BF16, I32 = jnp.float32, jnp.bfloat16, jnp.int32


def iota(shape, dim):
    return lax.broadcasted_iota(I32, shape, dim)


def split(x):
    high = x.astype(BF16)
    return high, (x - high.astype(F32)).astype(BF16)


def dot(a, b):
    return jnp.dot(a, b, preferred_element_type=F32)


def dot_nt(a, b):
    return lax.dot_general(a, b, (((1,), (1,)), ((), ())), preferred_element_type=F32)


def pick(onehot, x):
    first = x.astype(BF16)
    rest = x - first.astype(F32)
    second = rest.astype(BF16)
    third = (rest - second.astype(F32)).astype(BF16)
    return dot(onehot, first) + dot(onehot, second) + dot(onehot, third)


def tap(offset, sigma):
    reach = np.arange(-HALO, HALO + 1).astype(np.float64)
    total = np.exp(-reach * reach / (2.0 * sigma * sigma)).sum()
    inside = np.abs(offset) <= HALO
    return np.where(inside, np.exp(-(offset.astype(np.float64) ** 2) / (2.0 * sigma * sigma)) / total, 0.0)


def halves(x):
    x = np.asarray(x, np.float32)
    high = x.astype(BF16)
    return high, (x - high.astype(np.float32)).astype(BF16)


def row_bands():
    i, y = np.arange(2 * HALO)[:, None], np.arange(4 * HALO)[None, :]
    return halves(np.concatenate([tap(y - HALO - i, sigma) for sigma in SIGMAS]))


def col_bands():
    x, c = np.arange(2 * CHUNK)[:, None], np.arange(CHUNK)[None, :]
    return halves(np.stack([tap(x - SIDE - c, sigma) for sigma in SIGMAS]))


def slots_of(tile, width):
    n = tile.shape[0]
    own, other = iota((n, width), 0), lax.rem(iota((n, width), 1), n)
    tile_row = jnp.sum(jnp.where(own == other, tile, 0), axis=0, keepdims=True)
    same = tile == tile_row
    rank_row = jnp.sum(jnp.where(same & (own < other), 1, 0), axis=0, keepdims=True)
    once = iota((n, width), 1) < n
    rank_col = jnp.sum(jnp.where(same & (other < own) & once, 1, 0), axis=1, keepdims=True)
    return tile * 2 + rank_col, tile_row * 2 + rank_row


def greet_all(n, me, row):
    barrier = pltpu.get_barrier_semaphore()

    def greet(step, carry):
        peer = lax.rem(me + step, n)
        pl.semaphore_signal(barrier, inc=1, device_id=(row, peer), device_id_type=MESH)
        return carry

    lax.fori_loop(1, n, greet, 0)
    return barrier


def exchange(n, me, row, source, target, send_sem, recv_sem):
    def copy_to(peer, slot):
        return pltpu.make_async_remote_copy(
            src_ref=source.at[peer],
            dst_ref=target.at[slot],
            send_sem=send_sem.at[peer],
            recv_sem=recv_sem.at[slot],
            device_id=(row, peer),
            device_id_type=MESH,
        )

    def start(step, carry):
        copy_to(lax.rem(me + step, n), me).start()
        return carry

    def finish(step, carry):
        peer = lax.rem(me + n - step, n)
        copy_to(peer, peer).wait_recv()
        return carry

    def drain(step, carry):
        copy_to(lax.rem(me + step, n), me).wait_send()
        return carry

    lax.fori_loop(1, n, start, 0)
    target[pl.ds(me, 1)] = source[pl.ds(me, 1)]
    lax.fori_loop(1, n, finish, 0)
    lax.fori_loop(1, n, drain, 0)


def route_kernel(n, dose, frac, pos, count, tile, recv, send, send_sem, recv_sem):
    row, me = lax.axis_index("row"), lax.axis_index("col")
    barrier = greet_all(n, me, row)
    blocks = tile.shape[0]
    _, placed = slots_of(tile[...], LANES)
    eye = iota((blocks, blocks), 0) == iota((blocks, blocks), 1)
    live_count = jnp.sum(jnp.where(eye, count[...], 0), axis=1, keepdims=True)
    live = iota((blocks, LANES), 1) < live_count
    amount = jnp.where(live, dose[...], 0.0)
    place = jnp.where(live, pos[...] + 1, 0).astype(F32)
    packed = jnp.concatenate([amount, frac[0], frac[1], place], axis=0)
    out, col = iota((8 * n, LANES), 0), iota((8 * n, LANES), 1)
    wanted = 2 * (out >> 3) + ((out >> 2) & 1)
    chosen = (wanted == placed) & ((out & 3) == lax.div(col, blocks))
    onehot = jnp.where(chosen, 1.0, 0.0).astype(BF16)
    send[...] = pick(onehot, packed).reshape(n, 8, LANES)
    pl.semaphore_wait(barrier, n - 1)
    exchange(n, me, row, send, recv, send_sem, recv_sem)


def route(n, dose, frac, pos, count, tile):
    vmem = pl.BlockSpec(memory_space=pltpu.VMEM)
    return pl.pallas_call(
        functools.partial(route_kernel, n),
        out_shape=jax.ShapeDtypeStruct((n, 8, LANES), F32),
        in_specs=[vmem] * 5,
        out_specs=vmem,
        scratch_shapes=[
            pltpu.VMEM((n, 8, LANES), F32),
            pltpu.SemaphoreType.DMA((n,)),
            pltpu.SemaphoreType.DMA((n,)),
        ],
        compiler_params=pltpu.CompilerParams(collective_id=0, has_side_effects=True),
        name="route",
    )(dose, frac, pos, count, tile)


def return_kernel(n, grads, tile, out, back, send_sem, recv_sem):
    row, me = lax.axis_index("row"), lax.axis_index("col")
    barrier = greet_all(n, me, row)
    blocks = tile.shape[0]
    placed, _ = slots_of(tile[...], LANES)
    col = iota((blocks, 8 * n), 1)
    chosen = (placed == 2 * (col >> 3) + (col & 7)) & ((col & 7) < 2)
    onehot = jnp.where(chosen, 1.0, 0.0).astype(BF16)
    pl.semaphore_wait(barrier, n - 1)
    exchange(n, me, row, grads, back, send_sem, recv_sem)
    out[...] = pick(onehot, back[...].reshape(8 * n, LANES))


def give_back(n, grads, tile):
    vmem = pl.BlockSpec(memory_space=pltpu.VMEM)
    return pl.pallas_call(
        functools.partial(return_kernel, n),
        out_shape=jax.ShapeDtypeStruct((tile.shape[0], LANES), F32),
        in_specs=[vmem] * 2,
        out_specs=vmem,
        scratch_shapes=[
            pltpu.VMEM((n, 8, LANES), F32),
            pltpu.SemaphoreType.DMA((n,)),
            pltpu.SemaphoreType.DMA((n,)),
        ],
        compiler_params=pltpu.CompilerParams(collective_id=2, has_side_effects=True),
        name="give_back",
    )(grads, tile)


def shot_rows(buf, chunk):
    both = [buf[2 * chunk], buf[2 * chunk + 1]]
    line = lambda f: jnp.concatenate([part[f : f + 1] for part in both], axis=1)
    place = line(3).astype(I32) - 1
    return line(0), line(1), line(2), place


def table(index, low, high, count):
    here = iota((count, index.shape[1]), 0).astype(F32).astype(BF16)
    first = index.astype(F32).astype(BF16)
    second = (index + 1).astype(F32).astype(BF16)
    at_first, at_second = here == first, here == second
    zero = jnp.zeros((), BF16)
    return [jnp.where(at_first, lo, jnp.where(at_second, hi, zero)) for lo, hi in zip(low, high)]


def col_tables(place, frac, cols):
    pixel = jnp.minimum(place & (cols - 1), cols - 2)
    low, high = split(1.0 - frac), split(frac)
    for begin in range(0, cols, LANES):
        local = jnp.clip(pixel - begin, -2, LANES)
        yield table(local, low, high, LANES)


def deposit_kernel(recv, dose, buf, counts, row_counts, sem):
    n = recv.shape[0]
    rows, cols = dose.shape
    shift = int(math.log2(cols))
    lane = iota((8, LANES), 1)
    places = recv[:, 3, :], recv[:, 7, :]
    live = [jnp.sum(jnp.where(place > 0.0, 1, 0), axis=1, keepdims=True) for place in places]
    which = iota((n, LANES), 1)
    spread = jnp.where(which < n, live[0], live[1])
    chosen = (lax.rem(which, n) == iota((n, LANES), 0)) & (which < 2 * n)
    row_counts[...] = jnp.sum(jnp.where(chosen, spread, 0), axis=0, keepdims=True)
    copy = pltpu.make_async_copy(row_counts, counts, sem)
    copy.start()
    dose[...] = jnp.zeros_like(dose)
    copy.wait()

    def place_block(block, amount, carry):
        at, current = carry
        lane_at, tile_at = at & (LANES - 1), at >> 7
        moved = pltpu.roll(block, lane_at, axis=1)
        merged = jnp.where(lane < lane_at, current, moved)
        buf[tile_at] = merged
        full = jnp.full((8, LANES), lane_at + amount, I32) >= LANES
        return at + amount, jnp.where(full, moved, merged)

    def compact(i, carry):
        block = recv[i]
        carry = place_block(block, counts[0, i], carry)
        return place_block(pltpu.roll(block, 4, axis=0), counts[0, n + i], carry)

    total, last = lax.fori_loop(0, n, compact, (jnp.int32(0), jnp.zeros((8, LANES), F32)))
    buf[total >> 7] = jnp.where(lane < (total & (LANES - 1)), last, 0.0)
    buf[(total >> 7) + 1] = jnp.zeros((8, LANES), F32)

    def deposit(chunk, carry):
        amount, frac_row, frac_col, place = shot_rows(buf, chunk)
        pixel_row = jnp.minimum(place >> shift, rows - 2)
        row_high, row_low = table(
            pixel_row, split(amount * (1.0 - frac_row)), split(amount * frac_row), rows
        )
        tables = list(col_tables(place, frac_col, cols))
        for begin in range(0, cols, CHUNK):
            part = tables[begin // LANES : (begin + CHUNK) // LANES]
            high = jnp.concatenate([t[0] for t in part], axis=0)
            low = jnp.concatenate([t[1] for t in part], axis=0)
            dose[:, begin : begin + CHUNK] += (
                dot_nt(row_high, high) + dot_nt(row_low, high) + dot_nt(row_high, low)
            )
        return carry

    lax.fori_loop(0, (total + CHUNK - 1) >> 8, deposit, 0)


def deposit(recv, rows, cols):
    vmem = pl.BlockSpec(memory_space=pltpu.VMEM)
    smem = pl.BlockSpec(memory_space=pltpu.SMEM)
    tiles = 2 * recv.shape[0] + 2
    return pl.pallas_call(
        deposit_kernel,
        out_shape=[
            jax.ShapeDtypeStruct((rows, cols), F32),
            jax.ShapeDtypeStruct((tiles, 8, LANES), F32),
            jax.ShapeDtypeStruct((1, LANES), I32),
        ],
        in_specs=[vmem],
        out_specs=[vmem, vmem, smem],
        scratch_shapes=[pltpu.VMEM((1, LANES), I32), pltpu.SemaphoreType.DMA],
        compiler_params=pltpu.CompilerParams(vmem_limit_bytes=32 * 2**20),
        name="deposit",
    )(recv)


def sample_kernel(grad_high, grad_low, buf, counts, out, values):
    n = out.shape[0]
    rows, cols = grad_high.shape
    shift = int(math.log2(cols))
    lane = iota((1, LANES), 1)
    total = lax.fori_loop(0, 2 * n, lambda i, t: t + counts[0, i], jnp.int32(0))

    def sample(chunk, carry):
        _, frac_row, frac_col, place = shot_rows(buf, chunk)
        pixel_row = jnp.minimum(place >> shift, rows - 2)
        tables = list(col_tables(place, frac_col, cols))
        high = jnp.concatenate([t[0] for t in tables], axis=0)
        low = jnp.concatenate([t[1] for t in tables], axis=0)
        along = dot(grad_high[...], high) + dot(grad_low[...], high) + dot(grad_high[...], low)
        here = iota((rows, CHUNK), 0)
        weight = jnp.where(
            here == pixel_row, 1.0 - frac_row, jnp.where(here == pixel_row + 1, frac_row, 0.0)
        )
        got = jnp.sum(weight * along, axis=0, keepdims=True)
        values[2 * chunk, 0:1] = got[:, :LANES]
        values[2 * chunk + 1, 0:1] = got[:, LANES:]
        return carry

    lax.fori_loop(0, (total + CHUNK - 1) >> 8, sample, 0)

    def take_block(amount, at):
        lane_at, tile_at = at & (LANES - 1), at >> 7
        both = jnp.where(lane >= lane_at, values[tile_at, 0:1], values[tile_at + 1, 0:1])
        moved = pltpu.roll(both, LANES - lane_at, axis=1)
        return jnp.where(lane < amount, moved, 0.0)

    row = iota((8, LANES), 0)

    def spread(i, at):
        first = take_block(counts[0, i], at)
        at = at + counts[0, i]
        second = take_block(counts[0, n + i], at)
        out[i] = jnp.where(row == 0, first, jnp.where(row == 1, second, 0.0))
        return at + counts[0, n + i]

    lax.fori_loop(0, n, spread, jnp.int32(0))


def sample(grad_high, grad_low, buf, counts):
    vmem = pl.BlockSpec(memory_space=pltpu.VMEM)
    smem = pl.BlockSpec(memory_space=pltpu.SMEM)
    n = (buf.shape[0] - 2) // 2
    return pl.pallas_call(
        sample_kernel,
        out_shape=jax.ShapeDtypeStruct((n, 8, LANES), F32),
        in_specs=[vmem, vmem, vmem, smem],
        out_specs=vmem,
        scratch_shapes=[pltpu.VMEM(buf.shape, F32)],
        compiler_params=pltpu.CompilerParams(vmem_limit_bytes=32 * 2**20),
        name="sample",
    )(grad_high, grad_low, buf, counts)


SIDES = ((-1, 0), (1, 0), (0, -1), (0, 1), (-1, -1), (-1, 1), (1, -1), (1, 1))


def blur_kernel(
    dims, dose, target, zone, zone_weights, row_high, row_low, col_high, col_low,
    exposure, grad_high, grad_low,
    zone_own, zone_in, halo_rows, halo_cols, halo_corners, dose_high, dose_low, part_high, part_low,
    error, weight, dose_send, dose_recv, error_send, error_recv, zone_send, zone_recv,
):
    n_row, n_col = dims
    rows, cols = dose.shape
    wide = cols + 2 * SIDE
    row, col = lax.axis_index("row"), lax.axis_index("col")

    def exists(side):
        down, right = SIDES[side]
        tests = []
        if down:
            tests.append(row > 0 if down < 0 else row < n_row - 1)
        if right:
            tests.append(col > 0 if right < 0 else col < n_col - 1)
        return functools.reduce(jnp.logical_and, tests)

    def neighbour(side):
        down, right = SIDES[side]
        return (row + down, col + right)

    def opposite(side):
        down, right = SIDES[side]
        return SIDES.index((-down, -right))

    def landing(turn, side):
        if side < 2:
            return halo_rows.at[turn, side]
        if side < 4:
            return halo_cols.at[turn, side - 2]
        return halo_corners.at[turn, side - 4]

    def edge(field, side):
        down, right = SIDES[side]
        high = slice(None) if not down else (pl.ds(0, HALO) if down < 0 else pl.ds(rows - HALO, HALO))
        across = slice(None) if not right else (pl.ds(0, SIDE) if right < 0 else pl.ds(cols - SIDE, SIDE))
        return field.at[high, across]

    def halo_copy(field, turn, side):
        sends, recvs = (dose_send, dose_recv) if turn == 0 else (error_send, error_recv)
        return pltpu.make_async_remote_copy(
            src_ref=edge(field, side),
            dst_ref=landing(turn, opposite(side)),
            send_sem=sends.at[side],
            recv_sem=recvs.at[opposite(side)],
            device_id=neighbour(side),
            device_id_type=MESH,
        )

    def zone_copy(side):
        return pltpu.make_async_remote_copy(
            src_ref=zone_own,
            dst_ref=zone_in.at[opposite(side)],
            send_sem=zone_send.at[side],
            recv_sem=zone_recv.at[opposite(side)],
            device_id=neighbour(side),
            device_id_type=MESH,
        )

    barrier = pltpu.get_barrier_semaphore()
    zone_own[...] = jnp.zeros_like(zone_own)
    zone_own[0 : zone.shape[0], 0 : zone.shape[1]] = zone[...]
    for side in range(8):

        @pl.when(jnp.logical_not(exists(side)))
        def _(side=side):
            for turn in range(2):
                spot = landing(turn, side)
                spot[...] = jnp.zeros_like(spot)
            zone_in[side] = jnp.zeros_like(zone_own)

    for side in range(8):

        @pl.when(exists(side))
        def _(side=side):
            pl.semaphore_signal(barrier, inc=1, device_id=neighbour(side), device_id_type=MESH)

    tall = 1 + jnp.where(row > 0, 1, 0) + jnp.where(row < n_row - 1, 1, 0)
    broad = 1 + jnp.where(col > 0, 1, 0) + jnp.where(col < n_col - 1, 1, 0)
    pl.semaphore_wait(barrier, tall * broad - 1)

    for side in range(8):

        @pl.when(exists(side))
        def _(side=side):
            halo_copy(dose, 0, side).start()
            zone_copy(side).start()

    def await_halo(field, turn, sides):
        for side in sides:

            @pl.when(exists(side))
            def _(side=side):
                halo_copy(field, turn, opposite(side)).wait_recv()

    def put_dose(value, first_row, first_col):
        high, low = split(value)
        here = pl.ds(first_row, value.shape[0]), pl.ds(first_col, value.shape[1])
        dose_high[here] = high
        dose_low[here] = low

    def along_cols(field, kernel):
        count = field.shape[0]
        stacked = [
            jnp.concatenate([part[:, b : b + 2 * CHUNK] for b in range(0, cols, CHUNK)], axis=0)
            for part in split(field)
        ]
        high, low = stacked
        out = (
            dot(high, col_high[kernel]) + dot(low, col_high[kernel]) + dot(high, col_low[kernel])
        )
        return jnp.concatenate(
            [out[i * count : (i + 1) * count] for i in range(cols // CHUNK)], axis=1
        )

    windows = {
        "top": (0, HALO, 0, 0),
        "mid": (HALO, 2 * HALO, HALO, 0),
        "low": (rows - HALO, HALO, 2 * HALO, HALO),
    }

    def row_blur(kernel, window, in_high, in_low):
        first, count, begin, band = windows[window]
        take = pl.ds(kernel * 2 * HALO + band, count)
        here = pl.ds(begin, 4 * HALO)
        high, low = row_high[take], row_low[take]
        return dot(high, in_high[here]) + dot(low, in_high[here]) + dot(high, in_low[here])

    def forward(window):
        first, count, _, _ = windows[window]
        total = [jnp.zeros((HALO, cols), F32) for _ in range(count // HALO)]
        for kernel in range(3):
            field = along_cols(row_blur(kernel, window, dose_high, dose_low), kernel)
            for i in range(count // HALO):
                square = 8 * kernel + 1 + first // HALO + i
                factor = weight[square : square + 1, SIDE : SIDE + cols]
                total[i] = total[i] + factor * field[i * HALO : (i + 1) * HALO]
        for i in range(count // HALO):
            here = pl.ds(first + i * HALO, HALO)
            exposure[here] = total[i]
            error[here] = total[i] - target[here]

    def put_part(value, first_row, first_col):
        across = pl.ds(first_col, value.shape[1])
        for i in range(value.shape[0] // HALO):
            square = first_row // HALO + i
            here = pl.ds(first_row + i * HALO, HALO)
            piece = value[i * HALO : (i + 1) * HALO]
            for kernel in range(3):
                factor = weight[8 * kernel + square : 8 * kernel + square + 1, across]
                high, low = split(factor * piece)
                part_high[kernel, here, across] = high
                part_low[kernel, here, across] = low

    def backward(window):
        first, count, _, _ = windows[window]
        total = jnp.zeros((count, cols), F32)
        for kernel in range(3):
            field = row_blur(kernel, window, part_high.at[kernel], part_low.at[kernel])
            total = total + along_cols(field, kernel)
        high, low = split(total)
        here = pl.ds(first, count)
        grad_high[here] = high
        grad_low[here] = low

    def zone_table():
        sub, lane = iota((8, LANES), 0), iota((8, LANES), 1)
        high, across = zone.shape
        own = pltpu.roll(pltpu.roll(zone_own[...], 1, axis=0), 2, axis=1)
        table = own
        for side in range(8):
            down, right = SIDES[side]
            got = zone_in[side]
            got = pltpu.roll(got, (1 + down * high) % 8, axis=0)
            got = pltpu.roll(got, (2 + right * across) % LANES, axis=1)
            row_ok = (sub == 0) if down < 0 else (sub == high + 1) if down > 0 else (sub >= 1) & (sub <= high)
            col_ok = (
                (lane == 1) if right < 0 else (lane == across + 2) if right > 0 else (lane >= 2) & (lane < across + 2)
            )
            table = jnp.where(row_ok & col_ok, got, table)
        picked = []
        for kernel in range(3):
            value = jnp.zeros((8, LANES), F32)
            for z in range(ZONES):
                value = jnp.where(table == z, zone_weights[z, kernel], value)
            picked.append(value)
        spread = iota((LANES, wide), 0) == iota((LANES, wide), 1) // HALO
        return picked, spread

    put_dose(dose[...], HALO, SIDE)
    for side in range(8):

        @pl.when(exists(side))
        def _(side=side):
            zone_copy(opposite(side)).wait_recv()

    picked, spread = zone_table()
    spread = jnp.where(spread, 1.0, 0.0).astype(BF16)
    stacked = jnp.concatenate(picked, axis=0)
    first_part = stacked.astype(BF16)
    rest = stacked - first_part.astype(F32)
    second_part = rest.astype(BF16)
    third_part = (rest - second_part.astype(F32)).astype(BF16)
    weight[...] = dot(first_part, spread) + dot(second_part, spread) + dot(third_part, spread)

    await_halo(dose, 0, (2, 3))
    put_dose(halo_cols[0, 0], HALO, 0)
    put_dose(halo_cols[0, 1], HALO, SIDE + cols)
    forward("mid")
    await_halo(dose, 0, (0, 1, 4, 5, 6, 7))
    for place, first_row in ((0, 0), (1, HALO + rows)):
        put_dose(halo_rows[0, place], first_row, SIDE)
        put_dose(halo_corners[0, 2 * place], first_row, 0)
        put_dose(halo_corners[0, 2 * place + 1], first_row, SIDE + cols)
    forward("top")
    forward("low")
    for side in range(8):

        @pl.when(exists(side))
        def _(side=side):
            halo_copy(error, 1, side).start()

    put_part(error[...], HALO, SIDE)
    await_halo(error, 1, (2, 3))
    put_part(halo_cols[1, 0], HALO, 0)
    put_part(halo_cols[1, 1], HALO, SIDE + cols)
    backward("mid")
    await_halo(error, 1, (0, 1, 4, 5, 6, 7))
    for place, first_row in ((0, 0), (1, HALO + rows)):
        put_part(halo_rows[1, place], first_row, SIDE)
        put_part(halo_corners[1, 2 * place], first_row, 0)
        put_part(halo_corners[1, 2 * place + 1], first_row, SIDE + cols)
    backward("top")
    backward("low")
    for side in range(8):

        @pl.when(exists(side))
        def _(side=side):
            halo_copy(dose, 0, side).wait_send()
            halo_copy(error, 1, side).wait_send()
            zone_copy(side).wait_send()


def blur(dims, dose, target, zone, zone_weights):
    rows, cols = dose.shape
    wide, high = cols + 2 * SIDE, rows + 2 * HALO
    vmem = pl.BlockSpec(memory_space=pltpu.VMEM)
    smem = pl.BlockSpec(memory_space=pltpu.SMEM)
    dma = pltpu.SemaphoreType.DMA((8,))
    return pl.pallas_call(
        functools.partial(blur_kernel, dims),
        out_shape=[
            jax.ShapeDtypeStruct((rows, cols), F32),
            jax.ShapeDtypeStruct((rows, cols), BF16),
            jax.ShapeDtypeStruct((rows, cols), BF16),
        ],
        in_specs=[vmem, vmem, vmem, smem, vmem, vmem, vmem, vmem],
        out_specs=[vmem] * 3,
        scratch_shapes=[
            pltpu.VMEM((8, LANES), I32),
            pltpu.VMEM((8, 8, LANES), I32),
            pltpu.VMEM((2, 2, HALO, cols), F32),
            pltpu.VMEM((2, 2, rows, SIDE), F32),
            pltpu.VMEM((2, 4, HALO, SIDE), F32),
            pltpu.VMEM((high, wide), BF16),
            pltpu.VMEM((high, wide), BF16),
            pltpu.VMEM((3, high, wide), BF16),
            pltpu.VMEM((3, high, wide), BF16),
            pltpu.VMEM((rows, cols), F32),
            pltpu.VMEM((24, wide), F32),
            dma, dma, dma, dma, dma, dma,
        ],
        compiler_params=pltpu.CompilerParams(
            collective_id=1, has_side_effects=True, vmem_limit_bytes=48 * 2**20
        ),
        name="blur",
    )(dose, target, zone, zone_weights, *row_bands(), *col_bands())


def per_device(dims, shot_dose, shot_frac, shot_pos, block_count, shot_tile, zone, zone_weights, target):
    n = dims[1]
    rows, cols = target.shape
    recv = route(n, shot_dose, shot_frac, shot_pos, block_count.reshape(1, -1), shot_tile)
    dose, buf, counts = deposit(recv, rows, cols)
    exposure, grad_high, grad_low = blur(dims, dose, target, zone, zone_weights)
    slot_grad = sample(grad_high, grad_low, buf, counts)
    return exposure, give_back(n, slot_grad, shot_tile)


def solution(mesh):
    dims = (mesh.shape["row"], mesh.shape["col"])
    return jax.shard_map(
        functools.partial(per_device, dims),
        mesh=mesh,
        in_specs=(
            P(("row", "col"), None),
            P(None, ("row", "col"), None),
            P(("row", "col"), None),
            P(("row", "col")),
            P(("row", "col"), None),
            P("row", "col"),
            P(),
            P("row", "col"),
        ),
        out_specs=(P("row", "col"), P(("row", "col"), None)),
        check_vma=False,
    )
```

```python
import functools
import math

import jax
import jax.numpy as jnp
import numpy as np
from jax import lax
from jax.experimental import pallas as pl
from jax.experimental.pallas import tpu as pltpu
from jax.sharding import PartitionSpec as P

HALO = 64
ZONES = 8
LANES = 128
CHUNK = 256
SIDE = 128
SIGMAS = (0.125 * HALO, 0.25 * HALO, 0.5 * HALO)
MESH = pl.DeviceIdType.MESH
F32, BF16, I32 = jnp.float32, jnp.bfloat16, jnp.int32


def cost(us):
    return pl.CostEstimate(flops=0, bytes_accessed=int(us * 3.0e6), transcendentals=0)


def iota(shape, dim):
    return lax.broadcasted_iota(I32, shape, dim)


def split(x):
    high = x.astype(BF16)
    return high, (x - high.astype(F32)).astype(BF16)


def dot(a, b):
    return jnp.dot(a, b, preferred_element_type=F32)


def dot_nt(a, b):
    return lax.dot_general(a, b, (((1,), (1,)), ((), ())), preferred_element_type=F32)


def pick(onehot, x):
    first = x.astype(BF16)
    rest = x - first.astype(F32)
    second = rest.astype(BF16)
    third = (rest - second.astype(F32)).astype(BF16)
    return dot(onehot, first) + dot(onehot, second) + dot(onehot, third)


def tap(offset, sigma):
    reach = np.arange(-HALO, HALO + 1).astype(np.float64)
    total = np.exp(-reach * reach / (2.0 * sigma * sigma)).sum()
    inside = np.abs(offset) <= HALO
    return np.where(inside, np.exp(-(offset.astype(np.float64) ** 2) / (2.0 * sigma * sigma)) / total, 0.0)


def halves(x):
    x = np.asarray(x, np.float32)
    high = x.astype(BF16)
    return high, (x - high.astype(np.float32)).astype(BF16)


def row_bands():
    i, y = np.arange(2 * HALO)[:, None], np.arange(4 * HALO)[None, :]
    return halves(np.concatenate([tap(y - HALO - i, sigma) for sigma in SIGMAS]))


def col_bands():
    x, c = np.arange(2 * CHUNK)[:, None], np.arange(CHUNK)[None, :]
    return halves(np.stack([tap(x - SIDE - c, sigma) for sigma in SIGMAS]))


def slots_of(tile, width):
    n = tile.shape[0]
    times = width // n
    own, lane = iota((n, width), 0), iota((n, width), 1)
    other = lane // times
    tile_row = jnp.sum(jnp.where(own == other, tile, 0), axis=0, keepdims=True)
    same = tile == tile_row
    rank_row = jnp.sum(jnp.where(same & (own < other), 1, 0), axis=0, keepdims=True)
    once = lane % times == 0
    rank_col = jnp.sum(jnp.where(same & (other < own) & once, 1, 0), axis=1, keepdims=True)
    return tile * 2 + rank_col, tile_row * 2 + rank_row


def upright(line):
    n = line.shape[1]
    return jnp.sum(jnp.where(iota((n, n), 0) == iota((n, n), 1), line, 0), axis=1, keepdims=True)


def column_class(pixel):
    return 2 * (pixel >> 8) + jnp.where((pixel & (CHUNK - 1)) == CHUNK - 1, 1, 0)


def greet_all(n, me, row):
    barrier = pltpu.get_barrier_semaphore()

    def greet(step, carry):
        peer = lax.rem(me + step, n)
        pl.semaphore_signal(barrier, inc=1, device_id=(row, peer), device_id_type=MESH)
        return carry

    lax.fori_loop(1, n, greet, 0)
    return barrier


def exchange(n, me, row, source, target, send_sem, recv_sem):
    def copy_to(peer, slot):
        return pltpu.make_async_remote_copy(
            src_ref=source.at[peer],
            dst_ref=target.at[slot],
            send_sem=send_sem.at[peer],
            recv_sem=recv_sem.at[slot],
            device_id=(row, peer),
            device_id_type=MESH,
        )

    def start(step, carry):
        copy_to(lax.rem(me + step, n), me).start()
        return carry

    def finish(step, carry):
        peer = lax.rem(me + n - step, n)
        copy_to(peer, peer).wait_recv()
        return carry

    def drain(step, carry):
        copy_to(lax.rem(me + step, n), me).wait_send()
        return carry

    lax.fori_loop(1, n, start, 0)
    target[pl.ds(me, 1)] = source[pl.ds(me, 1)]
    lax.fori_loop(1, n, finish, 0)
    lax.fori_loop(1, n, drain, 0)


def route_kernel(
    n, cols, dose, frac, pos, count, tile, recv, order, parts, ordered, send, send_sem, recv_sem
):
    row, me = lax.axis_index("row"), lax.axis_index("col")
    barrier = greet_all(n, me, row)
    blocks = tile.shape[1]
    live = iota((blocks, LANES), 1) < upright(count[...])
    dead = 2 * (cols // CHUNK) - 1
    kind = jnp.where(live, column_class(jnp.minimum(pos[...] & (cols - 1), cols - 2)), dead)
    masks = [jnp.where(kind == j, 1.0, 0.0) for j in range(dead + 1)]
    before = jnp.where(iota((LANES, LANES), 0) < iota((LANES, LANES), 1), 1.0, 0.0).astype(BF16)
    prefix = dot(jnp.concatenate(masks, axis=0).astype(BF16), before)
    start = jnp.zeros((blocks, 1), F32)
    rank = jnp.zeros((blocks, LANES), F32)
    for j, mask in enumerate(masks):
        rank = rank + mask * (prefix[j * blocks : (j + 1) * blocks] + start)
        start = start + jnp.sum(mask, axis=1, keepdims=True)
    rank = rank.astype(I32)
    order[...] = rank
    fields = [
        jnp.where(live, dose[...], 0.0),
        frac[0],
        frac[1],
        jnp.where(live, pos[...] + 1, 0).astype(F32),
    ]
    for f, field in enumerate(fields):
        for part in range(3):
            piece = field.astype(BF16).astype(F32)
            parts[:, 4 * part + f] = piece
            field = field - piece
        parts[:, 12 + f] = jnp.zeros((blocks, LANES), F32)
    target = iota((LANES, LANES), 0)
    for b in range(blocks):
        moves = jnp.where(target == rank[b : b + 1], 1.0, 0.0).astype(BF16)
        ordered[b] = dot_nt(parts[b].astype(BF16), moves)
    width = 16 * blocks
    _, placed = slots_of(upright(tile[...]), width)
    out, col = iota((8 * n, width), 0), iota((8 * n, width), 1)
    chosen = (out // 4 == placed) & (out % 4 == col % 4) & (col % 16 < 12)
    onehot = jnp.where(chosen, 1.0, 0.0).astype(BF16)
    send[...] = dot(onehot, ordered[...].reshape(width, LANES).astype(BF16)).reshape(n, 8, LANES)
    pl.semaphore_wait(barrier, n - 1)
    exchange(n, me, row, send, recv, send_sem, recv_sem)


def route(n, cols, dose, frac, pos, count, tile):
    vmem = pl.BlockSpec(memory_space=pltpu.VMEM)
    blocks = tile.shape[1]
    return pl.pallas_call(
        functools.partial(route_kernel, n, cols),
        out_shape=[
            jax.ShapeDtypeStruct((n, 8, LANES), F32),
            jax.ShapeDtypeStruct((blocks, LANES), I32),
        ],
        in_specs=[vmem] * 5,
        out_specs=[vmem] * 2,
        scratch_shapes=[
            pltpu.VMEM((blocks, 16, LANES), F32),
            pltpu.VMEM((blocks, 16, LANES), F32),
            pltpu.VMEM((n, 8, LANES), F32),
            pltpu.SemaphoreType.DMA((n,)),
            pltpu.SemaphoreType.DMA((n,)),
        ],
        compiler_params=pltpu.CompilerParams(
            collective_id=0, has_side_effects=True, vmem_limit_bytes=8 * 2**20
        ),
        cost_estimate=cost(10),
        name="route",
    )(dose, frac, pos, count, tile)


def return_kernel(n, grads, tile, order, out, back, send_sem, recv_sem):
    row, me = lax.axis_index("row"), lax.axis_index("col")
    barrier = greet_all(n, me, row)
    blocks = tile.shape[1]
    placed, _ = slots_of(upright(tile[...]), blocks)
    col = iota((blocks, 8 * n), 1)
    chosen = (placed == 2 * (col >> 3) + (col & 7)) & ((col & 7) < 2)
    onehot = jnp.where(chosen, 1.0, 0.0).astype(BF16)
    pl.semaphore_wait(barrier, n - 1)
    exchange(n, me, row, grads, back, send_sem, recv_sem)
    found = pick(onehot, back[...].reshape(8 * n, LANES))
    out[...] = jnp.take_along_axis(found, order[...], axis=1)


def give_back(n, grads, tile, order):
    vmem = pl.BlockSpec(memory_space=pltpu.VMEM)
    return pl.pallas_call(
        functools.partial(return_kernel, n),
        out_shape=jax.ShapeDtypeStruct((tile.shape[1], LANES), F32),
        in_specs=[vmem] * 3,
        out_specs=vmem,
        scratch_shapes=[
            pltpu.VMEM((n, 8, LANES), F32),
            pltpu.SemaphoreType.DMA((n,)),
            pltpu.SemaphoreType.DMA((n,)),
        ],
        compiler_params=pltpu.CompilerParams(
            collective_id=2, has_side_effects=True, vmem_limit_bytes=8 * 2**20
        ),
        cost_estimate=cost(10),
        name="give_back",
    )(grads, tile, order)


def shot_rows(buf, first, end):
    lane = iota((8, LANES), 1)
    both = [jnp.where(lane < end, buf[first], 0.0), jnp.where(lane < end - LANES, buf[first + 1], 0.0)]
    line = lambda f: jnp.concatenate([part[f : f + 1] for part in both], axis=1)
    return line(0), line(1), line(2), line(3).astype(I32) - 1


def table(index, low, high, count):
    here = iota((count, index.shape[1]), 0).astype(F32).astype(BF16)
    first = index.astype(F32).astype(BF16)
    second = (index + 1).astype(F32).astype(BF16)
    at_first, at_second = here == first, here == second
    zero = jnp.zeros((), BF16)
    return [jnp.where(at_first, lo, jnp.where(at_second, hi, zero)) for lo, hi in zip(low, high)]


def col_table(place, frac, cols, window):
    pixel = jnp.minimum(place & (cols - 1), cols - 2)
    local = jnp.clip(pixel - window * CHUNK, -2, CHUNK)
    return table(local, split(1.0 - frac), split(frac), CHUNK)


def tiles_of_bin(n):
    return 2 * n + 2


def deposit_kernel(recv, dose, buf, spans, row_spans, sem):
    n = recv.shape[0]
    rows, cols = dose.shape
    bins = cols // CHUNK
    shift = int(math.log2(cols))
    lane = iota((8, LANES), 1)
    ends = []
    for half in range(2):
        place = recv[:, 4 * half + 3, :].astype(I32) - 1
        kind = column_class(jnp.minimum(place & (cols - 1), cols - 2))
        kind = jnp.where(place >= 0, kind, 2 * bins)
        ends.append([jnp.sum(jnp.where(kind <= j, 1, 0), axis=1, keepdims=True) for j in range(2 * bins)])
    which = iota((n, LANES), 1)
    chosen = (lax.rem(which, n) == iota((n, LANES), 0)) & (which < 2 * n)

    def to_lanes(first, second):
        spread = jnp.where(which < n, first, second)
        return jnp.sum(jnp.where(chosen, spread, 0), axis=0, keepdims=True)

    lines = []
    for q in range(bins):
        lines.append(to_lanes(*(e[2 * q - 2] if q else jnp.zeros((n, 1), I32) for e in ends)))
    for q in range(bins):
        lines.append(to_lanes(*(e[2 * q + 1] for e in ends)) - lines[q])
    row_spans[...] = jnp.concatenate(lines, axis=0)
    copy = pltpu.make_async_copy(row_spans, spans, sem)
    copy.start()
    dose[...] = jnp.zeros_like(dose)
    copy.wait()

    def append(block, begin, amount, carry):
        at, current = carry
        lane_at = at & (LANES - 1)
        moved = pltpu.roll(block, (at - begin) & (LANES - 1), axis=1)
        merged = jnp.where(lane < lane_at, current, moved)
        buf[at >> 7] = merged
        full = jnp.full((8, LANES), lane_at + amount, I32) >= LANES
        return at + amount, jnp.where(full, moved, merged)

    def gather(i, carry):
        block = recv[i]
        for half in range(2):
            index = half * n + i
            carry = [
                append(block, spans[q, index], spans[bins + q, index], carry[q]) for q in range(bins)
            ]
            block = pltpu.roll(block, 4, axis=0)
        return carry

    starts = [q * tiles_of_bin(n) for q in range(bins)]
    empty = jnp.zeros((8, LANES), F32)
    found = lax.fori_loop(0, n, gather, [(jnp.int32(s * LANES), empty) for s in starts])
    most = jnp.int32(0)
    for q, (at, last) in enumerate(found):
        buf[at >> 7] = jnp.where(lane < (at & (LANES - 1)), last, 0.0)
        buf[(at >> 7) + 1] = empty
        most = jnp.maximum(most, (at - starts[q] * LANES + CHUNK - 1) >> 8)
    spans[0, LANES - 1] = most

    def deposit(chunk, carry):
        for q in range(bins):
            first = starts[q] + 2 * chunk
            end = found[q][0] - first * LANES
            amount, frac_row, frac_col, place = shot_rows(buf, first, end)
            pixel_row = jnp.minimum(place >> shift, rows - 2)
            row_high, row_low = table(
                pixel_row, split(amount * (1.0 - frac_row)), split(amount * frac_row), rows
            )
            high, low = col_table(place, frac_col, cols, q)
            dose[:, q * CHUNK : (q + 1) * CHUNK] += (
                dot_nt(row_high, high) + dot_nt(row_low, high) + dot_nt(row_high, low)
            )
        return carry

    lax.fori_loop(0, most, deposit, 0)


def deposit(recv, rows, cols):
    vmem = pl.BlockSpec(memory_space=pltpu.VMEM)
    smem = pl.BlockSpec(memory_space=pltpu.SMEM)
    tiles = (cols // CHUNK) * tiles_of_bin(recv.shape[0])
    spans = (2 * (cols // CHUNK), LANES)
    return pl.pallas_call(
        deposit_kernel,
        out_shape=[
            jax.ShapeDtypeStruct((rows, cols), F32),
            jax.ShapeDtypeStruct((tiles, 8, LANES), F32),
            jax.ShapeDtypeStruct(spans, I32),
        ],
        in_specs=[vmem],
        out_specs=[vmem, vmem, smem],
        scratch_shapes=[pltpu.VMEM(spans, I32), pltpu.SemaphoreType.DMA],
        compiler_params=pltpu.CompilerParams(vmem_limit_bytes=16 * 2**20),
        cost_estimate=cost(8),
        name="deposit",
    )(recv)


def sample_kernel(grad_high, grad_low, buf, spans, out, values):
    n = out.shape[0]
    rows, cols = grad_high.shape
    bins = cols // CHUNK
    shift = int(math.log2(cols))
    starts = [q * tiles_of_bin(n) for q in range(bins)]

    def sample(chunk, carry):
        for q in range(bins):
            first = starts[q] + 2 * chunk
            _, frac_row, frac_col, place = shot_rows(buf, first, CHUNK)
            pixel_row = jnp.minimum(place >> shift, rows - 2)
            high, low = col_table(place, frac_col, cols, q)
            window = slice(q * CHUNK, (q + 1) * CHUNK)
            along = (
                dot(grad_high[:, window], high)
                + dot(grad_low[:, window], high)
                + dot(grad_high[:, window], low)
            )
            here = iota((rows, CHUNK), 0)
            weight = jnp.where(
                here == pixel_row, 1.0 - frac_row, jnp.where(here == pixel_row + 1, frac_row, 0.0)
            )
            got = jnp.sum(weight * along, axis=0, keepdims=True)
            values[first, 0:1] = got[:, :LANES]
            values[first + 1, 0:1] = got[:, LANES:]
        return carry

    lax.fori_loop(0, spans[0, LANES - 1], sample, 0)

    lane, row = iota((1, LANES), 1), iota((8, LANES), 0)

    def take(begin, amount, at):
        lane_at, tile_at = at & (LANES - 1), at >> 7
        both = jnp.where(lane >= lane_at, values[tile_at, 0:1], values[tile_at + 1, 0:1])
        moved = pltpu.roll(both, (begin - at) & (LANES - 1), axis=1)
        return jnp.where((lane >= begin) & (lane < begin + amount), moved, 0.0)

    def spread(i, at):
        at = list(at)
        both = []
        for half in range(2):
            total = jnp.zeros((1, LANES), F32)
            for q in range(bins):
                begin, amount = spans[q, half * n + i], spans[bins + q, half * n + i]
                total = total + take(begin, amount, at[q])
                at[q] = at[q] + amount
            both.append(total)
        out[i] = jnp.where(row == 0, both[0], jnp.where(row == 1, both[1], 0.0))
        return at

    lax.fori_loop(0, n, spread, [jnp.int32(s * LANES) for s in starts])


def sample(n, grad_high, grad_low, buf, spans):
    vmem = pl.BlockSpec(memory_space=pltpu.VMEM)
    smem = pl.BlockSpec(memory_space=pltpu.SMEM)
    return pl.pallas_call(
        sample_kernel,
        out_shape=jax.ShapeDtypeStruct((n, 8, LANES), F32),
        in_specs=[vmem, vmem, vmem, smem],
        out_specs=vmem,
        scratch_shapes=[pltpu.VMEM(buf.shape, F32)],
        compiler_params=pltpu.CompilerParams(vmem_limit_bytes=16 * 2**20),
        cost_estimate=cost(8),
        name="sample",
    )(grad_high, grad_low, buf, spans)


SIDES = ((-1, 0), (1, 0), (0, -1), (0, 1), (-1, -1), (-1, 1), (1, -1), (1, 1))


def blur_kernel(
    dims, dose, target_far, zone, zone_weights, row_high_far, row_low_far, col_high_far, col_low_far,
    exposure, grad_high, grad_low,
    target, row_high, row_low, col_high, col_low, near_sem,
    zone_own, zone_in, halo_rows, halo_cols, halo_corners, dose_high, dose_low, part_high, part_low,
    error, weight, dose_send, dose_recv, error_send, error_recv, zone_send, zone_recv,
):
    n_row, n_col = dims
    rows, cols = dose.shape
    wide = cols + 2 * SIDE
    row, col = lax.axis_index("row"), lax.axis_index("col")

    def exists(side):
        down, right = SIDES[side]
        tests = []
        if down:
            tests.append(row > 0 if down < 0 else row < n_row - 1)
        if right:
            tests.append(col > 0 if right < 0 else col < n_col - 1)
        return functools.reduce(jnp.logical_and, tests)

    def neighbour(side):
        down, right = SIDES[side]
        return (row + down, col + right)

    def opposite(side):
        down, right = SIDES[side]
        return SIDES.index((-down, -right))

    def landing(turn, side):
        if side < 2:
            return halo_rows.at[turn, side]
        if side < 4:
            return halo_cols.at[turn, side - 2]
        return halo_corners.at[turn, side - 4]

    def edge(field, side):
        down, right = SIDES[side]
        high = slice(None) if not down else (pl.ds(0, HALO) if down < 0 else pl.ds(rows - HALO, HALO))
        across = slice(None) if not right else (pl.ds(0, SIDE) if right < 0 else pl.ds(cols - SIDE, SIDE))
        return field.at[high, across]

    def halo_copy(field, turn, side):
        sends, recvs = (dose_send, dose_recv) if turn == 0 else (error_send, error_recv)
        return pltpu.make_async_remote_copy(
            src_ref=edge(field, side),
            dst_ref=landing(turn, opposite(side)),
            send_sem=sends.at[side],
            recv_sem=recvs.at[opposite(side)],
            device_id=neighbour(side),
            device_id_type=MESH,
        )

    def zone_copy(side):
        return pltpu.make_async_remote_copy(
            src_ref=zone_own,
            dst_ref=zone_in.at[opposite(side)],
            send_sem=zone_send.at[side],
            recv_sem=zone_recv.at[opposite(side)],
            device_id=neighbour(side),
            device_id_type=MESH,
        )

    near = [
        pltpu.make_async_copy(far, close, near_sem.at[i])
        for i, (far, close) in enumerate(
            (
                (row_high_far, row_high),
                (row_low_far, row_low),
                (col_high_far, col_high),
                (col_low_far, col_low),
                (target_far, target),
            )
        )
    ]
    for copy in near:
        copy.start()
    barrier = pltpu.get_barrier_semaphore()
    zone_own[...] = jnp.zeros_like(zone_own)
    zone_own[0 : zone.shape[0], 0 : zone.shape[1]] = zone[...]
    for side in range(8):

        @pl.when(jnp.logical_not(exists(side)))
        def _(side=side):
            for turn in range(2):
                spot = landing(turn, side)
                spot[...] = jnp.zeros_like(spot)
            zone_in[side] = jnp.zeros_like(zone_own)

    for side in range(8):

        @pl.when(exists(side))
        def _(side=side):
            pl.semaphore_signal(barrier, inc=1, device_id=neighbour(side), device_id_type=MESH)

    tall = 1 + jnp.where(row > 0, 1, 0) + jnp.where(row < n_row - 1, 1, 0)
    broad = 1 + jnp.where(col > 0, 1, 0) + jnp.where(col < n_col - 1, 1, 0)
    pl.semaphore_wait(barrier, tall * broad - 1)

    for side in range(8):

        @pl.when(exists(side))
        def _(side=side):
            halo_copy(dose, 0, side).start()
            zone_copy(side).start()

    def await_halo(field, turn, sides):
        for side in sides:

            @pl.when(exists(side))
            def _(side=side):
                halo_copy(field, turn, opposite(side)).wait_recv()

    def put_dose(value, first_row, first_col):
        high, low = split(value)
        here = pl.ds(first_row, value.shape[0]), pl.ds(first_col, value.shape[1])
        dose_high[here] = high
        dose_low[here] = low

    def along_cols(field, kernel):
        count = field.shape[0]
        stacked = [
            jnp.concatenate([part[:, b : b + 2 * CHUNK] for b in range(0, cols, CHUNK)], axis=0)
            for part in split(field)
        ]
        high, low = stacked
        out = (
            dot(high, col_high[kernel]) + dot(low, col_high[kernel]) + dot(high, col_low[kernel])
        )
        return jnp.concatenate(
            [out[i * count : (i + 1) * count] for i in range(cols // CHUNK)], axis=1
        )

    windows = {
        "top": (0, HALO, 0, 0),
        "mid": (HALO, 2 * HALO, HALO, 0),
        "low": (rows - HALO, HALO, 2 * HALO, HALO),
    }

    def row_blur(kernel, window, in_high, in_low):
        first, count, begin, band = windows[window]
        take = pl.ds(kernel * 2 * HALO + band, count)
        here = pl.ds(begin, 4 * HALO)
        high, low = row_high[take], row_low[take]
        return dot(high, in_high[here]) + dot(low, in_high[here]) + dot(high, in_low[here])

    def forward(window):
        first, count, _, _ = windows[window]
        total = [jnp.zeros((HALO, cols), F32) for _ in range(count // HALO)]
        for kernel in range(3):
            field = along_cols(row_blur(kernel, window, dose_high, dose_low), kernel)
            for i in range(count // HALO):
                square = 8 * kernel + 1 + first // HALO + i
                factor = weight[square : square + 1, SIDE : SIDE + cols]
                total[i] = total[i] + factor * field[i * HALO : (i + 1) * HALO]
        for i in range(count // HALO):
            here = pl.ds(first + i * HALO, HALO)
            exposure[here] = total[i]
            error[here] = total[i] - target[here]

    def put_part(value, first_row, first_col):
        across = pl.ds(first_col, value.shape[1])
        for i in range(value.shape[0] // HALO):
            square = first_row // HALO + i
            here = pl.ds(first_row + i * HALO, HALO)
            piece = value[i * HALO : (i + 1) * HALO]
            for kernel in range(3):
                factor = weight[8 * kernel + square : 8 * kernel + square + 1, across]
                high, low = split(factor * piece)
                part_high[kernel, here, across] = high
                part_low[kernel, here, across] = low

    def backward(window):
        first, count, _, _ = windows[window]
        total = jnp.zeros((count, cols), F32)
        for kernel in range(3):
            field = row_blur(kernel, window, part_high.at[kernel], part_low.at[kernel])
            total = total + along_cols(field, kernel)
        high, low = split(total)
        here = pl.ds(first, count)
        grad_high[here] = high
        grad_low[here] = low

    def zone_table():
        sub, lane = iota((8, LANES), 0), iota((8, LANES), 1)
        high, across = zone.shape
        own = pltpu.roll(pltpu.roll(zone_own[...], 1, axis=0), 2, axis=1)
        table = own
        for side in range(8):
            down, right = SIDES[side]
            got = zone_in[side]
            got = pltpu.roll(got, (1 + down * high) % 8, axis=0)
            got = pltpu.roll(got, (2 + right * across) % LANES, axis=1)
            row_ok = (sub == 0) if down < 0 else (sub == high + 1) if down > 0 else (sub >= 1) & (sub <= high)
            col_ok = (
                (lane == 1) if right < 0 else (lane == across + 2) if right > 0 else (lane >= 2) & (lane < across + 2)
            )
            table = jnp.where(row_ok & col_ok, got, table)
        picked = []
        for kernel in range(3):
            value = jnp.zeros((8, LANES), F32)
            for z in range(ZONES):
                value = jnp.where(table == z, zone_weights[kernel, z], value)
            picked.append(value)
        spread = iota((LANES, wide), 0) == iota((LANES, wide), 1) // HALO
        return picked, spread

    put_dose(dose[...], HALO, SIDE)
    for side in range(8):

        @pl.when(exists(side))
        def _(side=side):
            zone_copy(opposite(side)).wait_recv()

    picked, spread = zone_table()
    spread = jnp.where(spread, 1.0, 0.0).astype(BF16)
    stacked = jnp.concatenate(picked, axis=0)
    first_part = stacked.astype(BF16)
    rest = stacked - first_part.astype(F32)
    second_part = rest.astype(BF16)
    third_part = (rest - second_part.astype(F32)).astype(BF16)
    weight[...] = dot(first_part, spread) + dot(second_part, spread) + dot(third_part, spread)

    for copy in near:
        copy.wait()
    await_halo(dose, 0, (2, 3))
    put_dose(halo_cols[0, 0], HALO, 0)
    put_dose(halo_cols[0, 1], HALO, SIDE + cols)
    forward("mid")
    await_halo(dose, 0, (0, 1, 4, 5, 6, 7))
    for place, first_row in ((0, 0), (1, HALO + rows)):
        put_dose(halo_rows[0, place], first_row, SIDE)
        put_dose(halo_corners[0, 2 * place], first_row, 0)
        put_dose(halo_corners[0, 2 * place + 1], first_row, SIDE + cols)
    forward("top")
    forward("low")
    for side in range(8):

        @pl.when(exists(side))
        def _(side=side):
            halo_copy(error, 1, side).start()

    put_part(error[...], HALO, SIDE)
    await_halo(error, 1, (2, 3))
    put_part(halo_cols[1, 0], HALO, 0)
    put_part(halo_cols[1, 1], HALO, SIDE + cols)
    backward("mid")
    await_halo(error, 1, (0, 1, 4, 5, 6, 7))
    for place, first_row in ((0, 0), (1, HALO + rows)):
        put_part(halo_rows[1, place], first_row, SIDE)
        put_part(halo_corners[1, 2 * place], first_row, 0)
        put_part(halo_corners[1, 2 * place + 1], first_row, SIDE + cols)
    backward("top")
    backward("low")
    for side in range(8):

        @pl.when(exists(side))
        def _(side=side):
            halo_copy(dose, 0, side).wait_send()
            halo_copy(error, 1, side).wait_send()
            zone_copy(side).wait_send()


def blur(dims, dose, target, zone, zone_weights):
    rows, cols = dose.shape
    wide, high = cols + 2 * SIDE, rows + 2 * HALO
    vmem = pl.BlockSpec(memory_space=pltpu.VMEM)
    smem = pl.BlockSpec(memory_space=pltpu.SMEM)
    far = pl.BlockSpec(memory_space=pltpu.HBM)
    dma = pltpu.SemaphoreType.DMA((8,))
    bands = (*row_bands(), *col_bands())
    return pl.pallas_call(
        functools.partial(blur_kernel, dims),
        out_shape=[
            jax.ShapeDtypeStruct((rows, cols), F32),
            jax.ShapeDtypeStruct((rows, cols), BF16),
            jax.ShapeDtypeStruct((rows, cols), BF16),
        ],
        in_specs=[vmem, far, vmem, smem, far, far, far, far],
        out_specs=[vmem] * 3,
        scratch_shapes=[
            pltpu.VMEM((rows, cols), F32),
            *[pltpu.VMEM(band.shape, BF16) for band in bands],
            pltpu.SemaphoreType.DMA((5,)),
            pltpu.VMEM((8, LANES), I32),
            pltpu.VMEM((8, 8, LANES), I32),
            pltpu.VMEM((2, 2, HALO, cols), F32),
            pltpu.VMEM((2, 2, rows, SIDE), F32),
            pltpu.VMEM((2, 4, HALO, SIDE), F32),
            pltpu.VMEM((high, wide), BF16),
            pltpu.VMEM((high, wide), BF16),
            pltpu.VMEM((3, high, wide), BF16),
            pltpu.VMEM((3, high, wide), BF16),
            pltpu.VMEM((rows, cols), F32),
            pltpu.VMEM((24, wide), F32),
            dma, dma, dma, dma, dma, dma,
        ],
        compiler_params=pltpu.CompilerParams(
            collective_id=1, has_side_effects=True, vmem_limit_bytes=32 * 2**20
        ),
        cost_estimate=cost(25),
        name="blur",
    )(dose, target, zone, zone_weights, *bands)


def per_device(dims, shot_dose, shot_frac, shot_pos, block_count, shot_tile, zone, zone_weights, target):
    n = dims[1]
    rows, cols = target.shape
    count, tile = block_count.reshape(1, -1), shot_tile.reshape(1, -1)
    recv, order = route(n, cols, shot_dose, shot_frac, shot_pos, count, tile)
    dose, buf, spans = deposit(recv, rows, cols)
    exposure, grad_high, grad_low = blur(dims, dose, target, zone, zone_weights.T)
    slot_grad = sample(n, grad_high, grad_low, buf, spans)
    return exposure, give_back(n, slot_grad, tile, order)


def solution(mesh):
    dims = (mesh.shape["row"], mesh.shape["col"])
    return jax.shard_map(
        functools.partial(per_device, dims),
        mesh=mesh,
        in_specs=(
            P(("row", "col"), None),
            P(None, ("row", "col"), None),
            P(("row", "col"), None),
            P(("row", "col")),
            P(("row", "col"), None),
            P("row", "col"),
            P(),
            P("row", "col"),
        ),
        out_specs=(P("row", "col"), P(("row", "col"), None)),
        check_vma=False,
    )
```

```python
import functools
import math

import jax
import jax.numpy as jnp
import numpy as np
from jax import lax
from jax.experimental import pallas as pl
from jax.experimental.pallas import tpu as pltpu
from jax.sharding import PartitionSpec as P

HALO = 64
ZONES = 8
LANES = 128
CHUNK = 256
SIDE = 128
SIGMAS = (0.125 * HALO, 0.25 * HALO, 0.5 * HALO)
MESH = pl.DeviceIdType.MESH
F32, BF16, I32 = jnp.float32, jnp.bfloat16, jnp.int32


def cost(us):
    return pl.CostEstimate(flops=0, bytes_accessed=int(us * 3.0e6), transcendentals=0)


def iota(shape, dim):
    return lax.broadcasted_iota(I32, shape, dim)


def split(x):
    high = x.astype(BF16)
    return high, (x - high.astype(F32)).astype(BF16)


def dot(a, b):
    return jnp.dot(a, b, preferred_element_type=F32)


def dot_nt(a, b):
    return lax.dot_general(a, b, (((1,), (1,)), ((), ())), preferred_element_type=F32)


def pick(onehot, x):
    first = x.astype(BF16)
    rest = x - first.astype(F32)
    second = rest.astype(BF16)
    third = (rest - second.astype(F32)).astype(BF16)
    return dot(onehot, first) + dot(onehot, second) + dot(onehot, third)


def taps(offset, sigma):
    reach = np.arange(-HALO, HALO + 1).astype(np.float64)
    total = float(np.exp(-reach * reach / (2.0 * sigma * sigma)).sum())
    value = jnp.exp(offset * offset * (-1.0 / (2.0 * sigma * sigma))) * (1.0 / total)
    return jnp.where(jnp.abs(offset) <= float(HALO), value, 0.0)


def far(x):
    return pltpu.with_memory_space_constraint(x, pltpu.HBM)


def slots_of(tile, width):
    n = tile.shape[0]
    times = width // n
    own, lane = iota((n, width), 0), iota((n, width), 1)
    other = lane // times
    tile_row = jnp.sum(jnp.where(own == other, tile, 0), axis=0, keepdims=True)
    same = tile == tile_row
    rank_row = jnp.sum(jnp.where(same & (own < other), 1, 0), axis=0, keepdims=True)
    once = lane % times == 0
    rank_col = jnp.sum(jnp.where(same & (other < own) & once, 1, 0), axis=1, keepdims=True)
    return tile * 2 + rank_col, tile_row * 2 + rank_row


def upright(line):
    n = line.shape[1]
    return jnp.sum(jnp.where(iota((n, n), 0) == iota((n, n), 1), line, 0), axis=1, keepdims=True)


def column_class(pixel):
    return 2 * (pixel >> 8) + jnp.where((pixel & (CHUNK - 1)) == CHUNK - 1, 1, 0)


def greet_all(n, me, row):
    barrier = pltpu.get_barrier_semaphore()

    def greet(step, carry):
        peer = lax.rem(me + step, n)
        pl.semaphore_signal(barrier, inc=1, device_id=(row, peer), device_id_type=MESH)
        return carry

    lax.fori_loop(1, n, greet, 0)
    return barrier


def exchange(n, me, row, source, target, send_sem, recv_sem):
    def copy_to(peer, slot):
        return pltpu.make_async_remote_copy(
            src_ref=source.at[peer],
            dst_ref=target.at[slot],
            send_sem=send_sem.at[peer],
            recv_sem=recv_sem.at[slot],
            device_id=(row, peer),
            device_id_type=MESH,
        )

    def start(step, carry):
        copy_to(lax.rem(me + step, n), me).start()
        return carry

    def finish(step, carry):
        peer = lax.rem(me + n - step, n)
        copy_to(peer, peer).wait_recv()
        return carry

    def drain(step, carry):
        copy_to(lax.rem(me + step, n), me).wait_send()
        return carry

    lax.fori_loop(1, n, start, 0)
    target[pl.ds(me, 1)] = source[pl.ds(me, 1)]
    lax.fori_loop(1, n, finish, 0)
    lax.fori_loop(1, n, drain, 0)


def route_kernel(
    n, cols, dose, frac, pos, count, tile, recv, order, parts, ordered, send, send_sem, recv_sem
):
    row, me = lax.axis_index("row"), lax.axis_index("col")
    barrier = greet_all(n, me, row)
    blocks = tile.shape[1]
    live = iota((blocks, LANES), 1) < upright(count[...])
    dead = 2 * (cols // CHUNK) - 1
    kind = jnp.where(live, column_class(jnp.minimum(pos[...] & (cols - 1), cols - 2)), dead)
    masks = [jnp.where(kind == j, 1.0, 0.0) for j in range(dead + 1)]
    before = jnp.where(iota((LANES, LANES), 0) < iota((LANES, LANES), 1), 1.0, 0.0).astype(BF16)
    prefix = dot(jnp.concatenate(masks, axis=0).astype(BF16), before)
    start = jnp.zeros((blocks, 1), F32)
    rank = jnp.zeros((blocks, LANES), F32)
    for j, mask in enumerate(masks):
        rank = rank + mask * (prefix[j * blocks : (j + 1) * blocks] + start)
        start = start + jnp.sum(mask, axis=1, keepdims=True)
    rank = rank.astype(I32)
    order[...] = rank
    fields = [
        jnp.where(live, dose[...], 0.0),
        frac[0],
        frac[1],
        jnp.where(live, pos[...] + 1, 0).astype(F32),
    ]
    for f, field in enumerate(fields):
        for part in range(3):
            piece = field.astype(BF16).astype(F32)
            parts[:, 4 * part + f] = piece
            field = field - piece
        parts[:, 12 + f] = jnp.zeros((blocks, LANES), F32)
    target = iota((LANES, LANES), 0)
    for b in range(blocks):
        moves = jnp.where(target == rank[b : b + 1], 1.0, 0.0).astype(BF16)
        ordered[b] = dot_nt(parts[b].astype(BF16), moves)
    width = 16 * blocks
    _, placed = slots_of(upright(tile[...]), width)
    out, col = iota((8 * n, width), 0), iota((8 * n, width), 1)
    chosen = (out // 4 == placed) & (out % 4 == col % 4) & (col % 16 < 12)
    onehot = jnp.where(chosen, 1.0, 0.0).astype(BF16)
    send[...] = dot(onehot, ordered[...].reshape(width, LANES).astype(BF16)).reshape(n, 8, LANES)
    pl.semaphore_wait(barrier, n - 1)
    exchange(n, me, row, send, recv, send_sem, recv_sem)


def route(n, cols, dose, frac, pos, count, tile):
    vmem = pl.BlockSpec(memory_space=pltpu.VMEM)
    blocks = tile.shape[1]
    return pl.pallas_call(
        functools.partial(route_kernel, n, cols),
        out_shape=[
            jax.ShapeDtypeStruct((n, 8, LANES), F32),
            jax.ShapeDtypeStruct((blocks, LANES), I32),
        ],
        in_specs=[vmem] * 5,
        out_specs=[vmem] * 2,
        scratch_shapes=[
            pltpu.VMEM((blocks, 16, LANES), F32),
            pltpu.VMEM((blocks, 16, LANES), F32),
            pltpu.VMEM((n, 8, LANES), F32),
            pltpu.SemaphoreType.DMA((n,)),
            pltpu.SemaphoreType.DMA((n,)),
        ],
        compiler_params=pltpu.CompilerParams(
            collective_id=0, has_side_effects=True, vmem_limit_bytes=8 * 2**20
        ),
        cost_estimate=cost(10),
        name="route",
    )(*(far(x) for x in (dose, frac, pos, count, tile)))


def return_kernel(n, grads, tile, order, out, back, send_sem, recv_sem):
    row, me = lax.axis_index("row"), lax.axis_index("col")
    barrier = greet_all(n, me, row)
    blocks = tile.shape[1]
    placed, _ = slots_of(upright(tile[...]), blocks)
    col = iota((blocks, 8 * n), 1)
    chosen = (placed == 2 * (col >> 3) + (col & 7)) & ((col & 7) < 2)
    onehot = jnp.where(chosen, 1.0, 0.0).astype(BF16)
    pl.semaphore_wait(barrier, n - 1)
    exchange(n, me, row, grads, back, send_sem, recv_sem)
    found = pick(onehot, back[...].reshape(8 * n, LANES))
    out[...] = jnp.take_along_axis(found, order[...], axis=1)


def give_back(n, grads, tile, order):
    vmem = pl.BlockSpec(memory_space=pltpu.VMEM)
    return pl.pallas_call(
        functools.partial(return_kernel, n),
        out_shape=jax.ShapeDtypeStruct((tile.shape[1], LANES), F32),
        in_specs=[vmem] * 3,
        out_specs=vmem,
        scratch_shapes=[
            pltpu.VMEM((n, 8, LANES), F32),
            pltpu.SemaphoreType.DMA((n,)),
            pltpu.SemaphoreType.DMA((n,)),
        ],
        compiler_params=pltpu.CompilerParams(
            collective_id=2, has_side_effects=True, vmem_limit_bytes=8 * 2**20
        ),
        cost_estimate=cost(10),
        name="give_back",
    )(grads, far(tile), order)


def shot_rows(buf, first, end):
    lane = iota((8, LANES), 1)
    both = [jnp.where(lane < end, buf[first], 0.0), jnp.where(lane < end - LANES, buf[first + 1], 0.0)]
    line = lambda f: jnp.concatenate([part[f : f + 1] for part in both], axis=1)
    return line(0), line(1), line(2), line(3).astype(I32) - 1


def table(index, low, high, count):
    here = iota((count, index.shape[1]), 0).astype(F32).astype(BF16)
    first = index.astype(F32).astype(BF16)
    second = (index + 1).astype(F32).astype(BF16)
    at_first, at_second = here == first, here == second
    zero = jnp.zeros((), BF16)
    return [jnp.where(at_first, lo, jnp.where(at_second, hi, zero)) for lo, hi in zip(low, high)]


def col_table(place, frac, cols, window):
    pixel = jnp.minimum(place & (cols - 1), cols - 2)
    local = jnp.clip(pixel - window * CHUNK, -2, CHUNK)
    return table(local, split(1.0 - frac), split(frac), CHUNK)


def tiles_of_bin(n):
    return 2 * n + 2


def deposit_kernel(recv, dose, buf, spans, row_spans, sem):
    n = recv.shape[0]
    rows, cols = dose.shape
    bins = cols // CHUNK
    shift = int(math.log2(cols))
    lane = iota((8, LANES), 1)
    ends = []
    for half in range(2):
        place = recv[:, 4 * half + 3, :].astype(I32) - 1
        kind = column_class(jnp.minimum(place & (cols - 1), cols - 2))
        kind = jnp.where(place >= 0, kind, 2 * bins)
        ends.append([jnp.sum(jnp.where(kind <= j, 1, 0), axis=1, keepdims=True) for j in range(2 * bins)])
    which = iota((n, LANES), 1)
    chosen = (lax.rem(which, n) == iota((n, LANES), 0)) & (which < 2 * n)

    def to_lanes(first, second):
        spread = jnp.where(which < n, first, second)
        return jnp.sum(jnp.where(chosen, spread, 0), axis=0, keepdims=True)

    lines = []
    for q in range(bins):
        lines.append(to_lanes(*(e[2 * q - 2] if q else jnp.zeros((n, 1), I32) for e in ends)))
    for q in range(bins):
        lines.append(to_lanes(*(e[2 * q + 1] for e in ends)) - lines[q])
    row_spans[...] = jnp.concatenate(lines, axis=0)
    copy = pltpu.make_async_copy(row_spans, spans, sem)
    copy.start()
    dose[...] = jnp.zeros_like(dose)
    copy.wait()

    def append(block, begin, amount, carry):
        at, current = carry
        lane_at = at & (LANES - 1)
        moved = pltpu.roll(block, (at - begin) & (LANES - 1), axis=1)
        merged = jnp.where(lane < lane_at, current, moved)
        buf[at >> 7] = merged
        full = jnp.full((8, LANES), lane_at + amount, I32) >= LANES
        return at + amount, jnp.where(full, moved, merged)

    def gather(i, carry):
        block = recv[i]
        for half in range(2):
            index = half * n + i
            carry = [
                append(block, spans[q, index], spans[bins + q, index], carry[q]) for q in range(bins)
            ]
            block = pltpu.roll(block, 4, axis=0)
        return carry

    starts = [q * tiles_of_bin(n) for q in range(bins)]
    empty = jnp.zeros((8, LANES), F32)
    found = lax.fori_loop(0, n, gather, [(jnp.int32(s * LANES), empty) for s in starts])
    most = jnp.int32(0)
    for q, (at, last) in enumerate(found):
        buf[at >> 7] = jnp.where(lane < (at & (LANES - 1)), last, 0.0)
        buf[(at >> 7) + 1] = empty
        most = jnp.maximum(most, (at - starts[q] * LANES + CHUNK - 1) >> 8)
    spans[0, LANES - 1] = most

    def deposit(chunk, carry):
        for q in range(bins):
            first = starts[q] + 2 * chunk
            end = found[q][0] - first * LANES
            amount, frac_row, frac_col, place = shot_rows(buf, first, end)
            pixel_row = jnp.minimum(place >> shift, rows - 2)
            row_high, row_low = table(
                pixel_row, split(amount * (1.0 - frac_row)), split(amount * frac_row), rows
            )
            high, low = col_table(place, frac_col, cols, q)
            dose[:, q * CHUNK : (q + 1) * CHUNK] += (
                dot_nt(row_high, high) + dot_nt(row_low, high) + dot_nt(row_high, low)
            )
        return carry

    lax.fori_loop(0, most, deposit, 0)


def deposit(recv, rows, cols):
    vmem = pl.BlockSpec(memory_space=pltpu.VMEM)
    smem = pl.BlockSpec(memory_space=pltpu.SMEM)
    tiles = (cols // CHUNK) * tiles_of_bin(recv.shape[0])
    spans = (2 * (cols // CHUNK), LANES)
    return pl.pallas_call(
        deposit_kernel,
        out_shape=[
            jax.ShapeDtypeStruct((rows, cols), F32),
            jax.ShapeDtypeStruct((tiles, 8, LANES), F32),
            jax.ShapeDtypeStruct(spans, I32),
        ],
        in_specs=[vmem],
        out_specs=[vmem, vmem, smem],
        scratch_shapes=[pltpu.VMEM(spans, I32), pltpu.SemaphoreType.DMA],
        compiler_params=pltpu.CompilerParams(vmem_limit_bytes=16 * 2**20),
        cost_estimate=cost(8),
        name="deposit",
    )(recv)


def sample_kernel(grad_high, grad_low, buf, spans, exposure, out, exposure_out, values, sem):
    leave = pltpu.make_async_copy(exposure, exposure_out, sem)
    leave.start()
    n = out.shape[0]
    rows, cols = grad_high.shape
    bins = cols // CHUNK
    shift = int(math.log2(cols))
    starts = [q * tiles_of_bin(n) for q in range(bins)]

    def sample(chunk, carry):
        for q in range(bins):
            first = starts[q] + 2 * chunk
            _, frac_row, frac_col, place = shot_rows(buf, first, CHUNK)
            pixel_row = jnp.minimum(place >> shift, rows - 2)
            high, low = col_table(place, frac_col, cols, q)
            window = slice(q * CHUNK, (q + 1) * CHUNK)
            along = (
                dot(grad_high[:, window], high)
                + dot(grad_low[:, window], high)
                + dot(grad_high[:, window], low)
            )
            here = iota((rows, CHUNK), 0)
            weight = jnp.where(
                here == pixel_row, 1.0 - frac_row, jnp.where(here == pixel_row + 1, frac_row, 0.0)
            )
            got = jnp.sum(weight * along, axis=0, keepdims=True)
            values[first, 0:1] = got[:, :LANES]
            values[first + 1, 0:1] = got[:, LANES:]
        return carry

    lax.fori_loop(0, spans[0, LANES - 1], sample, 0)

    lane, row = iota((1, LANES), 1), iota((8, LANES), 0)

    def take(begin, amount, at):
        lane_at, tile_at = at & (LANES - 1), at >> 7
        both = jnp.where(lane >= lane_at, values[tile_at, 0:1], values[tile_at + 1, 0:1])
        moved = pltpu.roll(both, (begin - at) & (LANES - 1), axis=1)
        return jnp.where((lane >= begin) & (lane < begin + amount), moved, 0.0)

    def spread(i, at):
        at = list(at)
        both = []
        for half in range(2):
            total = jnp.zeros((1, LANES), F32)
            for q in range(bins):
                begin, amount = spans[q, half * n + i], spans[bins + q, half * n + i]
                total = total + take(begin, amount, at[q])
                at[q] = at[q] + amount
            both.append(total)
        out[i] = jnp.where(row == 0, both[0], jnp.where(row == 1, both[1], 0.0))
        return at

    lax.fori_loop(0, n, spread, [jnp.int32(s * LANES) for s in starts])
    leave.wait()


def sample(n, grad_high, grad_low, buf, spans, exposure):
    vmem = pl.BlockSpec(memory_space=pltpu.VMEM)
    smem = pl.BlockSpec(memory_space=pltpu.SMEM)
    return pl.pallas_call(
        sample_kernel,
        out_shape=[
            jax.ShapeDtypeStruct((n, 8, LANES), F32),
            jax.ShapeDtypeStruct(exposure.shape, F32),
        ],
        in_specs=[vmem, vmem, vmem, smem, pl.BlockSpec(memory_space=pl.ANY)],
        out_specs=[vmem, pl.BlockSpec(memory_space=pl.ANY)],
        scratch_shapes=[pltpu.VMEM(buf.shape, F32), pltpu.SemaphoreType.DMA],
        compiler_params=pltpu.CompilerParams(vmem_limit_bytes=16 * 2**20),
        cost_estimate=cost(8),
        name="sample",
    )(grad_high, grad_low, buf, spans, exposure)


SIDES = ((-1, 0), (1, 0), (0, -1), (0, 1), (-1, -1), (-1, 1), (1, -1), (1, 1))
PIECE_SIDE = (0, 0, 0, 0, 1, 1, 1, 1, 2, 3, 4, 5, 6, 7)
OPPOSITE = (4, 5, 6, 7, 0, 1, 2, 3, 9, 8, 13, 12, 11, 10)


def blur_kernel(
    dims, dose, target_far, zone, zone_weights,
    exposure, grad_high, grad_low,
    target, near_sem, mid_high, mid_low, edge_high, edge_low, col_high, col_low,
    zone_own, zone_in, halo_rows, halo_cols, halo_corners, dose_high, dose_low, part_high, part_low,
    mixed_high, mixed_low, error, weight, sends, recvs, zone_send, zone_recv,
):
    n_row, n_col = dims
    rows, cols = dose.shape
    wide = cols + 2 * SIDE
    steps = cols // CHUNK
    row, col = lax.axis_index("row"), lax.axis_index("col")

    def exists(side):
        down, right = SIDES[side]
        tests = []
        if down:
            tests.append(row > 0 if down < 0 else row < n_row - 1)
        if right:
            tests.append(col > 0 if right < 0 else col < n_col - 1)
        return functools.reduce(jnp.logical_and, tests)

    def neighbour(side):
        down, right = SIDES[side]
        return (row + down, col + right)

    def landing(turn, piece):
        if piece < 8:
            return halo_rows.at[turn, piece // 4, :, pl.ds(piece % 4 * CHUNK, CHUNK)]
        if piece < 10:
            return halo_cols.at[turn, piece - 8]
        return halo_corners.at[turn, piece - 10]

    def edge(field, piece):
        down, right = SIDES[PIECE_SIDE[piece]]
        high = pl.ds(0, rows) if not down else (pl.ds(0, HALO) if down < 0 else pl.ds(rows - HALO, HALO))
        if piece < 8:
            across = pl.ds(piece % 4 * CHUNK, CHUNK)
        else:
            across = pl.ds(0, SIDE) if right < 0 else pl.ds(cols - SIDE, SIDE)
        return field.at[high, across]

    def halo_copy(field, turn, piece):
        return pltpu.make_async_remote_copy(
            src_ref=edge(field, piece),
            dst_ref=landing(turn, OPPOSITE[piece]),
            send_sem=sends.at[turn, piece],
            recv_sem=recvs.at[turn, OPPOSITE[piece]],
            device_id=neighbour(PIECE_SIDE[piece]),
            device_id_type=MESH,
        )

    def zone_copy(side):
        down, right = SIDES[side]
        there = SIDES.index((-down, -right))
        return pltpu.make_async_remote_copy(
            src_ref=zone_own,
            dst_ref=zone_in.at[there],
            send_sem=zone_send.at[side],
            recv_sem=zone_recv.at[there],
            device_id=neighbour(side),
            device_id_type=MESH,
        )

    def by_side(pieces, act):
        for side in sorted({PIECE_SIDE[piece] for piece in pieces}, key=[PIECE_SIDE[p] for p in pieces].index):

            @pl.when(exists(side))
            def _(side=side):
                for piece in pieces:
                    if PIECE_SIDE[piece] == side:
                        act(piece)

    def send(field, turn, pieces):
        by_side(pieces, lambda piece: halo_copy(field, turn, piece).start())

    def await_halo(field, turn, pieces):
        by_side(pieces, lambda piece: halo_copy(field, turn, OPPOSITE[piece]).wait_recv())

    near = pltpu.make_async_copy(target_far, target, near_sem)
    near.start()
    barrier = pltpu.get_barrier_semaphore()
    zone_own[...] = jnp.zeros_like(zone_own)
    zone_own[0 : zone.shape[0], 0 : zone.shape[1]] = zone[...]
    for side in range(8):

        @pl.when(jnp.logical_not(exists(side)))
        def _(side=side):
            for turn in range(2):
                if side < 2:
                    halo_rows[turn, side] = jnp.zeros((HALO, cols), F32)
                elif side < 4:
                    halo_cols[turn, side - 2] = jnp.zeros((rows, SIDE), F32)
                else:
                    halo_corners[turn, side - 4] = jnp.zeros((HALO, SIDE), F32)
            zone_in[side] = jnp.zeros_like(zone_own)

    for side in range(8):

        @pl.when(exists(side))
        def _(side=side):
            pl.semaphore_signal(barrier, inc=1, device_id=neighbour(side), device_id_type=MESH)

    for kernel, sigma in enumerate(SIGMAS):
        shape = (2 * HALO, 4 * HALO)
        high, low = split(taps((iota(shape, 1) - iota(shape, 0) - HALO).astype(F32), sigma))
        for band, mid, edges in ((high, mid_high, edge_high), (low, mid_low, edge_low)):
            mid[kernel * 2 * HALO : (kernel + 1) * 2 * HALO] = band
            for e in range(2):
                edges[e, kernel * HALO : (kernel + 1) * HALO] = band[e * HALO : (e + 1) * HALO]
        shape = (2 * CHUNK, CHUNK)
        high, low = split(taps((iota(shape, 0) - iota(shape, 1) - SIDE).astype(F32), sigma))
        col_high[kernel] = high
        col_low[kernel] = low

    tall = 1 + jnp.where(row > 0, 1, 0) + jnp.where(row < n_row - 1, 1, 0)
    broad = 1 + jnp.where(col > 0, 1, 0) + jnp.where(col < n_col - 1, 1, 0)
    pl.semaphore_wait(barrier, tall * broad - 1)
    for side in range(8):

        @pl.when(exists(side))
        def _(side=side):
            zone_copy(side).start()

    send(dose, 0, (8, 9, 0, 1, 4, 5, 11, 13))
    send(dose, 0, (2, 3, 6, 7, 10, 12))

    def put_dose(value, first_row, first_col):
        high, low = split(value)
        here = pl.ds(first_row, value.shape[0]), pl.ds(first_col, value.shape[1])
        dose_high[here] = high
        dose_low[here] = low

    def put_part(value, square, first_col):
        across = pl.ds(first_col, value.shape[1])
        here = pl.ds(square * HALO, HALO)
        for kernel in range(3):
            factor = weight[8 * kernel + square : 8 * kernel + square + 1, across]
            high, low = split(factor * value)
            part_high[kernel, here, across] = high
            part_low[kernel, here, across] = low

    def tile_forward(edges, j):
        tile = pl.ds(j * CHUNK, CHUNK)

        def keep(band_high, band_low, first_row, first_out, count):
            here = pl.ds(first_row, 4 * HALO)
            in_high, in_low = dose_high[here, tile], dose_low[here, tile]
            field = dot(band_high, in_high) + dot(band_low, in_high) + dot(band_high, in_low)
            high, low = split(field)
            for kernel in range(3):
                part = slice(kernel * count, (kernel + 1) * count)
                mixed_high[edges, kernel, first_out : first_out + count, tile] = high[part]
                mixed_low[edges, kernel, first_out : first_out + count, tile] = low[part]

        if edges:
            keep(edge_high[0], edge_low[0], 0, 0, HALO)
            keep(edge_high[1], edge_low[1], 2 * HALO, HALO, HALO)
        else:
            keep(mid_high[...], mid_low[...], HALO, 0, 2 * HALO)

    def along_cols(edges, u, kernel):
        take = pl.ds(u * CHUNK, 2 * CHUNK)
        high, low = mixed_high[edges, kernel, :, take], mixed_low[edges, kernel, :, take]
        return dot(high, col_high[kernel]) + dot(low, col_high[kernel]) + dot(high, col_low[kernel])

    def window_forward(edges, u):
        squares = (1, rows // HALO) if edges else (2, 3)
        total = [jnp.zeros((HALO, CHUNK), F32) for _ in range(2)]
        for kernel in range(3):
            field = along_cols(edges, u, kernel)
            for half, square in enumerate(squares):
                line = 8 * kernel + square
                factor = weight[line : line + 1, SIDE + u * CHUNK : SIDE + (u + 1) * CHUNK]
                total[half] = total[half] + factor * field[half * HALO : (half + 1) * HALO]
        for half, square in enumerate(squares):
            here = pl.ds((square - 1) * HALO, HALO), pl.ds(u * CHUNK, CHUNK)
            exposure[here] = total[half]
            wrong = total[half] - target[here]
            error[here] = wrong
            put_part(wrong, square, SIDE + u * CHUNK)

    def tile_backward(edges, j):
        tile = pl.ds(j * CHUNK, CHUNK)

        def keep(kernel, band_high, band_low, first_row, first_out, count):
            here = pl.ds(first_row, 4 * HALO)
            in_high, in_low = part_high[kernel, here, tile], part_low[kernel, here, tile]
            field = dot(band_high, in_high) + dot(band_low, in_high) + dot(band_high, in_low)
            high, low = split(field)
            mixed_high[edges, kernel, first_out : first_out + count, tile] = high
            mixed_low[edges, kernel, first_out : first_out + count, tile] = low

        for kernel in range(3):
            if edges:
                part = pl.ds(kernel * HALO, HALO)
                keep(kernel, edge_high[0, part], edge_low[0, part], 0, 0, HALO)
                keep(kernel, edge_high[1, part], edge_low[1, part], 2 * HALO, HALO, HALO)
            else:
                part = pl.ds(kernel * 2 * HALO, 2 * HALO)
                keep(kernel, mid_high[part], mid_low[part], HALO, 0, 2 * HALO)

    def window_backward(edges, u):
        squares = (1, rows // HALO) if edges else (2, 3)
        high, low = split(sum(along_cols(edges, u, kernel) for kernel in range(3)))
        for half, square in enumerate(squares):
            here = pl.ds((square - 1) * HALO, HALO), pl.ds(u * CHUNK, CHUNK)
            grad_high[here] = high[half * HALO : (half + 1) * HALO]
            grad_low[here] = low[half * HALO : (half + 1) * HALO]

    def zone_table():
        sub, lane = iota((8, LANES), 0), iota((8, LANES), 1)
        high, across = zone.shape
        table = pltpu.roll(pltpu.roll(zone_own[...], 1, axis=0), 2, axis=1)
        for side in range(8):
            down, right = SIDES[side]
            got = pltpu.roll(zone_in[side], (1 + down * high) % 8, axis=0)
            got = pltpu.roll(got, (2 + right * across) % LANES, axis=1)
            row_ok = (sub == 0) if down < 0 else (sub == high + 1) if down > 0 else (sub >= 1) & (sub <= high)
            col_ok = (
                (lane == 1) if right < 0 else (lane == across + 2) if right > 0 else (lane >= 2) & (lane < across + 2)
            )
            table = jnp.where(row_ok & col_ok, got, table)
        picked = []
        for kernel in range(3):
            value = jnp.zeros((8, LANES), F32)
            for z in range(ZONES):
                value = jnp.where(table == z, zone_weights[kernel, z], value)
            picked.append(value)
        return jnp.concatenate(picked, axis=0)

    put_dose(dose[...], HALO, SIDE)
    for side in range(8):

        @pl.when(exists(side))
        def _(side=side):
            down, right = SIDES[side]
            zone_copy(SIDES.index((-down, -right))).wait_recv()

    spread = jnp.where(iota((LANES, wide), 0) == iota((LANES, wide), 1) // HALO, 1.0, 0.0).astype(BF16)
    table = zone_table()
    for _ in range(3):
        piece = table.astype(BF16)
        weight[...] = dot(piece, spread) if _ == 0 else weight[...] + dot(piece, spread)
        table = table - piece.astype(F32)

    def sweep(tile, window, edges, before, after):
        for u in range(steps):
            before(u)
            if u == 0:
                tile(edges, 0)
            tile(edges, u + 1)
            window(edges, u)
            after(u)

    def nothing(u):
        return None

    near.wait()
    await_halo(dose, 0, (8, 9))
    put_dose(halo_cols[0, 0], HALO, 0)
    put_dose(halo_cols[0, 1], HALO, SIDE + cols)
    sweep(tile_forward, window_forward, 0, nothing, nothing)

    def arrive(turn, field, put, u):
        chunks = (0, 1) if u == 0 else (u + 1,) if u + 1 < steps else ()
        corners = (10, 12) if u == 0 else (11, 13) if u == steps - 1 else ()
        await_halo(field, turn, (*chunks, *(4 + c for c in chunks), *corners))
        for side, square in ((0, 0), (1, rows // HALO + 1)):
            for c in chunks:
                put(halo_rows[turn, side, :, c * CHUNK : (c + 1) * CHUNK], square, SIDE + c * CHUNK)
            if u == 0:
                put(halo_corners[turn, 2 * side], square, 0)
            if u == steps - 1:
                put(halo_corners[turn, 2 * side + 1], square, SIDE + cols)

    def send_error(u):
        sides = (8, 10, 12) if u == 0 else (9, 11, 13) if u == steps - 1 else ()
        send(error, 1, (u, 4 + u, *sides))

    sweep(
        tile_forward,
        window_forward,
        1,
        lambda u: arrive(0, dose, lambda value, square, at: put_dose(value, square * HALO, at), u),
        send_error,
    )
    await_halo(error, 1, (8, 9))
    for side, at in ((0, 0), (1, SIDE + cols)):
        for square in range(rows // HALO):
            put_part(halo_cols[1, side, square * HALO : (square + 1) * HALO], 1 + square, at)
    sweep(tile_backward, window_backward, 0, nothing, nothing)
    sweep(tile_backward, window_backward, 1, lambda u: arrive(1, error, put_part, u), nothing)
    by_side(range(14), lambda piece: halo_copy(dose, 0, piece).wait_send())
    by_side(range(14), lambda piece: halo_copy(error, 1, piece).wait_send())
    for side in range(8):

        @pl.when(exists(side))
        def _(side=side):
            zone_copy(side).wait_send()


def blur(dims, dose, target, zone, zone_weights):
    rows, cols = dose.shape
    wide, high = cols + 2 * SIDE, rows + 2 * HALO
    vmem = pl.BlockSpec(memory_space=pltpu.VMEM)
    smem = pl.BlockSpec(memory_space=pltpu.SMEM)
    dma = pltpu.SemaphoreType.DMA
    return pl.pallas_call(
        functools.partial(blur_kernel, dims),
        out_shape=[
            jax.ShapeDtypeStruct((rows, cols), F32),
            jax.ShapeDtypeStruct((rows, cols), BF16),
            jax.ShapeDtypeStruct((rows, cols), BF16),
        ],
        in_specs=[vmem, pl.BlockSpec(memory_space=pl.ANY), vmem, smem],
        out_specs=[vmem] * 3,
        scratch_shapes=[
            pltpu.VMEM((rows, cols), F32),
            dma,
            pltpu.VMEM((6 * HALO, 4 * HALO), BF16),
            pltpu.VMEM((6 * HALO, 4 * HALO), BF16),
            pltpu.VMEM((2, 3 * HALO, 4 * HALO), BF16),
            pltpu.VMEM((2, 3 * HALO, 4 * HALO), BF16),
            pltpu.VMEM((3, 2 * CHUNK, CHUNK), BF16),
            pltpu.VMEM((3, 2 * CHUNK, CHUNK), BF16),
            pltpu.VMEM((8, LANES), I32),
            pltpu.VMEM((8, 8, LANES), I32),
            pltpu.VMEM((2, 2, HALO, cols), F32),
            pltpu.VMEM((2, 2, rows, SIDE), F32),
            pltpu.VMEM((2, 4, HALO, SIDE), F32),
            pltpu.VMEM((high, wide), BF16),
            pltpu.VMEM((high, wide), BF16),
            pltpu.VMEM((3, high, wide), BF16),
            pltpu.VMEM((3, high, wide), BF16),
            pltpu.VMEM((2, 3, 2 * HALO, wide), BF16),
            pltpu.VMEM((2, 3, 2 * HALO, wide), BF16),
            pltpu.VMEM((rows, cols), F32),
            pltpu.VMEM((24, wide), F32),
            dma((2, 14)), dma((2, 14)), dma((8,)), dma((8,)),
        ],
        compiler_params=pltpu.CompilerParams(
            collective_id=1, has_side_effects=True, vmem_limit_bytes=40 * 2**20
        ),
        cost_estimate=cost(25),
        name="blur",
    )(dose, far(target), far(zone), far(zone_weights))


def per_device(dims, shot_dose, shot_frac, shot_pos, block_count, shot_tile, zone, zone_weights, target):
    n = dims[1]
    rows, cols = target.shape
    count, tile = block_count.reshape(1, -1), shot_tile.reshape(1, -1)
    recv, order = route(n, cols, shot_dose, shot_frac, shot_pos, count, tile)
    dose, buf, spans = deposit(recv, rows, cols)
    exposure, grad_high, grad_low = blur(dims, dose, target, zone, zone_weights.T)
    slot_grad, exposure = sample(n, grad_high, grad_low, buf, spans, exposure)
    return exposure, give_back(n, slot_grad, tile, order)


def solution(mesh):
    dims = (mesh.shape["row"], mesh.shape["col"])
    return jax.shard_map(
        functools.partial(per_device, dims),
        mesh=mesh,
        in_specs=(
            P(("row", "col"), None),
            P(None, ("row", "col"), None),
            P(("row", "col"), None),
            P(("row", "col")),
            P(("row", "col"), None),
            P("row", "col"),
            P(),
            P("row", "col"),
        ),
        out_specs=(P("row", "col"), P(("row", "col"), None)),
        check_vma=False,
    )
```

```python
import functools
import math

import jax
import jax.numpy as jnp
import numpy as np
from jax import lax
from jax.experimental import pallas as pl
from jax.experimental.pallas import tpu as pltpu
from jax.sharding import PartitionSpec as P

HALO = 64
ZONES = 8
LANES = 128
CHUNK = 256
SHOTS = 512
SIDE = 128
SIGMAS = (0.125 * HALO, 0.25 * HALO, 0.5 * HALO)
MESH = pl.DeviceIdType.MESH
F32, BF16, I32 = jnp.float32, jnp.bfloat16, jnp.int32


def cost(us):
    return pl.CostEstimate(flops=0, bytes_accessed=int(us * 3.0e6), transcendentals=0)


def iota(shape, dim):
    return lax.broadcasted_iota(I32, shape, dim)


def split(x):
    high = x.astype(BF16)
    return high, (x - high.astype(F32)).astype(BF16)


def dot(a, b):
    return jnp.dot(a, b, preferred_element_type=F32)


def dot_nt(a, b):
    return lax.dot_general(a, b, (((1,), (1,)), ((), ())), preferred_element_type=F32)


def pick(onehot, x):
    first = x.astype(BF16)
    rest = x - first.astype(F32)
    second = rest.astype(BF16)
    third = (rest - second.astype(F32)).astype(BF16)
    return dot(onehot, first) + dot(onehot, second) + dot(onehot, third)


def taps(offset, sigma):
    reach = np.arange(-HALO, HALO + 1).astype(np.float64)
    total = float(np.exp(-reach * reach / (2.0 * sigma * sigma)).sum())
    value = jnp.exp(offset * offset * (-1.0 / (2.0 * sigma * sigma))) * (1.0 / total)
    return jnp.where(jnp.abs(offset) <= float(HALO), value, 0.0)


def far(x):
    return pltpu.with_memory_space_constraint(x, pltpu.HBM)


def slots_of(tile, width):
    n = tile.shape[0]
    times = width // n
    own, lane = iota((n, width), 0), iota((n, width), 1)
    other = lane // times
    tile_row = jnp.sum(jnp.where(own == other, tile, 0), axis=0, keepdims=True)
    same = tile == tile_row
    rank_row = jnp.sum(jnp.where(same & (own < other), 1, 0), axis=0, keepdims=True)
    once = lane % times == 0
    rank_col = jnp.sum(jnp.where(same & (other < own) & once, 1, 0), axis=1, keepdims=True)
    return tile * 2 + rank_col, tile_row * 2 + rank_row


def upright(line):
    n = line.shape[1]
    return jnp.sum(jnp.where(iota((n, n), 0) == iota((n, n), 1), line, 0), axis=1, keepdims=True)


def column_class(pixel):
    return 2 * (pixel >> 8) + jnp.where((pixel & (CHUNK - 1)) == CHUNK - 1, 1, 0)


def greet_all(n, me, row):
    barrier = pltpu.get_barrier_semaphore()

    def greet(step, carry):
        peer = lax.rem(me + step, n)
        pl.semaphore_signal(barrier, inc=1, device_id=(row, peer), device_id_type=MESH)
        return carry

    lax.fori_loop(1, n, greet, 0)
    return barrier


def exchange(n, me, row, source, target, send_sem, recv_sem):
    def copy_to(peer, slot):
        return pltpu.make_async_remote_copy(
            src_ref=source.at[peer],
            dst_ref=target.at[slot],
            send_sem=send_sem.at[peer],
            recv_sem=recv_sem.at[slot],
            device_id=(row, peer),
            device_id_type=MESH,
        )

    def start(step, carry):
        copy_to(lax.rem(me + step, n), me).start()
        return carry

    def finish(step, carry):
        peer = lax.rem(me + n - step, n)
        copy_to(peer, peer).wait_recv()
        return carry

    def drain(step, carry):
        copy_to(lax.rem(me + step, n), me).wait_send()
        return carry

    lax.fori_loop(1, n, start, 0)
    target[pl.ds(me, 1)] = source[pl.ds(me, 1)]
    lax.fori_loop(1, n, finish, 0)
    lax.fori_loop(1, n, drain, 0)


def route_kernel(
    n, cols, dose, frac, pos, count, tile, recv, order, parts, ordered, send, send_sem, recv_sem
):
    row, me = lax.axis_index("row"), lax.axis_index("col")
    barrier = greet_all(n, me, row)
    blocks = tile.shape[1]
    live = iota((blocks, LANES), 1) < upright(count[...])
    dead = 2 * (cols // CHUNK) - 1
    kind = jnp.where(live, column_class(jnp.minimum(pos[...] & (cols - 1), cols - 2)), dead)
    masks = [jnp.where(kind == j, 1.0, 0.0) for j in range(dead + 1)]
    before = jnp.where(iota((LANES, LANES), 0) < iota((LANES, LANES), 1), 1.0, 0.0).astype(BF16)
    prefix = dot(jnp.concatenate(masks, axis=0).astype(BF16), before)
    start = jnp.zeros((blocks, 1), F32)
    rank = jnp.zeros((blocks, LANES), F32)
    for j, mask in enumerate(masks):
        rank = rank + mask * (prefix[j * blocks : (j + 1) * blocks] + start)
        start = start + jnp.sum(mask, axis=1, keepdims=True)
    rank = rank.astype(I32)
    order[...] = rank
    fields = [
        jnp.where(live, dose[...], 0.0),
        frac[0],
        frac[1],
        jnp.where(live, pos[...] + 1, 0).astype(F32),
    ]
    for f, field in enumerate(fields):
        for part in range(3):
            piece = field.astype(BF16).astype(F32)
            parts[:, 4 * part + f] = piece
            field = field - piece
        parts[:, 12 + f] = jnp.zeros((blocks, LANES), F32)
    target = iota((LANES, LANES), 0)
    for b in range(blocks):
        moves = jnp.where(target == rank[b : b + 1], 1.0, 0.0).astype(BF16)
        ordered[b] = dot_nt(parts[b].astype(BF16), moves)
    width = 16 * blocks
    _, placed = slots_of(upright(tile[...]), width)
    out, col = iota((8 * n, width), 0), iota((8 * n, width), 1)
    chosen = (out // 4 == placed) & (out % 4 == col % 4) & (col % 16 < 12)
    onehot = jnp.where(chosen, 1.0, 0.0).astype(BF16)
    send[...] = dot(onehot, ordered[...].reshape(width, LANES).astype(BF16)).reshape(n, 8, LANES)
    pl.semaphore_wait(barrier, n - 1)
    exchange(n, me, row, send, recv, send_sem, recv_sem)


def route(n, cols, dose, frac, pos, count, tile):
    vmem = pl.BlockSpec(memory_space=pltpu.VMEM)
    blocks = tile.shape[1]
    return pl.pallas_call(
        functools.partial(route_kernel, n, cols),
        out_shape=[
            jax.ShapeDtypeStruct((n, 8, LANES), F32),
            jax.ShapeDtypeStruct((blocks, LANES), I32),
        ],
        in_specs=[vmem] * 5,
        out_specs=[vmem] * 2,
        scratch_shapes=[
            pltpu.VMEM((blocks, 16, LANES), F32),
            pltpu.VMEM((blocks, 16, LANES), F32),
            pltpu.VMEM((n, 8, LANES), F32),
            pltpu.SemaphoreType.DMA((n,)),
            pltpu.SemaphoreType.DMA((n,)),
        ],
        compiler_params=pltpu.CompilerParams(
            collective_id=0, has_side_effects=True, vmem_limit_bytes=8 * 2**20
        ),
        cost_estimate=cost(10),
        name="route",
    )(*(far(x) for x in (dose, frac, pos, count, tile)))


def return_kernel(n, grads, tile, order, out, back, send_sem, recv_sem):
    row, me = lax.axis_index("row"), lax.axis_index("col")
    barrier = greet_all(n, me, row)
    blocks = tile.shape[1]
    placed, _ = slots_of(upright(tile[...]), blocks)
    col = iota((blocks, 8 * n), 1)
    chosen = (placed == 2 * (col >> 3) + (col & 7)) & ((col & 7) < 2)
    onehot = jnp.where(chosen, 1.0, 0.0).astype(BF16)
    pl.semaphore_wait(barrier, n - 1)
    exchange(n, me, row, grads, back, send_sem, recv_sem)
    found = pick(onehot, back[...].reshape(8 * n, LANES))
    out[...] = jnp.take_along_axis(found, order[...], axis=1)


def give_back(n, grads, tile, order):
    vmem = pl.BlockSpec(memory_space=pltpu.VMEM)
    return pl.pallas_call(
        functools.partial(return_kernel, n),
        out_shape=jax.ShapeDtypeStruct((tile.shape[1], LANES), F32),
        in_specs=[vmem] * 3,
        out_specs=vmem,
        scratch_shapes=[
            pltpu.VMEM((n, 8, LANES), F32),
            pltpu.SemaphoreType.DMA((n,)),
            pltpu.SemaphoreType.DMA((n,)),
        ],
        compiler_params=pltpu.CompilerParams(
            collective_id=2, has_side_effects=True, vmem_limit_bytes=8 * 2**20
        ),
        cost_estimate=cost(10),
        name="give_back",
    )(grads, far(tile), order)


def shot_rows(buf, first, end):
    lane = iota((8, LANES), 1)
    tiles = [jnp.where(lane < end - i * LANES, buf[first + i], 0.0) for i in range(SHOTS // LANES)]
    line = lambda f: jnp.concatenate([tile[f : f + 1] for tile in tiles], axis=1)
    return line(0), line(1), line(2), line(3).astype(I32) - 1


def table(index, low, high, count):
    here = iota((count, index.shape[1]), 0).astype(F32).astype(BF16)
    first = index.astype(F32).astype(BF16)
    second = (index + 1).astype(F32).astype(BF16)
    at_first, at_second = here == first, here == second
    zero = jnp.zeros((), BF16)
    return [jnp.where(at_first, lo, jnp.where(at_second, hi, zero)) for lo, hi in zip(low, high)]


def col_table(place, frac, cols, window):
    pixel = jnp.minimum(place & (cols - 1), cols - 2)
    local = jnp.clip(pixel - window * CHUNK, -2, CHUNK)
    return table(local, split(1.0 - frac), split(frac), CHUNK)


def tiles_of_bin(n):
    return 2 * n + 2


def deposit_kernel(recv, dose, buf, spans, row_spans, sem):
    n = recv.shape[0]
    rows, cols = dose.shape
    bins = cols // CHUNK
    shift = int(math.log2(cols))
    lane = iota((8, LANES), 1)
    ends = []
    for half in range(2):
        place = recv[:, 4 * half + 3, :].astype(I32) - 1
        kind = column_class(jnp.minimum(place & (cols - 1), cols - 2))
        kind = jnp.where(place >= 0, kind, 2 * bins)
        ends.append([jnp.sum(jnp.where(kind <= j, 1, 0), axis=1, keepdims=True) for j in range(2 * bins)])
    which = iota((n, LANES), 1)
    chosen = (lax.rem(which, n) == iota((n, LANES), 0)) & (which < 2 * n)

    def to_lanes(first, second):
        spread = jnp.where(which < n, first, second)
        return jnp.sum(jnp.where(chosen, spread, 0), axis=0, keepdims=True)

    lines = []
    for q in range(bins):
        lines.append(to_lanes(*(e[2 * q - 2] if q else jnp.zeros((n, 1), I32) for e in ends)))
    for q in range(bins):
        lines.append(to_lanes(*(e[2 * q + 1] for e in ends)) - lines[q])
    row_spans[...] = jnp.concatenate(lines, axis=0)
    copy = pltpu.make_async_copy(row_spans, spans, sem)
    copy.start()
    dose[...] = jnp.zeros_like(dose)
    copy.wait()

    def append(block, begin, amount, carry):
        at, current = carry
        lane_at = at & (LANES - 1)
        moved = pltpu.roll(block, (at - begin) & (LANES - 1), axis=1)
        merged = jnp.where(lane < lane_at, current, moved)
        buf[at >> 7] = merged
        full = jnp.full((8, LANES), lane_at + amount, I32) >= LANES
        return at + amount, jnp.where(full, moved, merged)

    def gather(step, carry):
        for i in range(4):
            block = recv[4 * step + i]
            for half in range(2):
                index = half * n + 4 * step + i
                carry = [
                    append(block, spans[q, index], spans[bins + q, index], carry[q]) for q in range(bins)
                ]
                block = pltpu.roll(block, 4, axis=0)
        return carry

    starts = [q * tiles_of_bin(n) for q in range(bins)]
    empty = jnp.zeros((8, LANES), F32)
    found = lax.fori_loop(0, n // 4, gather, [(jnp.int32(s * LANES), empty) for s in starts])
    most = jnp.int32(0)
    for q, (at, last) in enumerate(found):
        buf[at >> 7] = jnp.where(lane < (at & (LANES - 1)), last, 0.0)
        buf[(at >> 7) + 1] = empty
        most = jnp.maximum(most, (at - starts[q] * LANES + SHOTS - 1) >> SHOTS.bit_length() - 1)
    spans[0, LANES - 1] = most

    def deposit(chunk, carry):
        for q in range(bins):
            first = starts[q] + SHOTS // LANES * chunk
            end = found[q][0] - first * LANES
            amount, frac_row, frac_col, place = shot_rows(buf, first, end)
            pixel_row = jnp.minimum(place >> shift, rows - 2)
            row_high, row_low = table(
                pixel_row, split(amount * (1.0 - frac_row)), split(amount * frac_row), rows
            )
            high, low = col_table(place, frac_col, cols, q)
            dose[:, q * CHUNK : (q + 1) * CHUNK] += (
                dot_nt(row_high, high) + dot_nt(row_low, high) + dot_nt(row_high, low)
            )
        return carry

    lax.fori_loop(0, most, deposit, 0)


def deposit(recv, rows, cols):
    vmem = pl.BlockSpec(memory_space=pltpu.VMEM)
    smem = pl.BlockSpec(memory_space=pltpu.SMEM)
    tiles = (cols // CHUNK) * tiles_of_bin(recv.shape[0])
    spans = (2 * (cols // CHUNK), LANES)
    return pl.pallas_call(
        deposit_kernel,
        out_shape=[
            jax.ShapeDtypeStruct((rows, cols), F32),
            jax.ShapeDtypeStruct((tiles, 8, LANES), F32),
            jax.ShapeDtypeStruct(spans, I32),
        ],
        in_specs=[vmem],
        out_specs=[vmem, vmem, smem],
        scratch_shapes=[pltpu.VMEM(spans, I32), pltpu.SemaphoreType.DMA],
        compiler_params=pltpu.CompilerParams(vmem_limit_bytes=16 * 2**20),
        cost_estimate=cost(8),
        name="deposit",
    )(recv)


def sample_kernel(grad_high, grad_low, buf, spans, exposure, out, exposure_out, values, sem):
    leave = pltpu.make_async_copy(exposure, exposure_out, sem)
    leave.start()
    n = out.shape[0]
    rows, cols = grad_high.shape
    bins = cols // CHUNK
    shift = int(math.log2(cols))
    starts = [q * tiles_of_bin(n) for q in range(bins)]

    def sample(chunk, carry):
        for q in range(bins):
            first = starts[q] + SHOTS // LANES * chunk
            _, frac_row, frac_col, place = shot_rows(buf, first, SHOTS)
            pixel_row = jnp.minimum(place >> shift, rows - 2)
            high, low = col_table(place, frac_col, cols, q)
            window = slice(q * CHUNK, (q + 1) * CHUNK)
            along = (
                dot(grad_high[:, window], high)
                + dot(grad_low[:, window], high)
                + dot(grad_high[:, window], low)
            )
            here = iota((rows, SHOTS), 0)
            weight = jnp.where(
                here == pixel_row, 1.0 - frac_row, jnp.where(here == pixel_row + 1, frac_row, 0.0)
            )
            got = jnp.sum(weight * along, axis=0, keepdims=True)
            for i in range(SHOTS // LANES):
                values[first + i, 0:1] = got[:, i * LANES : (i + 1) * LANES]
        return carry

    lax.fori_loop(0, spans[0, LANES - 1], sample, 0)

    lane, row = iota((1, LANES), 1), iota((8, LANES), 0)

    def take(begin, amount, at):
        lane_at, tile_at = at & (LANES - 1), at >> 7
        both = jnp.where(lane >= lane_at, values[tile_at, 0:1], values[tile_at + 1, 0:1])
        moved = pltpu.roll(both, (begin - at) & (LANES - 1), axis=1)
        return jnp.where((lane >= begin) & (lane < begin + amount), moved, 0.0)

    def spread(step, at):
        for i in range(8):
            at = spread_one(8 * step + i, at)
        return at

    def spread_one(i, at):
        at = list(at)
        both = []
        for half in range(2):
            total = jnp.zeros((1, LANES), F32)
            for q in range(bins):
                begin, amount = spans[q, half * n + i], spans[bins + q, half * n + i]
                total = total + take(begin, amount, at[q])
                at[q] = at[q] + amount
            both.append(total)
        out[i] = jnp.where(row == 0, both[0], jnp.where(row == 1, both[1], 0.0))
        return at

    lax.fori_loop(0, n // 8, spread, [jnp.int32(s * LANES) for s in starts])
    leave.wait()


def sample(n, grad_high, grad_low, buf, spans, exposure):
    vmem = pl.BlockSpec(memory_space=pltpu.VMEM)
    smem = pl.BlockSpec(memory_space=pltpu.SMEM)
    return pl.pallas_call(
        sample_kernel,
        out_shape=[
            jax.ShapeDtypeStruct((n, 8, LANES), F32),
            jax.ShapeDtypeStruct(exposure.shape, F32),
        ],
        in_specs=[vmem, vmem, vmem, smem, pl.BlockSpec(memory_space=pl.ANY)],
        out_specs=[vmem, pl.BlockSpec(memory_space=pl.ANY)],
        scratch_shapes=[pltpu.VMEM(buf.shape, F32), pltpu.SemaphoreType.DMA],
        compiler_params=pltpu.CompilerParams(vmem_limit_bytes=16 * 2**20),
        cost_estimate=cost(8),
        name="sample",
    )(grad_high, grad_low, buf, spans, exposure)


SIDES = ((-1, 0), (1, 0), (0, -1), (0, 1), (-1, -1), (-1, 1), (1, -1), (1, 1))
PIECE_SIDE = (0, 0, 0, 0, 1, 1, 1, 1, 2, 3, 4, 5, 6, 7)
OPPOSITE = (4, 5, 6, 7, 0, 1, 2, 3, 9, 8, 13, 12, 11, 10)


def blur_kernel(
    dims, dose, target_far, zone, zone_weights,
    exposure, grad_high, grad_low,
    target, near_sem, mid_high, mid_low, edge_high, edge_low, col_high, col_low,
    zone_own, zone_in, halo_rows, halo_cols, halo_corners, dose_high, dose_low, part_high, part_low,
    mixed_high, mixed_low, error, weight, sends, recvs, zone_send, zone_recv,
):
    n_row, n_col = dims
    rows, cols = dose.shape
    wide = cols + 2 * SIDE
    steps = cols // CHUNK
    row, col = lax.axis_index("row"), lax.axis_index("col")

    def exists(side):
        down, right = SIDES[side]
        tests = []
        if down:
            tests.append(row > 0 if down < 0 else row < n_row - 1)
        if right:
            tests.append(col > 0 if right < 0 else col < n_col - 1)
        return functools.reduce(jnp.logical_and, tests)

    def neighbour(side):
        down, right = SIDES[side]
        return (row + down, col + right)

    def landing(turn, piece):
        if piece < 8:
            return halo_rows.at[turn, piece // 4, :, pl.ds(piece % 4 * CHUNK, CHUNK)]
        if piece < 10:
            return halo_cols.at[turn, piece - 8]
        return halo_corners.at[turn, piece - 10]

    def edge(field, piece):
        down, right = SIDES[PIECE_SIDE[piece]]
        high = pl.ds(0, rows) if not down else (pl.ds(0, HALO) if down < 0 else pl.ds(rows - HALO, HALO))
        if piece < 8:
            across = pl.ds(piece % 4 * CHUNK, CHUNK)
        else:
            across = pl.ds(0, SIDE) if right < 0 else pl.ds(cols - SIDE, SIDE)
        return field.at[high, across]

    def halo_copy(field, turn, piece):
        return pltpu.make_async_remote_copy(
            src_ref=edge(field, piece),
            dst_ref=landing(turn, OPPOSITE[piece]),
            send_sem=sends.at[turn, piece],
            recv_sem=recvs.at[turn, OPPOSITE[piece]],
            device_id=neighbour(PIECE_SIDE[piece]),
            device_id_type=MESH,
        )

    def zone_copy(side):
        down, right = SIDES[side]
        there = SIDES.index((-down, -right))
        return pltpu.make_async_remote_copy(
            src_ref=zone_own,
            dst_ref=zone_in.at[there],
            send_sem=zone_send.at[side],
            recv_sem=zone_recv.at[there],
            device_id=neighbour(side),
            device_id_type=MESH,
        )

    def by_side(pieces, act):
        for side in sorted({PIECE_SIDE[piece] for piece in pieces}, key=[PIECE_SIDE[p] for p in pieces].index):

            @pl.when(exists(side))
            def _(side=side):
                for piece in pieces:
                    if PIECE_SIDE[piece] == side:
                        act(piece)

    def send(field, turn, pieces):
        by_side(pieces, lambda piece: halo_copy(field, turn, piece).start())

    def await_halo(field, turn, pieces):
        by_side(pieces, lambda piece: halo_copy(field, turn, OPPOSITE[piece]).wait_recv())

    near = pltpu.make_async_copy(target_far, target, near_sem)
    near.start()
    barrier = pltpu.get_barrier_semaphore()
    zone_own[...] = jnp.zeros_like(zone_own)
    zone_own[0 : zone.shape[0], 0 : zone.shape[1]] = zone[...]
    for side in range(8):

        @pl.when(jnp.logical_not(exists(side)))
        def _(side=side):
            for turn in range(2):
                if side < 2:
                    halo_rows[turn, side] = jnp.zeros((HALO, cols), F32)
                elif side < 4:
                    halo_cols[turn, side - 2] = jnp.zeros((rows, SIDE), F32)
                else:
                    halo_corners[turn, side - 4] = jnp.zeros((HALO, SIDE), F32)
            zone_in[side] = jnp.zeros_like(zone_own)

    for side in range(8):

        @pl.when(exists(side))
        def _(side=side):
            pl.semaphore_signal(barrier, inc=1, device_id=neighbour(side), device_id_type=MESH)

    for kernel, sigma in enumerate(SIGMAS):
        shape = (2 * HALO, 4 * HALO)
        high, low = split(taps((iota(shape, 1) - iota(shape, 0) - HALO).astype(F32), sigma))
        for band, mid, edges in ((high, mid_high, edge_high), (low, mid_low, edge_low)):
            mid[kernel * 2 * HALO : (kernel + 1) * 2 * HALO] = band
            for e in range(2):
                edges[e, kernel * HALO : (kernel + 1) * HALO] = band[e * HALO : (e + 1) * HALO]
        shape = (2 * CHUNK, CHUNK)
        high, low = split(taps((iota(shape, 0) - iota(shape, 1) - SIDE).astype(F32), sigma))
        col_high[kernel] = high
        col_low[kernel] = low

    tall = 1 + jnp.where(row > 0, 1, 0) + jnp.where(row < n_row - 1, 1, 0)
    broad = 1 + jnp.where(col > 0, 1, 0) + jnp.where(col < n_col - 1, 1, 0)
    pl.semaphore_wait(barrier, tall * broad - 1)
    for side in range(8):

        @pl.when(exists(side))
        def _(side=side):
            zone_copy(side).start()

    send(dose, 0, (8, 9, 0, 1, 4, 5, 11, 13))
    send(dose, 0, (2, 3, 6, 7, 10, 12))

    def put_dose(value, first_row, first_col):
        high, low = split(value)
        here = pl.ds(first_row, value.shape[0]), pl.ds(first_col, value.shape[1])
        dose_high[here] = high
        dose_low[here] = low

    def put_part(value, square, first_col):
        across = pl.ds(first_col, value.shape[1])
        here = pl.ds(square * HALO, HALO)
        for kernel in range(3):
            factor = weight[8 * kernel + square : 8 * kernel + square + 1, across]
            high, low = split(factor * value)
            part_high[kernel, here, across] = high
            part_low[kernel, here, across] = low

    def tile_forward(edges, j):
        tile = pl.ds(j * CHUNK, CHUNK)

        def keep(band_high, band_low, first_row, first_out, count):
            here = pl.ds(first_row, 4 * HALO)
            in_high, in_low = dose_high[here, tile], dose_low[here, tile]
            field = dot(band_high, in_high) + dot(band_low, in_high) + dot(band_high, in_low)
            high, low = split(field)
            for kernel in range(3):
                part = slice(kernel * count, (kernel + 1) * count)
                mixed_high[edges, kernel, first_out : first_out + count, tile] = high[part]
                mixed_low[edges, kernel, first_out : first_out + count, tile] = low[part]

        if edges:
            keep(edge_high[0], edge_low[0], 0, 0, HALO)
            keep(edge_high[1], edge_low[1], 2 * HALO, HALO, HALO)
        else:
            keep(mid_high[...], mid_low[...], HALO, 0, 2 * HALO)

    def along_cols(edges, u, kernel):
        take = pl.ds(u * CHUNK, 2 * CHUNK)
        high, low = mixed_high[edges, kernel, :, take], mixed_low[edges, kernel, :, take]
        both = dot(jnp.concatenate([high, low], axis=0), col_high[kernel])
        return both[: 2 * HALO] + both[2 * HALO :] + dot(high, col_low[kernel])

    def window_forward(edges, u):
        squares = (1, rows // HALO) if edges else (2, 3)
        total = [jnp.zeros((HALO, CHUNK), F32) for _ in range(2)]
        for kernel in range(3):
            field = along_cols(edges, u, kernel)
            for half, square in enumerate(squares):
                line = 8 * kernel + square
                factor = weight[line : line + 1, SIDE + u * CHUNK : SIDE + (u + 1) * CHUNK]
                total[half] = total[half] + factor * field[half * HALO : (half + 1) * HALO]
        for half, square in enumerate(squares):
            here = pl.ds((square - 1) * HALO, HALO), pl.ds(u * CHUNK, CHUNK)
            exposure[here] = total[half]
            wrong = total[half] - target[here]
            error[here] = wrong
            put_part(wrong, square, SIDE + u * CHUNK)

    def tile_backward(edges, j):
        tile = pl.ds(j * CHUNK, CHUNK)

        def keep(kernel, band_high, band_low, first_row, first_out, count):
            here = pl.ds(first_row, 4 * HALO)
            in_high, in_low = part_high[kernel, here, tile], part_low[kernel, here, tile]
            field = dot(band_high, in_high) + dot(band_low, in_high) + dot(band_high, in_low)
            high, low = split(field)
            mixed_high[edges, kernel, first_out : first_out + count, tile] = high
            mixed_low[edges, kernel, first_out : first_out + count, tile] = low

        for kernel in range(3):
            if edges:
                part = pl.ds(kernel * HALO, HALO)
                keep(kernel, edge_high[0, part], edge_low[0, part], 0, 0, HALO)
                keep(kernel, edge_high[1, part], edge_low[1, part], 2 * HALO, HALO, HALO)
            else:
                part = pl.ds(kernel * 2 * HALO, 2 * HALO)
                keep(kernel, mid_high[part], mid_low[part], HALO, 0, 2 * HALO)

    def window_backward(edges, u):
        squares = (1, rows // HALO) if edges else (2, 3)
        high, low = split(sum(along_cols(edges, u, kernel) for kernel in range(3)))
        for half, square in enumerate(squares):
            here = pl.ds((square - 1) * HALO, HALO), pl.ds(u * CHUNK, CHUNK)
            grad_high[here] = high[half * HALO : (half + 1) * HALO]
            grad_low[here] = low[half * HALO : (half + 1) * HALO]

    def zone_table():
        sub, lane = iota((8, LANES), 0), iota((8, LANES), 1)
        high, across = zone.shape
        table = pltpu.roll(pltpu.roll(zone_own[...], 1, axis=0), 2, axis=1)
        for side in range(8):
            down, right = SIDES[side]
            got = pltpu.roll(zone_in[side], (1 + down * high) % 8, axis=0)
            got = pltpu.roll(got, (2 + right * across) % LANES, axis=1)
            row_ok = (sub == 0) if down < 0 else (sub == high + 1) if down > 0 else (sub >= 1) & (sub <= high)
            col_ok = (
                (lane == 1) if right < 0 else (lane == across + 2) if right > 0 else (lane >= 2) & (lane < across + 2)
            )
            table = jnp.where(row_ok & col_ok, got, table)
        picked = []
        for kernel in range(3):
            value = jnp.zeros((8, LANES), F32)
            for z in range(ZONES):
                value = jnp.where(table == z, zone_weights[kernel, z], value)
            picked.append(value)
        return jnp.concatenate(picked, axis=0)

    put_dose(dose[...], HALO, SIDE)
    for side in range(8):

        @pl.when(exists(side))
        def _(side=side):
            down, right = SIDES[side]
            zone_copy(SIDES.index((-down, -right))).wait_recv()

    spread = jnp.where(iota((LANES, wide), 0) == iota((LANES, wide), 1) // HALO, 1.0, 0.0).astype(BF16)
    table = zone_table()
    for _ in range(3):
        piece = table.astype(BF16)
        weight[...] = dot(piece, spread) if _ == 0 else weight[...] + dot(piece, spread)
        table = table - piece.astype(F32)

    def sweep(tile, window, edges, before, after):
        ahead = 2
        done = 0
        for u in range(steps):
            before(u)
            while done <= min(u + ahead, steps):
                tile(edges, done)
                done += 1
            window(edges, u)
            after(u)

    def nothing(u):
        return None

    near.wait()
    await_halo(dose, 0, (8, 9))
    put_dose(halo_cols[0, 0], HALO, 0)
    put_dose(halo_cols[0, 1], HALO, SIDE + cols)
    sweep(tile_forward, window_forward, 0, nothing, nothing)

    def arrive(turn, field, put, u):
        chunks = (0, 1, 2) if u == 0 else (u + 2,) if u + 2 < steps else ()
        corners = (10, 12) if u == 0 else (11, 13) if u == steps - 2 else ()
        await_halo(field, turn, (*chunks, *(4 + c for c in chunks), *corners))
        for side, square in ((0, 0), (1, rows // HALO + 1)):
            for c in chunks:
                put(halo_rows[turn, side, :, c * CHUNK : (c + 1) * CHUNK], square, SIDE + c * CHUNK)
            if u == 0:
                put(halo_corners[turn, 2 * side], square, 0)
            if u == steps - 2:
                put(halo_corners[turn, 2 * side + 1], square, SIDE + cols)

    def send_error(u):
        sides = (8, 10, 12) if u == 0 else (9, 11, 13) if u == steps - 1 else ()
        send(error, 1, (u, 4 + u, *sides))

    sweep(
        tile_forward,
        window_forward,
        1,
        lambda u: arrive(0, dose, lambda value, square, at: put_dose(value, square * HALO, at), u),
        send_error,
    )
    await_halo(error, 1, (8, 9))
    for side, at in ((0, 0), (1, SIDE + cols)):
        for square in range(rows // HALO):
            put_part(halo_cols[1, side, square * HALO : (square + 1) * HALO], 1 + square, at)
    sweep(tile_backward, window_backward, 0, nothing, nothing)
    sweep(tile_backward, window_backward, 1, lambda u: arrive(1, error, put_part, u), nothing)
    by_side(range(14), lambda piece: halo_copy(dose, 0, piece).wait_send())
    by_side(range(14), lambda piece: halo_copy(error, 1, piece).wait_send())
    for side in range(8):

        @pl.when(exists(side))
        def _(side=side):
            zone_copy(side).wait_send()


def blur(dims, dose, target, zone, zone_weights):
    rows, cols = dose.shape
    wide, high = cols + 2 * SIDE, rows + 2 * HALO
    vmem = pl.BlockSpec(memory_space=pltpu.VMEM)
    smem = pl.BlockSpec(memory_space=pltpu.SMEM)
    dma = pltpu.SemaphoreType.DMA
    return pl.pallas_call(
        functools.partial(blur_kernel, dims),
        out_shape=[
            jax.ShapeDtypeStruct((rows, cols), F32),
            jax.ShapeDtypeStruct((rows, cols), BF16),
            jax.ShapeDtypeStruct((rows, cols), BF16),
        ],
        in_specs=[vmem, pl.BlockSpec(memory_space=pl.ANY), vmem, smem],
        out_specs=[vmem] * 3,
        scratch_shapes=[
            pltpu.VMEM((rows, cols), F32),
            dma,
            pltpu.VMEM((6 * HALO, 4 * HALO), BF16),
            pltpu.VMEM((6 * HALO, 4 * HALO), BF16),
            pltpu.VMEM((2, 3 * HALO, 4 * HALO), BF16),
            pltpu.VMEM((2, 3 * HALO, 4 * HALO), BF16),
            pltpu.VMEM((3, 2 * CHUNK, CHUNK), BF16),
            pltpu.VMEM((3, 2 * CHUNK, CHUNK), BF16),
            pltpu.VMEM((8, LANES), I32),
            pltpu.VMEM((8, 8, LANES), I32),
            pltpu.VMEM((2, 2, HALO, cols), F32),
            pltpu.VMEM((2, 2, rows, SIDE), F32),
            pltpu.VMEM((2, 4, HALO, SIDE), F32),
            pltpu.VMEM((high, wide), BF16),
            pltpu.VMEM((high, wide), BF16),
            pltpu.VMEM((3, high, wide), BF16),
            pltpu.VMEM((3, high, wide), BF16),
            pltpu.VMEM((2, 3, 2 * HALO, wide), BF16),
            pltpu.VMEM((2, 3, 2 * HALO, wide), BF16),
            pltpu.VMEM((rows, cols), F32),
            pltpu.VMEM((24, wide), F32),
            dma((2, 14)), dma((2, 14)), dma((8,)), dma((8,)),
        ],
        compiler_params=pltpu.CompilerParams(
            collective_id=1, has_side_effects=True, vmem_limit_bytes=40 * 2**20
        ),
        cost_estimate=cost(25),
        name="blur",
    )(dose, far(target), far(zone), far(zone_weights))


def per_device(dims, shot_dose, shot_frac, shot_pos, block_count, shot_tile, zone, zone_weights, target):
    n = dims[1]
    rows, cols = target.shape
    count, tile = block_count.reshape(1, -1), shot_tile.reshape(1, -1)
    recv, order = route(n, cols, shot_dose, shot_frac, shot_pos, count, tile)
    dose, buf, spans = deposit(recv, rows, cols)
    exposure, grad_high, grad_low = blur(dims, dose, target, zone, zone_weights.T)
    slot_grad, exposure = sample(n, grad_high, grad_low, buf, spans, exposure)
    return exposure, give_back(n, slot_grad, tile, order)


def solution(mesh):
    dims = (mesh.shape["row"], mesh.shape["col"])
    return jax.shard_map(
        functools.partial(per_device, dims),
        mesh=mesh,
        in_specs=(
            P(("row", "col"), None),
            P(None, ("row", "col"), None),
            P(("row", "col"), None),
            P(("row", "col")),
            P(("row", "col"), None),
            P("row", "col"),
            P(),
            P("row", "col"),
        ),
        out_specs=(P("row", "col"), P(("row", "col"), None)),
        check_vma=False,
    )
```

```python
import functools
import math

import jax
import jax.numpy as jnp
import numpy as np
from jax import lax
from jax.experimental import pallas as pl
from jax.experimental.pallas import tpu as pltpu
from jax.sharding import PartitionSpec as P

HALO = 64
ZONES = 8
LANES = 128
CHUNK = 256
SHOTS = 512
SIDE = 128
SIGMAS = (0.125 * HALO, 0.25 * HALO, 0.5 * HALO)
MESH = pl.DeviceIdType.MESH
F32, BF16, I32 = jnp.float32, jnp.bfloat16, jnp.int32


def cost(us):
    return pl.CostEstimate(flops=0, bytes_accessed=int(us * 3.0e6), transcendentals=0)


def iota(shape, dim):
    return lax.broadcasted_iota(I32, shape, dim)


def split(x):
    high = x.astype(BF16)
    return high, (x - high.astype(F32)).astype(BF16)


def dot(a, b):
    return jnp.dot(a, b, preferred_element_type=F32)


def dot_nt(a, b):
    return lax.dot_general(a, b, (((1,), (1,)), ((), ())), preferred_element_type=F32)


def pick(onehot, x):
    first = x.astype(BF16)
    rest = x - first.astype(F32)
    second = rest.astype(BF16)
    third = (rest - second.astype(F32)).astype(BF16)
    return dot(onehot, first) + dot(onehot, second) + dot(onehot, third)


def taps(offset, sigma):
    reach = np.arange(-HALO, HALO + 1).astype(np.float64)
    total = float(np.exp(-reach * reach / (2.0 * sigma * sigma)).sum())
    value = jnp.exp(offset * offset * (-1.0 / (2.0 * sigma * sigma))) * (1.0 / total)
    return jnp.where(jnp.abs(offset) <= float(HALO), value, 0.0)


def far(x):
    return pltpu.with_memory_space_constraint(x, pltpu.HBM)


def slots_of(tile, width):
    n = tile.shape[0]
    times = width // n
    own, lane = iota((n, width), 0), iota((n, width), 1)
    other = lane // times
    tile_row = jnp.sum(jnp.where(own == other, tile, 0), axis=0, keepdims=True)
    same = tile == tile_row
    rank_row = jnp.sum(jnp.where(same & (own < other), 1, 0), axis=0, keepdims=True)
    once = lane % times == 0
    rank_col = jnp.sum(jnp.where(same & (other < own) & once, 1, 0), axis=1, keepdims=True)
    return tile * 2 + rank_col, tile_row * 2 + rank_row


def upright(line):
    n = line.shape[1]
    return jnp.sum(jnp.where(iota((n, n), 0) == iota((n, n), 1), line, 0), axis=1, keepdims=True)


def column_class(pixel):
    return 2 * (pixel >> 8) + jnp.where((pixel & (CHUNK - 1)) == CHUNK - 1, 1, 0)


def greet_all(n, me, row):
    barrier = pltpu.get_barrier_semaphore()

    def greet(step, carry):
        peer = (me + step) & (n - 1)
        pl.semaphore_signal(barrier, inc=1, device_id=(row, peer), device_id_type=MESH)
        return carry

    lax.fori_loop(1, n, greet, 0)
    return barrier


def exchange(n, me, row, source, target, send_sem, recv_sem, meanwhile):
    def copy(peer, source_slots, target_slots):
        return pltpu.make_async_remote_copy(
            src_ref=source.at[source_slots],
            dst_ref=target.at[target_slots],
            send_sem=send_sem,
            recv_sem=recv_sem,
            device_id=(row, peer),
            device_id_type=MESH,
        )

    def start(step, carry):
        peer = (me + step) & (n - 1)
        copy(peer, peer, me).start()
        return carry

    lax.fori_loop(1, n, start, 0)
    target[pl.ds(me, 1)] = source[pl.ds(me, 1)]
    meanwhile()
    every = copy((me + 1) & (n - 1), pl.ds(0, n - 1), pl.ds(0, n - 1))
    every.wait_recv()
    every.wait_send()


def make_bands(mid_high, mid_low, edge_high, edge_low, col_high, col_low):
    for kernel, sigma in enumerate(SIGMAS):
        shape = (2 * HALO, 4 * HALO)
        high, low = split(taps((iota(shape, 1) - iota(shape, 0) - HALO).astype(F32), sigma))
        for band, mid, edges in ((high, mid_high, edge_high), (low, mid_low, edge_low)):
            mid[kernel * 2 * HALO : (kernel + 1) * 2 * HALO] = band
            for e in range(2):
                edges[e, kernel * HALO : (kernel + 1) * HALO] = band[e * HALO : (e + 1) * HALO]
        shape = (2 * CHUNK, CHUNK)
        high, low = split(taps((iota(shape, 0) - iota(shape, 1) - SIDE).astype(F32), sigma))
        col_high[kernel] = high
        col_low[kernel] = low


BANDS = [
    jax.ShapeDtypeStruct(shape, BF16)
    for shape in ((6 * HALO, 4 * HALO), (2, 3 * HALO, 4 * HALO), (3, 2 * CHUNK, CHUNK))
    for _ in range(2)
]


def route_kernel(
    n, cols, dose, frac, pos, count, tile, recv, order, *rest
):
    bands, (parts, ordered, send, send_sem, recv_sem) = rest[:6], rest[6:]
    row, me = lax.axis_index("row"), lax.axis_index("col")
    barrier = greet_all(n, me, row)
    blocks = tile.shape[1]
    live = iota((blocks, LANES), 1) < upright(count[...])
    dead = 2 * (cols // CHUNK) - 1
    kind = jnp.where(live, column_class(jnp.minimum(pos[...] & (cols - 1), cols - 2)), dead)
    masks = [jnp.where(kind == j, 1.0, 0.0) for j in range(dead + 1)]
    before = jnp.where(iota((LANES, LANES), 0) < iota((LANES, LANES), 1), 1.0, 0.0).astype(BF16)
    prefix = dot(jnp.concatenate(masks, axis=0).astype(BF16), before)
    start = jnp.zeros((blocks, 1), F32)
    rank = jnp.zeros((blocks, LANES), F32)
    for j, mask in enumerate(masks):
        rank = rank + mask * (prefix[j * blocks : (j + 1) * blocks] + start)
        start = start + jnp.sum(mask, axis=1, keepdims=True)
    rank = rank.astype(I32)
    order[...] = rank
    fields = [
        jnp.where(live, dose[...], 0.0),
        frac[0],
        frac[1],
        jnp.where(live, pos[...] + 1, 0).astype(F32),
    ]
    for f, field in enumerate(fields):
        for part in range(3):
            piece = field.astype(BF16).astype(F32)
            parts[:, 4 * part + f] = piece
            field = field - piece
        parts[:, 12 + f] = jnp.zeros((blocks, LANES), F32)
    target = iota((LANES, LANES), 0)
    for b in range(blocks):
        moves = jnp.where(target == rank[b : b + 1], 1.0, 0.0).astype(BF16)
        ordered[b] = dot_nt(parts[b].astype(BF16), moves)
    width = 16 * blocks
    _, placed = slots_of(upright(tile[...]), width)
    out, col = iota((8 * n, width), 0), iota((8 * n, width), 1)
    chosen = (out // 4 == placed) & (out % 4 == col % 4) & (col % 16 < 12)
    onehot = jnp.where(chosen, 1.0, 0.0).astype(BF16)
    send[...] = dot(onehot, ordered[...].reshape(width, LANES).astype(BF16)).reshape(n, 8, LANES)
    pl.semaphore_wait(barrier, n - 1)
    exchange(n, me, row, send, recv, send_sem, recv_sem, lambda: make_bands(*bands))


def route(n, cols, dose, frac, pos, count, tile):
    vmem = pl.BlockSpec(memory_space=pltpu.VMEM)
    blocks = tile.shape[1]
    return pl.pallas_call(
        functools.partial(route_kernel, n, cols),
        out_shape=[
            jax.ShapeDtypeStruct((n, 8, LANES), F32),
            jax.ShapeDtypeStruct((blocks, LANES), I32),
            *BANDS,
        ],
        in_specs=[vmem] * 5,
        out_specs=[vmem] * 8,
        scratch_shapes=[
            pltpu.VMEM((blocks, 16, LANES), F32),
            pltpu.VMEM((blocks, 16, LANES), F32),
            pltpu.VMEM((n, 8, LANES), F32),
            pltpu.SemaphoreType.DMA,
            pltpu.SemaphoreType.DMA,
        ],
        compiler_params=pltpu.CompilerParams(
            collective_id=0, has_side_effects=True, vmem_limit_bytes=8 * 2**20
        ),
        cost_estimate=cost(10),
        name="route",
    )(*(far(x) for x in (dose, frac, pos, count, tile)))


def return_kernel(n, grads, tile, order, out, back, send_sem, recv_sem):
    row, me = lax.axis_index("row"), lax.axis_index("col")
    barrier = greet_all(n, me, row)
    blocks = tile.shape[1]
    placed, _ = slots_of(upright(tile[...]), blocks)
    col = iota((blocks, 8 * n), 1)
    chosen = (placed == 2 * (col >> 3) + (col & 7)) & ((col & 7) < 2)
    onehot = jnp.where(chosen, 1.0, 0.0).astype(BF16)
    pl.semaphore_wait(barrier, n - 1)
    exchange(n, me, row, grads, back, send_sem, recv_sem, lambda: None)
    found = pick(onehot, back[...].reshape(8 * n, LANES))
    out[...] = jnp.take_along_axis(found, order[...], axis=1)


def give_back(n, grads, tile, order):
    vmem = pl.BlockSpec(memory_space=pltpu.VMEM)
    return pl.pallas_call(
        functools.partial(return_kernel, n),
        out_shape=jax.ShapeDtypeStruct((tile.shape[1], LANES), F32),
        in_specs=[vmem] * 3,
        out_specs=vmem,
        scratch_shapes=[
            pltpu.VMEM((n, 8, LANES), F32),
            pltpu.SemaphoreType.DMA,
            pltpu.SemaphoreType.DMA,
        ],
        compiler_params=pltpu.CompilerParams(
            collective_id=2, has_side_effects=True, vmem_limit_bytes=8 * 2**20
        ),
        cost_estimate=cost(10),
        name="give_back",
    )(grads, far(tile), order)


def shot_rows(buf, first, end):
    lane = iota((8, LANES), 1)
    tiles = [jnp.where(lane < end - i * LANES, buf[first + i], 0.0) for i in range(SHOTS // LANES)]
    line = lambda f: jnp.concatenate([tile[f : f + 1] for tile in tiles], axis=1)
    return line(0), line(1), line(2), line(3).astype(I32) - 1


def table(index, low, high, count):
    here = iota((count, index.shape[1]), 0).astype(F32).astype(BF16)
    first = index.astype(F32).astype(BF16)
    second = (index + 1).astype(F32).astype(BF16)
    at_first, at_second = here == first, here == second
    zero = jnp.zeros((), BF16)
    return [jnp.where(at_first, lo, jnp.where(at_second, hi, zero)) for lo, hi in zip(low, high)]


def col_table(place, frac, cols, window):
    pixel = jnp.minimum(place & (cols - 1), cols - 2)
    local = jnp.clip(pixel - window * CHUNK, -2, CHUNK)
    return table(local, split(1.0 - frac), split(frac), CHUNK)


def tiles_of_bin(n):
    return 2 * n + 2


def deposit_kernel(recv, dose, buf, spans, row_spans, sem):
    n = recv.shape[0]
    rows, cols = dose.shape
    bins = cols // CHUNK
    shift = int(math.log2(cols))
    lane = iota((8, LANES), 1)
    ends = []
    for half in range(2):
        place = recv[:, 4 * half + 3, :].astype(I32) - 1
        kind = column_class(jnp.minimum(place & (cols - 1), cols - 2))
        kind = jnp.where(place >= 0, kind, 2 * bins)
        ends.append([jnp.sum(jnp.where(kind <= j, 1, 0), axis=1, keepdims=True) for j in range(2 * bins)])
    which = iota((n, LANES), 1)
    chosen = (lax.rem(which, n) == iota((n, LANES), 0)) & (which < 2 * n)

    def to_lanes(first, second):
        spread = jnp.where(which < n, first, second)
        return jnp.sum(jnp.where(chosen, spread, 0), axis=0, keepdims=True)

    lines = []
    for q in range(bins):
        lines.append(to_lanes(*(e[2 * q - 2] if q else jnp.zeros((n, 1), I32) for e in ends)))
    for q in range(bins):
        lines.append(to_lanes(*(e[2 * q + 1] for e in ends)) - lines[q])
    row_spans[...] = jnp.concatenate(lines, axis=0)
    copy = pltpu.make_async_copy(row_spans, spans, sem)
    copy.start()
    dose[...] = jnp.zeros_like(dose)
    copy.wait()

    def append(block, begin, amount, carry):
        at, current = carry
        lane_at = at & (LANES - 1)
        moved = pltpu.roll(block, (at - begin) & (LANES - 1), axis=1)
        merged = jnp.where(lane < lane_at, current, moved)
        buf[at >> 7] = merged
        full = jnp.full((8, LANES), lane_at + amount, I32) >= LANES
        return at + amount, jnp.where(full, moved, merged)

    def gather(step, carry):
        for i in range(4):
            block = recv[4 * step + i]
            for half in range(2):
                index = half * n + 4 * step + i
                carry = [
                    append(block, spans[q, index], spans[bins + q, index], carry[q]) for q in range(bins)
                ]
                block = pltpu.roll(block, 4, axis=0)
        return carry

    starts = [q * tiles_of_bin(n) for q in range(bins)]
    empty = jnp.zeros((8, LANES), F32)
    found = lax.fori_loop(0, n // 4, gather, [(jnp.int32(s * LANES), empty) for s in starts])
    most = jnp.int32(0)
    for q, (at, last) in enumerate(found):
        buf[at >> 7] = jnp.where(lane < (at & (LANES - 1)), last, 0.0)
        buf[(at >> 7) + 1] = empty
        most = jnp.maximum(most, (at - starts[q] * LANES + SHOTS - 1) >> SHOTS.bit_length() - 1)
    spans[0, LANES - 1] = most

    def deposit(chunk, carry):
        for q in range(bins):
            first = starts[q] + SHOTS // LANES * chunk
            end = found[q][0] - first * LANES
            amount, frac_row, frac_col, place = shot_rows(buf, first, end)
            pixel_row = jnp.minimum(place >> shift, rows - 2)
            row_high, row_low = table(
                pixel_row, split(amount * (1.0 - frac_row)), split(amount * frac_row), rows
            )
            high, low = col_table(place, frac_col, cols, q)
            dose[:, q * CHUNK : (q + 1) * CHUNK] += (
                dot_nt(row_high, high) + dot_nt(row_low, high) + dot_nt(row_high, low)
            )
        return carry

    lax.fori_loop(0, most, deposit, 0)


def deposit(recv, rows, cols):
    vmem = pl.BlockSpec(memory_space=pltpu.VMEM)
    smem = pl.BlockSpec(memory_space=pltpu.SMEM)
    tiles = (cols // CHUNK) * tiles_of_bin(recv.shape[0])
    spans = (2 * (cols // CHUNK), LANES)
    return pl.pallas_call(
        deposit_kernel,
        out_shape=[
            jax.ShapeDtypeStruct((rows, cols), F32),
            jax.ShapeDtypeStruct((tiles, 8, LANES), F32),
            jax.ShapeDtypeStruct(spans, I32),
        ],
        in_specs=[vmem],
        out_specs=[vmem, vmem, smem],
        scratch_shapes=[pltpu.VMEM(spans, I32), pltpu.SemaphoreType.DMA],
        compiler_params=pltpu.CompilerParams(vmem_limit_bytes=16 * 2**20),
        cost_estimate=cost(8),
        name="deposit",
    )(recv)


def sample_kernel(grad_high, grad_low, buf, spans, exposure, out, exposure_out, values, sem):
    leave = pltpu.make_async_copy(exposure, exposure_out, sem)
    leave.start()
    n = out.shape[0]
    rows, cols = grad_high.shape
    bins = cols // CHUNK
    shift = int(math.log2(cols))
    starts = [q * tiles_of_bin(n) for q in range(bins)]

    def sample(chunk, carry):
        for q in range(bins):
            first = starts[q] + SHOTS // LANES * chunk
            _, frac_row, frac_col, place = shot_rows(buf, first, SHOTS)
            pixel_row = jnp.minimum(place >> shift, rows - 2)
            high, low = col_table(place, frac_col, cols, q)
            window = slice(q * CHUNK, (q + 1) * CHUNK)
            along = (
                dot(grad_high[:, window], high)
                + dot(grad_low[:, window], high)
                + dot(grad_high[:, window], low)
            )
            here = iota((rows, SHOTS), 0)
            weight = jnp.where(
                here == pixel_row, 1.0 - frac_row, jnp.where(here == pixel_row + 1, frac_row, 0.0)
            )
            got = jnp.sum(weight * along, axis=0, keepdims=True)
            for i in range(SHOTS // LANES):
                values[first + i, 0:1] = got[:, i * LANES : (i + 1) * LANES]
        return carry

    lax.fori_loop(0, spans[0, LANES - 1], sample, 0)

    lane, row = iota((1, LANES), 1), iota((8, LANES), 0)

    def take(begin, amount, at):
        lane_at, tile_at = at & (LANES - 1), at >> 7
        both = jnp.where(lane >= lane_at, values[tile_at, 0:1], values[tile_at + 1, 0:1])
        moved = pltpu.roll(both, (begin - at) & (LANES - 1), axis=1)
        return jnp.where((lane >= begin) & (lane < begin + amount), moved, 0.0)

    def spread(step, at):
        for i in range(8):
            at = spread_one(8 * step + i, at)
        return at

    def spread_one(i, at):
        at = list(at)
        both = []
        for half in range(2):
            total = jnp.zeros((1, LANES), F32)
            for q in range(bins):
                begin, amount = spans[q, half * n + i], spans[bins + q, half * n + i]
                total = total + take(begin, amount, at[q])
                at[q] = at[q] + amount
            both.append(total)
        out[i] = jnp.where(row == 0, both[0], jnp.where(row == 1, both[1], 0.0))
        return at

    lax.fori_loop(0, n // 8, spread, [jnp.int32(s * LANES) for s in starts])
    leave.wait()


def sample(n, grad_high, grad_low, buf, spans, exposure):
    vmem = pl.BlockSpec(memory_space=pltpu.VMEM)
    smem = pl.BlockSpec(memory_space=pltpu.SMEM)
    return pl.pallas_call(
        sample_kernel,
        out_shape=[
            jax.ShapeDtypeStruct((n, 8, LANES), F32),
            jax.ShapeDtypeStruct(exposure.shape, F32),
        ],
        in_specs=[vmem, vmem, vmem, smem, pl.BlockSpec(memory_space=pl.ANY)],
        out_specs=[vmem, pl.BlockSpec(memory_space=pl.ANY)],
        scratch_shapes=[pltpu.VMEM(buf.shape, F32), pltpu.SemaphoreType.DMA],
        compiler_params=pltpu.CompilerParams(vmem_limit_bytes=16 * 2**20),
        cost_estimate=cost(8),
        name="sample",
    )(grad_high, grad_low, buf, spans, exposure)


SIDES = ((-1, 0), (1, 0), (0, -1), (0, 1), (-1, -1), (-1, 1), (1, -1), (1, 1))
PIECE_SIDE = (0, 0, 0, 0, 1, 1, 1, 1, 2, 3, 4, 5, 6, 7)
OPPOSITE = (4, 5, 6, 7, 0, 1, 2, 3, 9, 8, 13, 12, 11, 10)


def blur_kernel(
    dims, dose, target_far, zone, zone_weights,
    mid_high, mid_low, edge_high, edge_low, col_high, col_low,
    exposure, grad_high, grad_low,
    target, near_sem,
    zone_own, zone_in, halo_rows, halo_cols, halo_corners, dose_high, dose_low, part_high, part_low,
    mixed_high, mixed_low, error, weight, sends, recvs, zone_send, zone_recv,
):
    n_row, n_col = dims
    rows, cols = dose.shape
    wide = cols + 2 * SIDE
    steps = cols // CHUNK
    row, col = lax.axis_index("row"), lax.axis_index("col")

    def exists(side):
        down, right = SIDES[side]
        tests = []
        if down:
            tests.append(row > 0 if down < 0 else row < n_row - 1)
        if right:
            tests.append(col > 0 if right < 0 else col < n_col - 1)
        return functools.reduce(jnp.logical_and, tests)

    def neighbour(side):
        down, right = SIDES[side]
        return (row + down, col + right)

    def landing(turn, piece):
        if piece < 8:
            return halo_rows.at[turn, piece // 4, :, pl.ds(piece % 4 * CHUNK, CHUNK)]
        if piece < 10:
            return halo_cols.at[turn, piece - 8]
        return halo_corners.at[turn, piece - 10]

    def edge(field, piece):
        down, right = SIDES[PIECE_SIDE[piece]]
        high = pl.ds(0, rows) if not down else (pl.ds(0, HALO) if down < 0 else pl.ds(rows - HALO, HALO))
        if piece < 8:
            across = pl.ds(piece % 4 * CHUNK, CHUNK)
        else:
            across = pl.ds(0, SIDE) if right < 0 else pl.ds(cols - SIDE, SIDE)
        return field.at[high, across]

    def halo_copy(field, turn, piece):
        return pltpu.make_async_remote_copy(
            src_ref=edge(field, piece),
            dst_ref=landing(turn, OPPOSITE[piece]),
            send_sem=sends.at[turn, piece],
            recv_sem=recvs.at[turn, OPPOSITE[piece]],
            device_id=neighbour(PIECE_SIDE[piece]),
            device_id_type=MESH,
        )

    def zone_copy(side):
        down, right = SIDES[side]
        there = SIDES.index((-down, -right))
        return pltpu.make_async_remote_copy(
            src_ref=zone_own,
            dst_ref=zone_in.at[there],
            send_sem=zone_send.at[side],
            recv_sem=zone_recv.at[there],
            device_id=neighbour(side),
            device_id_type=MESH,
        )

    def by_side(pieces, act):
        for side in sorted({PIECE_SIDE[piece] for piece in pieces}, key=[PIECE_SIDE[p] for p in pieces].index):

            @pl.when(exists(side))
            def _(side=side):
                for piece in pieces:
                    if PIECE_SIDE[piece] == side:
                        act(piece)

    def send(field, turn, pieces):
        by_side(pieces, lambda piece: halo_copy(field, turn, piece).start())

    def await_halo(field, turn, pieces):
        by_side(pieces, lambda piece: halo_copy(field, turn, OPPOSITE[piece]).wait_recv())

    near = pltpu.make_async_copy(target_far, target, near_sem)
    near.start()
    barrier = pltpu.get_barrier_semaphore()
    zone_own[...] = jnp.zeros_like(zone_own)
    zone_own[0 : zone.shape[0], 0 : zone.shape[1]] = zone[...]
    for side in range(8):

        @pl.when(jnp.logical_not(exists(side)))
        def _(side=side):
            for turn in range(2):
                if side < 2:
                    halo_rows[turn, side] = jnp.zeros((HALO, cols), F32)
                elif side < 4:
                    halo_cols[turn, side - 2] = jnp.zeros((rows, SIDE), F32)
                else:
                    halo_corners[turn, side - 4] = jnp.zeros((HALO, SIDE), F32)
            zone_in[side] = jnp.zeros_like(zone_own)

    for side in range(8):

        @pl.when(exists(side))
        def _(side=side):
            pl.semaphore_signal(barrier, inc=1, device_id=neighbour(side), device_id_type=MESH)

    tall = 1 + jnp.where(row > 0, 1, 0) + jnp.where(row < n_row - 1, 1, 0)
    broad = 1 + jnp.where(col > 0, 1, 0) + jnp.where(col < n_col - 1, 1, 0)
    pl.semaphore_wait(barrier, tall * broad - 1)
    for side in range(8):

        @pl.when(exists(side))
        def _(side=side):
            zone_copy(side).start()

    send(dose, 0, (8, 9, 0, 1, 4, 5, 11, 13))
    send(dose, 0, (2, 3, 6, 7, 10, 12))

    def put_dose(value, first_row, first_col):
        high, low = split(value)
        here = pl.ds(first_row, value.shape[0]), pl.ds(first_col, value.shape[1])
        dose_high[here] = high
        dose_low[here] = low

    def put_part(value, square, first_col):
        across = pl.ds(first_col, value.shape[1])
        here = pl.ds(square * HALO, HALO)
        for kernel in range(3):
            factor = weight[8 * kernel + square : 8 * kernel + square + 1, across]
            high, low = split(factor * value)
            part_high[kernel, here, across] = high
            part_low[kernel, here, across] = low

    def tile_forward(edges, j):
        tile = pl.ds(j * CHUNK, CHUNK)

        def keep(band_high, band_low, first_row, first_out, count):
            here = pl.ds(first_row, 4 * HALO)
            in_high, in_low = dose_high[here, tile], dose_low[here, tile]
            field = dot(band_high, in_high) + dot(band_low, in_high) + dot(band_high, in_low)
            high, low = split(field)
            for kernel in range(3):
                part = slice(kernel * count, (kernel + 1) * count)
                mixed_high[edges, kernel, first_out : first_out + count, tile] = high[part]
                mixed_low[edges, kernel, first_out : first_out + count, tile] = low[part]

        if edges:
            keep(edge_high[0], edge_low[0], 0, 0, HALO)
            keep(edge_high[1], edge_low[1], 2 * HALO, HALO, HALO)
        else:
            keep(mid_high[...], mid_low[...], HALO, 0, 2 * HALO)

    def along_cols(edges, u, kernel):
        take = pl.ds(u * CHUNK, 2 * CHUNK)
        high, low = mixed_high[edges, kernel, :, take], mixed_low[edges, kernel, :, take]
        both = dot(jnp.concatenate([high, low], axis=0), col_high[kernel])
        return both[: 2 * HALO] + both[2 * HALO :] + dot(high, col_low[kernel])

    def window_forward(edges, u):
        squares = (1, rows // HALO) if edges else (2, 3)
        total = [jnp.zeros((HALO, CHUNK), F32) for _ in range(2)]
        for kernel in range(3):
            field = along_cols(edges, u, kernel)
            for half, square in enumerate(squares):
                line = 8 * kernel + square
                factor = weight[line : line + 1, SIDE + u * CHUNK : SIDE + (u + 1) * CHUNK]
                total[half] = total[half] + factor * field[half * HALO : (half + 1) * HALO]
        for half, square in enumerate(squares):
            here = pl.ds((square - 1) * HALO, HALO), pl.ds(u * CHUNK, CHUNK)
            exposure[here] = total[half]
            wrong = total[half] - target[here]
            error[here] = wrong
            put_part(wrong, square, SIDE + u * CHUNK)

    def tile_backward(edges, j):
        tile = pl.ds(j * CHUNK, CHUNK)

        def keep(kernel, band_high, band_low, first_row, first_out, count):
            here = pl.ds(first_row, 4 * HALO)
            in_high, in_low = part_high[kernel, here, tile], part_low[kernel, here, tile]
            field = dot(band_high, in_high) + dot(band_low, in_high) + dot(band_high, in_low)
            high, low = split(field)
            mixed_high[edges, kernel, first_out : first_out + count, tile] = high
            mixed_low[edges, kernel, first_out : first_out + count, tile] = low

        for kernel in range(3):
            if edges:
                part = pl.ds(kernel * HALO, HALO)
                keep(kernel, edge_high[0, part], edge_low[0, part], 0, 0, HALO)
                keep(kernel, edge_high[1, part], edge_low[1, part], 2 * HALO, HALO, HALO)
            else:
                part = pl.ds(kernel * 2 * HALO, 2 * HALO)
                keep(kernel, mid_high[part], mid_low[part], HALO, 0, 2 * HALO)

    def window_backward(edges, u):
        squares = (1, rows // HALO) if edges else (2, 3)
        high, low = split(sum(along_cols(edges, u, kernel) for kernel in range(3)))
        for half, square in enumerate(squares):
            here = pl.ds((square - 1) * HALO, HALO), pl.ds(u * CHUNK, CHUNK)
            grad_high[here] = high[half * HALO : (half + 1) * HALO]
            grad_low[here] = low[half * HALO : (half + 1) * HALO]

    def zone_table():
        sub, lane = iota((8, LANES), 0), iota((8, LANES), 1)
        high, across = zone.shape
        table = pltpu.roll(pltpu.roll(zone_own[...], 1, axis=0), 2, axis=1)
        for side in range(8):
            down, right = SIDES[side]
            got = pltpu.roll(zone_in[side], (1 + down * high) % 8, axis=0)
            got = pltpu.roll(got, (2 + right * across) % LANES, axis=1)
            row_ok = (sub == 0) if down < 0 else (sub == high + 1) if down > 0 else (sub >= 1) & (sub <= high)
            col_ok = (
                (lane == 1) if right < 0 else (lane == across + 2) if right > 0 else (lane >= 2) & (lane < across + 2)
            )
            table = jnp.where(row_ok & col_ok, got, table)
        picked = []
        for kernel in range(3):
            value = jnp.zeros((8, LANES), F32)
            for z in range(ZONES):
                value = jnp.where(table == z, zone_weights[kernel, z], value)
            picked.append(value)
        return jnp.concatenate(picked, axis=0)

    put_dose(dose[...], HALO, SIDE)
    for side in range(8):

        @pl.when(exists(side))
        def _(side=side):
            down, right = SIDES[side]
            zone_copy(SIDES.index((-down, -right))).wait_recv()

    spread = jnp.where(iota((LANES, wide), 0) == iota((LANES, wide), 1) // HALO, 1.0, 0.0).astype(BF16)
    table = zone_table()
    for _ in range(3):
        piece = table.astype(BF16)
        weight[...] = dot(piece, spread) if _ == 0 else weight[...] + dot(piece, spread)
        table = table - piece.astype(F32)

    def sweep(tile, window, edges, before, after):
        ahead = 2
        done = 0
        for u in range(steps):
            before(u)
            while done <= min(u + ahead, steps):
                tile(edges, done)
                done += 1
            window(edges, u)
            after(u)

    def nothing(u):
        return None

    await_halo(dose, 0, (8, 9))
    put_dose(halo_cols[0, 0], HALO, 0)
    put_dose(halo_cols[0, 1], HALO, SIDE + cols)
    sweep(tile_forward, window_forward, 0, lambda u: near.wait() if u == 0 else None, nothing)

    def arrive(turn, field, put, u):
        chunks = (0, 1, 2) if u == 0 else (u + 2,) if u + 2 < steps else ()
        corners = (10, 12) if u == 0 else (11, 13) if u == steps - 2 else ()
        await_halo(field, turn, (*chunks, *(4 + c for c in chunks), *corners))
        for side, square in ((0, 0), (1, rows // HALO + 1)):
            for c in chunks:
                put(halo_rows[turn, side, :, c * CHUNK : (c + 1) * CHUNK], square, SIDE + c * CHUNK)
            if u == 0:
                put(halo_corners[turn, 2 * side], square, 0)
            if u == steps - 2:
                put(halo_corners[turn, 2 * side + 1], square, SIDE + cols)

    def send_error(u):
        sides = (8, 10, 12) if u == 0 else (9, 11, 13) if u == steps - 1 else ()
        send(error, 1, (u, 4 + u, *sides))

    sweep(
        tile_forward,
        window_forward,
        1,
        lambda u: arrive(0, dose, lambda value, square, at: put_dose(value, square * HALO, at), u),
        send_error,
    )
    await_halo(error, 1, (8, 9))
    for side, at in ((0, 0), (1, SIDE + cols)):
        for square in range(rows // HALO):
            put_part(halo_cols[1, side, square * HALO : (square + 1) * HALO], 1 + square, at)
    sweep(tile_backward, window_backward, 0, nothing, nothing)
    sweep(tile_backward, window_backward, 1, lambda u: arrive(1, error, put_part, u), nothing)
    by_side(range(14), lambda piece: halo_copy(dose, 0, piece).wait_send())
    by_side(range(14), lambda piece: halo_copy(error, 1, piece).wait_send())
    for side in range(8):

        @pl.when(exists(side))
        def _(side=side):
            zone_copy(side).wait_send()


def blur(dims, dose, target, zone, zone_weights, bands):
    rows, cols = dose.shape
    wide, high = cols + 2 * SIDE, rows + 2 * HALO
    vmem = pl.BlockSpec(memory_space=pltpu.VMEM)
    smem = pl.BlockSpec(memory_space=pltpu.SMEM)
    dma = pltpu.SemaphoreType.DMA
    return pl.pallas_call(
        functools.partial(blur_kernel, dims),
        out_shape=[
            jax.ShapeDtypeStruct((rows, cols), F32),
            jax.ShapeDtypeStruct((rows, cols), BF16),
            jax.ShapeDtypeStruct((rows, cols), BF16),
        ],
        in_specs=[vmem, pl.BlockSpec(memory_space=pl.ANY), vmem, smem, *[vmem] * 6],
        out_specs=[vmem] * 3,
        scratch_shapes=[
            pltpu.VMEM((rows, cols), F32),
            dma,
            pltpu.VMEM((8, LANES), I32),
            pltpu.VMEM((8, 8, LANES), I32),
            pltpu.VMEM((2, 2, HALO, cols), F32),
            pltpu.VMEM((2, 2, rows, SIDE), F32),
            pltpu.VMEM((2, 4, HALO, SIDE), F32),
            pltpu.VMEM((high, wide), BF16),
            pltpu.VMEM((high, wide), BF16),
            pltpu.VMEM((3, high, wide), BF16),
            pltpu.VMEM((3, high, wide), BF16),
            pltpu.VMEM((2, 3, 2 * HALO, wide), BF16),
            pltpu.VMEM((2, 3, 2 * HALO, wide), BF16),
            pltpu.VMEM((rows, cols), F32),
            pltpu.VMEM((24, wide), F32),
            dma((2, 14)), dma((2, 14)), dma((8,)), dma((8,)),
        ],
        compiler_params=pltpu.CompilerParams(
            collective_id=1, has_side_effects=True, vmem_limit_bytes=40 * 2**20
        ),
        cost_estimate=cost(25),
        name="blur",
    )(dose, far(target), far(zone), far(zone_weights), *bands)


def per_device(dims, shot_dose, shot_frac, shot_pos, block_count, shot_tile, zone, zone_weights, target):
    n = dims[1]
    rows, cols = target.shape
    count, tile = block_count.reshape(1, -1), shot_tile.reshape(1, -1)
    recv, order, *bands = route(n, cols, shot_dose, shot_frac, shot_pos, count, tile)
    dose, buf, spans = deposit(recv, rows, cols)
    exposure, grad_high, grad_low = blur(dims, dose, target, zone, zone_weights.T, bands)
    slot_grad, exposure = sample(n, grad_high, grad_low, buf, spans, exposure)
    return exposure, give_back(n, slot_grad, tile, order)


def solution(mesh):
    dims = (mesh.shape["row"], mesh.shape["col"])
    return jax.shard_map(
        functools.partial(per_device, dims),
        mesh=mesh,
        in_specs=(
            P(("row", "col"), None),
            P(None, ("row", "col"), None),
            P(("row", "col"), None),
            P(("row", "col")),
            P(("row", "col"), None),
            P("row", "col"),
            P(),
            P("row", "col"),
        ),
        out_specs=(P("row", "col"), P(("row", "col"), None)),
        check_vma=False,
    )
```

```python
import functools
import math

import jax
import jax.numpy as jnp
import numpy as np
from jax import lax
from jax.experimental import pallas as pl
from jax.experimental.pallas import tpu as pltpu
from jax.sharding import PartitionSpec as P

HALO = 64
ZONES = 8
LANES = 128
CHUNK = 256
SHOTS = 512
SIDE = 128
SIGMAS = (0.125 * HALO, 0.25 * HALO, 0.5 * HALO)
MESH = pl.DeviceIdType.MESH
F32, BF16, I32 = jnp.float32, jnp.bfloat16, jnp.int32


def cost(us):
    return pl.CostEstimate(flops=0, bytes_accessed=int(us * 3.0e6), transcendentals=0)


def iota(shape, dim):
    return lax.broadcasted_iota(I32, shape, dim)


def split(x):
    high = x.astype(BF16)
    return high, (x - high.astype(F32)).astype(BF16)


def dot(a, b):
    return jnp.dot(a, b, preferred_element_type=F32)


def dot_nt(a, b):
    return lax.dot_general(a, b, (((1,), (1,)), ((), ())), preferred_element_type=F32)


def pick(onehot, x):
    first = x.astype(BF16)
    rest = x - first.astype(F32)
    second = rest.astype(BF16)
    third = (rest - second.astype(F32)).astype(BF16)
    return dot(onehot, first) + dot(onehot, second) + dot(onehot, third)


def taps(offset, sigma):
    reach = np.arange(-HALO, HALO + 1).astype(np.float64)
    total = float(np.exp(-reach * reach / (2.0 * sigma * sigma)).sum())
    value = jnp.exp(offset * offset * (-1.0 / (2.0 * sigma * sigma))) * (1.0 / total)
    return jnp.where(jnp.abs(offset) <= float(HALO), value, 0.0)


def far(x):
    return pltpu.with_memory_space_constraint(x, pltpu.HBM)


def slots_of(tile, width):
    n = tile.shape[0]
    times = width // n
    own, lane = iota((n, width), 0), iota((n, width), 1)
    other = lane // times
    tile_row = jnp.sum(jnp.where(own == other, tile, 0), axis=0, keepdims=True)
    same = tile == tile_row
    rank_row = jnp.sum(jnp.where(same & (own < other), 1, 0), axis=0, keepdims=True)
    once = lane % times == 0
    rank_col = jnp.sum(jnp.where(same & (other < own) & once, 1, 0), axis=1, keepdims=True)
    return tile * 2 + rank_col, tile_row * 2 + rank_row


def upright(line):
    n = line.shape[1]
    return jnp.sum(jnp.where(iota((n, n), 0) == iota((n, n), 1), line, 0), axis=1, keepdims=True)


def column_class(pixel):
    return 2 * (pixel >> 8) + jnp.where((pixel & (CHUNK - 1)) == CHUNK - 1, 1, 0)


def greet_all(n, me, row):
    barrier = pltpu.get_barrier_semaphore()
    for step in range(1, n):
        peer = (me + step) & (n - 1)
        pl.semaphore_signal(barrier, inc=1, device_id=(row, peer), device_id_type=MESH)
    return barrier


def exchange(n, me, row, source, target, send_sem, recv_sem, meanwhile):
    def copy(peer, source_slots, target_slots):
        return pltpu.make_async_remote_copy(
            src_ref=source.at[source_slots],
            dst_ref=target.at[target_slots],
            send_sem=send_sem,
            recv_sem=recv_sem,
            device_id=(row, peer),
            device_id_type=MESH,
        )

    for step in range(1, n):
        peer = (me + step) & (n - 1)
        copy(peer, peer, me).start()
    target[pl.ds(me, 1)] = source[pl.ds(me, 1)]
    meanwhile()
    every = copy((me + 1) & (n - 1), pl.ds(0, n - 1), pl.ds(0, n - 1))
    every.wait_recv()
    every.wait_send()


def make_bands(mid_high, mid_low, edge_high, edge_low, col_high, col_low):
    for kernel, sigma in enumerate(SIGMAS):
        shape = (2 * HALO, 4 * HALO)
        high, low = split(taps((iota(shape, 1) - iota(shape, 0) - HALO).astype(F32), sigma))
        for band, mid, edges in ((high, mid_high, edge_high), (low, mid_low, edge_low)):
            mid[kernel * 2 * HALO : (kernel + 1) * 2 * HALO] = band
            for e in range(2):
                edges[e, kernel * HALO : (kernel + 1) * HALO] = band[e * HALO : (e + 1) * HALO]
        shape = (2 * CHUNK, CHUNK)
        high, low = split(taps((iota(shape, 0) - iota(shape, 1) - SIDE).astype(F32), sigma))
        col_high[kernel] = high
        col_low[kernel] = low


BANDS = [
    jax.ShapeDtypeStruct(shape, BF16)
    for shape in ((6 * HALO, 4 * HALO), (2, 3 * HALO, 4 * HALO), (3, 2 * CHUNK, CHUNK))
    for _ in range(2)
]


def route_kernel(
    n, cols, dose, frac, pos, count, tile, recv, order, *rest
):
    bands, (parts, ordered, send, send_sem, recv_sem) = rest[:6], rest[6:]
    row, me = lax.axis_index("row"), lax.axis_index("col")
    barrier = greet_all(n, me, row)
    blocks = tile.shape[1]
    live = iota((blocks, LANES), 1) < upright(count[...])
    dead = 2 * (cols // CHUNK) - 1
    kind = jnp.where(live, column_class(jnp.minimum(pos[...] & (cols - 1), cols - 2)), dead)
    masks = [jnp.where(kind == j, 1.0, 0.0) for j in range(dead + 1)]
    before = jnp.where(iota((LANES, LANES), 0) < iota((LANES, LANES), 1), 1.0, 0.0).astype(BF16)
    prefix = dot(jnp.concatenate(masks, axis=0).astype(BF16), before)
    start = jnp.zeros((blocks, 1), F32)
    rank = jnp.zeros((blocks, LANES), F32)
    for j, mask in enumerate(masks):
        rank = rank + mask * (prefix[j * blocks : (j + 1) * blocks] + start)
        start = start + jnp.sum(mask, axis=1, keepdims=True)
    rank = rank.astype(I32)
    order[...] = rank
    fields = [
        jnp.where(live, dose[...], 0.0),
        frac[0],
        frac[1],
        jnp.where(live, pos[...] + 1, 0).astype(F32),
    ]
    for f, field in enumerate(fields):
        for part in range(3):
            piece = field.astype(BF16).astype(F32)
            parts[:, 4 * part + f] = piece
            field = field - piece
        parts[:, 12 + f] = jnp.zeros((blocks, LANES), F32)
    target = iota((LANES, LANES), 0)
    for b in range(blocks):
        moves = jnp.where(target == rank[b : b + 1], 1.0, 0.0).astype(BF16)
        ordered[b] = dot_nt(parts[b].astype(BF16), moves)
    width = 16 * blocks
    _, placed = slots_of(upright(tile[...]), width)
    out, col = iota((8 * n, width), 0), iota((8 * n, width), 1)
    chosen = (out // 4 == placed) & (out % 4 == col % 4) & (col % 16 < 12)
    onehot = jnp.where(chosen, 1.0, 0.0).astype(BF16)
    send[...] = dot(onehot, ordered[...].reshape(width, LANES).astype(BF16)).reshape(n, 8, LANES)
    pl.semaphore_wait(barrier, n - 1)
    exchange(n, me, row, send, recv, send_sem, recv_sem, lambda: make_bands(*bands))


def route(n, cols, dose, frac, pos, count, tile):
    vmem = pl.BlockSpec(memory_space=pltpu.VMEM)
    blocks = tile.shape[1]
    return pl.pallas_call(
        functools.partial(route_kernel, n, cols),
        out_shape=[
            jax.ShapeDtypeStruct((n, 8, LANES), F32),
            jax.ShapeDtypeStruct((blocks, LANES), I32),
            *BANDS,
        ],
        in_specs=[vmem] * 5,
        out_specs=[vmem] * 8,
        scratch_shapes=[
            pltpu.VMEM((blocks, 16, LANES), F32),
            pltpu.VMEM((blocks, 16, LANES), F32),
            pltpu.VMEM((n, 8, LANES), F32),
            pltpu.SemaphoreType.DMA,
            pltpu.SemaphoreType.DMA,
        ],
        compiler_params=pltpu.CompilerParams(
            collective_id=0, has_side_effects=True, vmem_limit_bytes=8 * 2**20
        ),
        cost_estimate=cost(10),
        name="route",
    )(*(far(x) for x in (dose, frac, pos, count, tile)))


def return_kernel(n, grads, tile, order, out, back, send_sem, recv_sem):
    row, me = lax.axis_index("row"), lax.axis_index("col")
    barrier = greet_all(n, me, row)
    blocks = tile.shape[1]
    placed, _ = slots_of(upright(tile[...]), blocks)
    onehot = jnp.where(placed == iota((blocks, 2 * n), 1), 1.0, 0.0).astype(BF16)
    pl.semaphore_wait(barrier, n - 1)
    exchange(n, me, row, grads, back, send_sem, recv_sem, lambda: None)
    found = pick(onehot, jnp.concatenate([back[i] for i in range(n)], axis=0))
    out[...] = jnp.take_along_axis(found, order[...], axis=1)


def give_back(n, grads, tile, order):
    vmem = pl.BlockSpec(memory_space=pltpu.VMEM)
    return pl.pallas_call(
        functools.partial(return_kernel, n),
        out_shape=jax.ShapeDtypeStruct((tile.shape[1], LANES), F32),
        in_specs=[vmem] * 3,
        out_specs=vmem,
        scratch_shapes=[
            pltpu.VMEM((n, 2, LANES), F32),
            pltpu.SemaphoreType.DMA,
            pltpu.SemaphoreType.DMA,
        ],
        compiler_params=pltpu.CompilerParams(
            collective_id=2, has_side_effects=True, vmem_limit_bytes=8 * 2**20
        ),
        cost_estimate=cost(10),
        name="give_back",
    )(grads, far(tile), order)


def shot_rows(buf, first, end):
    lane = iota((8, LANES), 1)
    tiles = [jnp.where(lane < end - i * LANES, buf[first + i], 0.0) for i in range(SHOTS // LANES)]
    line = lambda f: jnp.concatenate([tile[f : f + 1] for tile in tiles], axis=1)
    return line(0), line(1), line(2), line(3).astype(I32) - 1


def table(index, low, high, count):
    here = iota((count, index.shape[1]), 0).astype(F32).astype(BF16)
    first = index.astype(F32).astype(BF16)
    second = (index + 1).astype(F32).astype(BF16)
    at_first, at_second = here == first, here == second
    zero = jnp.zeros((), BF16)
    return [jnp.where(at_first, lo, jnp.where(at_second, hi, zero)) for lo, hi in zip(low, high)]


def col_table(place, frac, cols, window):
    pixel = jnp.minimum(place & (cols - 1), cols - 2)
    local = jnp.clip(pixel - window * CHUNK, -2, CHUNK)
    return table(local, split(1.0 - frac), split(frac), CHUNK)


def tiles_of_bin(n):
    return 2 * n + 2


def deposit_kernel(recv, dose, buf, spans, row_spans, sem):
    n = recv.shape[0]
    rows, cols = dose.shape
    bins = cols // CHUNK
    shift = int(math.log2(cols))
    lane = iota((8, LANES), 1)
    ends = []
    for half in range(2):
        place = recv[:, 4 * half + 3, :].astype(I32) - 1
        kind = column_class(jnp.minimum(place & (cols - 1), cols - 2))
        kind = jnp.where(place >= 0, kind, 2 * bins)
        ends.append([jnp.sum(jnp.where(kind <= j, 1, 0), axis=1, keepdims=True) for j in range(2 * bins)])
    which = iota((n, LANES), 1)
    chosen = (lax.rem(which, n) == iota((n, LANES), 0)) & (which < 2 * n)

    def to_lanes(first, second):
        spread = jnp.where(which < n, first, second)
        return jnp.sum(jnp.where(chosen, spread, 0), axis=0, keepdims=True)

    lines = []
    for q in range(bins):
        lines.append(to_lanes(*(e[2 * q - 2] if q else jnp.zeros((n, 1), I32) for e in ends)))
    for q in range(bins):
        lines.append(to_lanes(*(e[2 * q + 1] for e in ends)) - lines[q])
    row_spans[...] = jnp.concatenate(lines, axis=0)
    copy = pltpu.make_async_copy(row_spans, spans, sem)
    copy.start()
    dose[...] = jnp.zeros_like(dose)
    copy.wait()

    def append(block, begin, amount, carry):
        at, current = carry
        lane_at = at & (LANES - 1)
        moved = pltpu.roll(block, (at - begin) & (LANES - 1), axis=1)
        merged = jnp.where(lane < lane_at, current, moved)
        buf[at >> 7] = merged
        full = jnp.full((8, LANES), lane_at + amount, I32) >= LANES
        return at + amount, jnp.where(full, moved, merged)

    def gather(step, carry):
        for i in range(4):
            block = recv[4 * step + i]
            for half in range(2):
                index = half * n + 4 * step + i
                carry = [
                    append(block, spans[q, index], spans[bins + q, index], carry[q]) for q in range(bins)
                ]
                block = pltpu.roll(block, 4, axis=0)
        return carry

    starts = [q * tiles_of_bin(n) for q in range(bins)]
    empty = jnp.zeros((8, LANES), F32)
    found = lax.fori_loop(0, n // 4, gather, [(jnp.int32(s * LANES), empty) for s in starts])
    most = jnp.int32(0)
    for q, (at, last) in enumerate(found):
        buf[at >> 7] = jnp.where(lane < (at & (LANES - 1)), last, 0.0)
        buf[(at >> 7) + 1] = empty
        most = jnp.maximum(most, (at - starts[q] * LANES + SHOTS - 1) >> SHOTS.bit_length() - 1)
    spans[0, LANES - 1] = most

    def deposit(chunk, carry):
        for q in range(bins):
            first = starts[q] + SHOTS // LANES * chunk
            end = found[q][0] - first * LANES
            amount, frac_row, frac_col, place = shot_rows(buf, first, end)
            pixel_row = jnp.minimum(place >> shift, rows - 2)
            row_high, row_low = table(
                pixel_row, split(amount * (1.0 - frac_row)), split(amount * frac_row), rows
            )
            high, low = col_table(place, frac_col, cols, q)
            dose[:, q * CHUNK : (q + 1) * CHUNK] += (
                dot_nt(row_high, high) + dot_nt(row_low, high) + dot_nt(row_high, low)
            )
        return carry

    lax.fori_loop(0, most, deposit, 0)


def deposit(recv, rows, cols):
    vmem = pl.BlockSpec(memory_space=pltpu.VMEM)
    smem = pl.BlockSpec(memory_space=pltpu.SMEM)
    tiles = (cols // CHUNK) * tiles_of_bin(recv.shape[0])
    spans = (2 * (cols // CHUNK), LANES)
    return pl.pallas_call(
        deposit_kernel,
        out_shape=[
            jax.ShapeDtypeStruct((rows, cols), F32),
            jax.ShapeDtypeStruct((tiles, 8, LANES), F32),
            jax.ShapeDtypeStruct(spans, I32),
        ],
        in_specs=[vmem],
        out_specs=[vmem, vmem, smem],
        scratch_shapes=[pltpu.VMEM(spans, I32), pltpu.SemaphoreType.DMA],
        compiler_params=pltpu.CompilerParams(vmem_limit_bytes=16 * 2**20),
        cost_estimate=cost(8),
        name="deposit",
    )(recv)


def sample_kernel(grad_high, grad_low, buf, spans, exposure, out, exposure_out, values, sem):
    leave = pltpu.make_async_copy(exposure, exposure_out, sem)
    leave.start()
    n = out.shape[0]
    rows, cols = grad_high.shape
    bins = cols // CHUNK
    shift = int(math.log2(cols))
    starts = [q * tiles_of_bin(n) for q in range(bins)]

    def sample(chunk, carry):
        for q in range(bins):
            first = starts[q] + SHOTS // LANES * chunk
            _, frac_row, frac_col, place = shot_rows(buf, first, SHOTS)
            pixel_row = jnp.minimum(place >> shift, rows - 2)
            high, low = col_table(place, frac_col, cols, q)
            window = slice(q * CHUNK, (q + 1) * CHUNK)
            along = (
                dot(grad_high[:, window], high)
                + dot(grad_low[:, window], high)
                + dot(grad_high[:, window], low)
            )
            here = iota((rows, SHOTS), 0)
            weight = jnp.where(
                here == pixel_row, 1.0 - frac_row, jnp.where(here == pixel_row + 1, frac_row, 0.0)
            )
            got = jnp.sum(weight * along, axis=0, keepdims=True)
            for i in range(SHOTS // LANES):
                values[first + i, 0:1] = got[:, i * LANES : (i + 1) * LANES]
        return carry

    lax.fori_loop(0, spans[0, LANES - 1], sample, 0)

    lane = iota((1, LANES), 1)

    def take(begin, amount, at):
        lane_at, tile_at = at & (LANES - 1), at >> 7
        both = jnp.where(lane >= lane_at, values[tile_at, 0:1], values[tile_at + 1, 0:1])
        moved = pltpu.roll(both, (begin - at) & (LANES - 1), axis=1)
        return jnp.where((lane >= begin) & (lane < begin + amount), moved, 0.0)

    def spread(step, at):
        for i in range(8):
            at = spread_one(8 * step + i, at)
        return at

    def spread_one(i, at):
        at = list(at)
        both = []
        for half in range(2):
            total = jnp.zeros((1, LANES), F32)
            for q in range(bins):
                begin, amount = spans[q, half * n + i], spans[bins + q, half * n + i]
                total = total + take(begin, amount, at[q])
                at[q] = at[q] + amount
            both.append(total)
        out[i] = jnp.concatenate(both, axis=0)
        return at

    lax.fori_loop(0, n // 8, spread, [jnp.int32(s * LANES) for s in starts])
    leave.wait()


def sample(n, grad_high, grad_low, buf, spans, exposure):
    vmem = pl.BlockSpec(memory_space=pltpu.VMEM)
    smem = pl.BlockSpec(memory_space=pltpu.SMEM)
    return pl.pallas_call(
        sample_kernel,
        out_shape=[
            jax.ShapeDtypeStruct((n, 2, LANES), F32),
            jax.ShapeDtypeStruct(exposure.shape, F32),
        ],
        in_specs=[vmem, vmem, vmem, smem, pl.BlockSpec(memory_space=pl.ANY)],
        out_specs=[vmem, pl.BlockSpec(memory_space=pl.ANY)],
        scratch_shapes=[pltpu.VMEM(buf.shape, F32), pltpu.SemaphoreType.DMA],
        compiler_params=pltpu.CompilerParams(vmem_limit_bytes=16 * 2**20),
        cost_estimate=cost(8),
        name="sample",
    )(grad_high, grad_low, buf, spans, exposure)


SIDES = ((-1, 0), (1, 0), (0, -1), (0, 1), (-1, -1), (-1, 1), (1, -1), (1, 1))
PIECE_SIDE = (0, 0, 0, 0, 1, 1, 1, 1, 2, 3, 4, 5, 6, 7)
OPPOSITE = (4, 5, 6, 7, 0, 1, 2, 3, 9, 8, 13, 12, 11, 10)


def blur_kernel(
    dims, dose, target_far, zone, zone_weights,
    mid_high, mid_low, edge_high, edge_low, col_high, col_low,
    exposure, grad_high, grad_low,
    target, near_sem,
    zone_own, zone_in, halo_rows, halo_cols, halo_corners, dose_high, dose_low, part_high, part_low,
    mixed_high, mixed_low, error, weight, sends, recvs, zone_send, zone_recv,
):
    n_row, n_col = dims
    rows, cols = dose.shape
    wide = cols + 2 * SIDE
    steps = cols // CHUNK
    row, col = lax.axis_index("row"), lax.axis_index("col")

    def exists(side):
        down, right = SIDES[side]
        tests = []
        if down:
            tests.append(row > 0 if down < 0 else row < n_row - 1)
        if right:
            tests.append(col > 0 if right < 0 else col < n_col - 1)
        return functools.reduce(jnp.logical_and, tests)

    def neighbour(side):
        down, right = SIDES[side]
        return (row + down, col + right)

    def landing(turn, piece):
        if piece < 8:
            return halo_rows.at[turn, piece // 4, :, pl.ds(piece % 4 * CHUNK, CHUNK)]
        if piece < 10:
            return halo_cols.at[turn, piece - 8]
        return halo_corners.at[turn, piece - 10]

    def edge(field, piece):
        down, right = SIDES[PIECE_SIDE[piece]]
        high = pl.ds(0, rows) if not down else (pl.ds(0, HALO) if down < 0 else pl.ds(rows - HALO, HALO))
        if piece < 8:
            across = pl.ds(piece % 4 * CHUNK, CHUNK)
        else:
            across = pl.ds(0, SIDE) if right < 0 else pl.ds(cols - SIDE, SIDE)
        return field.at[high, across]

    def halo_copy(field, turn, piece):
        return pltpu.make_async_remote_copy(
            src_ref=edge(field, piece),
            dst_ref=landing(turn, OPPOSITE[piece]),
            send_sem=sends.at[turn, piece],
            recv_sem=recvs.at[turn, OPPOSITE[piece]],
            device_id=neighbour(PIECE_SIDE[piece]),
            device_id_type=MESH,
        )

    def zone_copy(side):
        down, right = SIDES[side]
        there = SIDES.index((-down, -right))
        return pltpu.make_async_remote_copy(
            src_ref=zone_own,
            dst_ref=zone_in.at[there],
            send_sem=zone_send.at[side],
            recv_sem=zone_recv.at[there],
            device_id=neighbour(side),
            device_id_type=MESH,
        )

    def by_side(pieces, act):
        for side in sorted({PIECE_SIDE[piece] for piece in pieces}, key=[PIECE_SIDE[p] for p in pieces].index):

            @pl.when(exists(side))
            def _(side=side):
                for piece in pieces:
                    if PIECE_SIDE[piece] == side:
                        act(piece)

    def send(field, turn, pieces):
        by_side(pieces, lambda piece: halo_copy(field, turn, piece).start())

    def await_halo(field, turn, pieces):
        by_side(pieces, lambda piece: halo_copy(field, turn, OPPOSITE[piece]).wait_recv())

    barrier = pltpu.get_barrier_semaphore()
    for side in range(8):

        @pl.when(exists(side))
        def _(side=side):
            pl.semaphore_signal(barrier, inc=1, device_id=neighbour(side), device_id_type=MESH)

    near = pltpu.make_async_copy(target_far, target, near_sem)
    near.start()
    zone_own[...] = jnp.zeros_like(zone_own)
    zone_own[0 : zone.shape[0], 0 : zone.shape[1]] = zone[...]
    for side in range(8):

        @pl.when(jnp.logical_not(exists(side)))
        def _(side=side):
            for turn in range(2):
                if side < 2:
                    halo_rows[turn, side] = jnp.zeros((HALO, cols), F32)
                elif side < 4:
                    halo_cols[turn, side - 2] = jnp.zeros((rows, SIDE), F32)
                else:
                    halo_corners[turn, side - 4] = jnp.zeros((HALO, SIDE), F32)
            zone_in[side] = jnp.zeros_like(zone_own)

    tall = 1 + jnp.where(row > 0, 1, 0) + jnp.where(row < n_row - 1, 1, 0)
    broad = 1 + jnp.where(col > 0, 1, 0) + jnp.where(col < n_col - 1, 1, 0)
    pl.semaphore_wait(barrier, tall * broad - 1)
    for side in range(8):

        @pl.when(exists(side))
        def _(side=side):
            zone_copy(side).start()

    send(dose, 0, (8, 9, 0, 1, 4, 5, 11, 13))
    send(dose, 0, (2, 3, 6, 7, 10, 12))

    def put_dose(value, first_row, first_col):
        high, low = split(value)
        here = pl.ds(first_row, value.shape[0]), pl.ds(first_col, value.shape[1])
        dose_high[here] = high
        dose_low[here] = low

    def put_part(value, square, first_col):
        across = pl.ds(first_col, value.shape[1])
        here = pl.ds(square * HALO, HALO)
        for kernel in range(3):
            factor = weight[8 * kernel + square : 8 * kernel + square + 1, across]
            high, low = split(factor * value)
            part_high[kernel, here, across] = high
            part_low[kernel, here, across] = low

    def tile_forward(edges, j):
        tile = pl.ds(j * CHUNK, CHUNK)

        def keep(band_high, band_low, first_row, first_out, count):
            here = pl.ds(first_row, 4 * HALO)
            in_high, in_low = dose_high[here, tile], dose_low[here, tile]
            field = dot(band_high, in_high) + dot(band_low, in_high) + dot(band_high, in_low)
            high, low = split(field)
            for kernel in range(3):
                part = slice(kernel * count, (kernel + 1) * count)
                mixed_high[edges, kernel, first_out : first_out + count, tile] = high[part]
                mixed_low[edges, kernel, first_out : first_out + count, tile] = low[part]

        if edges:
            keep(edge_high[0], edge_low[0], 0, 0, HALO)
            keep(edge_high[1], edge_low[1], 2 * HALO, HALO, HALO)
        else:
            keep(mid_high[...], mid_low[...], HALO, 0, 2 * HALO)

    def along_cols(edges, u, kernel):
        take = pl.ds(u * CHUNK, 2 * CHUNK)
        high, low = mixed_high[edges, kernel, :, take], mixed_low[edges, kernel, :, take]
        both = dot(jnp.concatenate([high, low], axis=0), col_high[kernel])
        return both[: 2 * HALO] + both[2 * HALO :] + dot(high, col_low[kernel])

    def window_forward(edges, u):
        squares = (1, rows // HALO) if edges else (2, 3)
        total = [jnp.zeros((HALO, CHUNK), F32) for _ in range(2)]
        for kernel in range(3):
            field = along_cols(edges, u, kernel)
            for half, square in enumerate(squares):
                line = 8 * kernel + square
                factor = weight[line : line + 1, SIDE + u * CHUNK : SIDE + (u + 1) * CHUNK]
                total[half] = total[half] + factor * field[half * HALO : (half + 1) * HALO]
        for half, square in enumerate(squares):
            here = pl.ds((square - 1) * HALO, HALO), pl.ds(u * CHUNK, CHUNK)
            exposure[here] = total[half]
            wrong = total[half] - target[here]
            error[here] = wrong
            put_part(wrong, square, SIDE + u * CHUNK)

    def tile_backward(edges, j):
        tile = pl.ds(j * CHUNK, CHUNK)

        def keep(kernel, band_high, band_low, first_row, first_out, count):
            here = pl.ds(first_row, 4 * HALO)
            in_high, in_low = part_high[kernel, here, tile], part_low[kernel, here, tile]
            field = dot(band_high, in_high) + dot(band_low, in_high) + dot(band_high, in_low)
            high, low = split(field)
            mixed_high[edges, kernel, first_out : first_out + count, tile] = high
            mixed_low[edges, kernel, first_out : first_out + count, tile] = low

        for kernel in range(3):
            if edges:
                part = pl.ds(kernel * HALO, HALO)
                keep(kernel, edge_high[0, part], edge_low[0, part], 0, 0, HALO)
                keep(kernel, edge_high[1, part], edge_low[1, part], 2 * HALO, HALO, HALO)
            else:
                part = pl.ds(kernel * 2 * HALO, 2 * HALO)
                keep(kernel, mid_high[part], mid_low[part], HALO, 0, 2 * HALO)

    def window_backward(edges, u):
        squares = (1, rows // HALO) if edges else (2, 3)
        high, low = split(sum(along_cols(edges, u, kernel) for kernel in range(3)))
        for half, square in enumerate(squares):
            here = pl.ds((square - 1) * HALO, HALO), pl.ds(u * CHUNK, CHUNK)
            grad_high[here] = high[half * HALO : (half + 1) * HALO]
            grad_low[here] = low[half * HALO : (half + 1) * HALO]

    def zone_table():
        sub, lane = iota((8, LANES), 0), iota((8, LANES), 1)
        high, across = zone.shape
        table = pltpu.roll(pltpu.roll(zone_own[...], 1, axis=0), 2, axis=1)
        for side in range(8):
            down, right = SIDES[side]
            got = pltpu.roll(zone_in[side], (1 + down * high) % 8, axis=0)
            got = pltpu.roll(got, (2 + right * across) % LANES, axis=1)
            row_ok = (sub == 0) if down < 0 else (sub == high + 1) if down > 0 else (sub >= 1) & (sub <= high)
            col_ok = (
                (lane == 1) if right < 0 else (lane == across + 2) if right > 0 else (lane >= 2) & (lane < across + 2)
            )
            table = jnp.where(row_ok & col_ok, got, table)
        picked = []
        for kernel in range(3):
            value = jnp.zeros((8, LANES), F32)
            for z in range(ZONES):
                value = jnp.where(table == z, zone_weights[kernel, z], value)
            picked.append(value)
        return jnp.concatenate(picked, axis=0)

    put_dose(dose[...], HALO, SIDE)
    for side in range(8):

        @pl.when(exists(side))
        def _(side=side):
            down, right = SIDES[side]
            zone_copy(SIDES.index((-down, -right))).wait_recv()

    spread = jnp.where(iota((LANES, wide), 0) == iota((LANES, wide), 1) // HALO, 1.0, 0.0).astype(BF16)
    table = zone_table()
    for _ in range(3):
        piece = table.astype(BF16)
        weight[...] = dot(piece, spread) if _ == 0 else weight[...] + dot(piece, spread)
        table = table - piece.astype(F32)

    def sweep(tile, window, edges, before, after):
        ahead = 2
        done = 0
        for u in range(steps):
            before(u)
            while done <= min(u + ahead, steps):
                tile(edges, done)
                done += 1
            window(edges, u)
            after(u)

    def nothing(u):
        return None

    await_halo(dose, 0, (8, 9))
    put_dose(halo_cols[0, 0], HALO, 0)
    put_dose(halo_cols[0, 1], HALO, SIDE + cols)
    sweep(tile_forward, window_forward, 0, lambda u: near.wait() if u == 0 else None, nothing)

    def arrive(turn, field, put, u):
        chunks = (0, 1, 2) if u == 0 else (u + 2,) if u + 2 < steps else ()
        corners = (10, 12) if u == 0 else (11, 13) if u == steps - 2 else ()
        await_halo(field, turn, (*chunks, *(4 + c for c in chunks), *corners))
        for side, square in ((0, 0), (1, rows // HALO + 1)):
            for c in chunks:
                put(halo_rows[turn, side, :, c * CHUNK : (c + 1) * CHUNK], square, SIDE + c * CHUNK)
            if u == 0:
                put(halo_corners[turn, 2 * side], square, 0)
            if u == steps - 2:
                put(halo_corners[turn, 2 * side + 1], square, SIDE + cols)

    def send_error(u):
        sides = (8, 10, 12) if u == 0 else (9, 11, 13) if u == steps - 1 else ()
        send(error, 1, (u, 4 + u, *sides))

    sweep(
        tile_forward,
        window_forward,
        1,
        lambda u: arrive(0, dose, lambda value, square, at: put_dose(value, square * HALO, at), u),
        send_error,
    )
    await_halo(error, 1, (8, 9))
    for side, at in ((0, 0), (1, SIDE + cols)):
        for square in range(rows // HALO):
            put_part(halo_cols[1, side, square * HALO : (square + 1) * HALO], 1 + square, at)
    sweep(tile_backward, window_backward, 0, nothing, nothing)
    sweep(tile_backward, window_backward, 1, lambda u: arrive(1, error, put_part, u), nothing)
    by_side(range(14), lambda piece: halo_copy(dose, 0, piece).wait_send())
    by_side(range(14), lambda piece: halo_copy(error, 1, piece).wait_send())
    for side in range(8):

        @pl.when(exists(side))
        def _(side=side):
            zone_copy(side).wait_send()


def blur(dims, dose, target, zone, zone_weights, bands):
    rows, cols = dose.shape
    wide, high = cols + 2 * SIDE, rows + 2 * HALO
    vmem = pl.BlockSpec(memory_space=pltpu.VMEM)
    smem = pl.BlockSpec(memory_space=pltpu.SMEM)
    dma = pltpu.SemaphoreType.DMA
    return pl.pallas_call(
        functools.partial(blur_kernel, dims),
        out_shape=[
            jax.ShapeDtypeStruct((rows, cols), F32),
            jax.ShapeDtypeStruct((rows, cols), BF16),
            jax.ShapeDtypeStruct((rows, cols), BF16),
        ],
        in_specs=[vmem, pl.BlockSpec(memory_space=pl.ANY), vmem, smem, *[vmem] * 6],
        out_specs=[vmem] * 3,
        scratch_shapes=[
            pltpu.VMEM((rows, cols), F32),
            dma,
            pltpu.VMEM((8, LANES), I32),
            pltpu.VMEM((8, 8, LANES), I32),
            pltpu.VMEM((2, 2, HALO, cols), F32),
            pltpu.VMEM((2, 2, rows, SIDE), F32),
            pltpu.VMEM((2, 4, HALO, SIDE), F32),
            pltpu.VMEM((high, wide), BF16),
            pltpu.VMEM((high, wide), BF16),
            pltpu.VMEM((3, high, wide), BF16),
            pltpu.VMEM((3, high, wide), BF16),
            pltpu.VMEM((2, 3, 2 * HALO, wide), BF16),
            pltpu.VMEM((2, 3, 2 * HALO, wide), BF16),
            pltpu.VMEM((rows, cols), F32),
            pltpu.VMEM((24, wide), F32),
            dma((2, 14)), dma((2, 14)), dma((8,)), dma((8,)),
        ],
        compiler_params=pltpu.CompilerParams(
            collective_id=1, has_side_effects=True, vmem_limit_bytes=40 * 2**20
        ),
        cost_estimate=cost(25),
        name="blur",
    )(dose, far(target), far(zone), far(zone_weights), *bands)


def per_device(dims, shot_dose, shot_frac, shot_pos, block_count, shot_tile, zone, zone_weights, target):
    n = dims[1]
    rows, cols = target.shape
    count, tile = block_count.reshape(1, -1), shot_tile.reshape(1, -1)
    recv, order, *bands = route(n, cols, shot_dose, shot_frac, shot_pos, count, tile)
    dose, buf, spans = deposit(recv, rows, cols)
    exposure, grad_high, grad_low = blur(dims, dose, target, zone, zone_weights.T, bands)
    slot_grad, exposure = sample(n, grad_high, grad_low, buf, spans, exposure)
    return exposure, give_back(n, slot_grad, tile, order)


def solution(mesh):
    dims = (mesh.shape["row"], mesh.shape["col"])
    return jax.shard_map(
        functools.partial(per_device, dims),
        mesh=mesh,
        in_specs=(
            P(("row", "col"), None),
            P(None, ("row", "col"), None),
            P(("row", "col"), None),
            P(("row", "col")),
            P(("row", "col"), None),
            P("row", "col"),
            P(),
            P("row", "col"),
        ),
        out_specs=(P("row", "col"), P(("row", "col"), None)),
        check_vma=False,
    )
```

```python
import functools
import math

import jax
import jax.numpy as jnp
import numpy as np
from jax import lax
from jax.experimental import pallas as pl
from jax.experimental.pallas import tpu as pltpu
from jax.sharding import PartitionSpec as P

HALO = 64
ZONES = 8
LANES = 128
CHUNK = 256
SHOTS = 512
SIDE = 128
SIGMAS = (0.125 * HALO, 0.25 * HALO, 0.5 * HALO)
MESH = pl.DeviceIdType.MESH
F32, BF16, I32 = jnp.float32, jnp.bfloat16, jnp.int32


def cost(us):
    return pl.CostEstimate(flops=0, bytes_accessed=int(us * 3.0e6), transcendentals=0)


def iota(shape, dim):
    return lax.broadcasted_iota(I32, shape, dim)


def split(x):
    high = x.astype(BF16)
    return high, (x - high.astype(F32)).astype(BF16)


def dot(a, b):
    return jnp.dot(a, b, preferred_element_type=F32)


def dot_nt(a, b):
    return lax.dot_general(a, b, (((1,), (1,)), ((), ())), preferred_element_type=F32)


def pick(onehot, x):
    first = x.astype(BF16)
    rest = x - first.astype(F32)
    second = rest.astype(BF16)
    third = (rest - second.astype(F32)).astype(BF16)
    return dot(onehot, first) + dot(onehot, second) + dot(onehot, third)


def taps(offset, sigma):
    reach = np.arange(-HALO, HALO + 1).astype(np.float64)
    total = float(np.exp(-reach * reach / (2.0 * sigma * sigma)).sum())
    value = jnp.exp(offset * offset * (-1.0 / (2.0 * sigma * sigma))) * (1.0 / total)
    return jnp.where(jnp.abs(offset) <= float(HALO), value, 0.0)


def far(x):
    return pltpu.with_memory_space_constraint(x, pltpu.HBM)


def slots_of(tile, width):
    n = tile.shape[0]
    times = width // n
    own, lane = iota((n, width), 0), iota((n, width), 1)
    other = lane // times
    tile_row = jnp.sum(jnp.where(own == other, tile, 0), axis=0, keepdims=True)
    same = tile == tile_row
    rank_row = jnp.sum(jnp.where(same & (own < other), 1, 0), axis=0, keepdims=True)
    once = lane % times == 0
    rank_col = jnp.sum(jnp.where(same & (other < own) & once, 1, 0), axis=1, keepdims=True)
    return tile * 2 + rank_col, tile_row * 2 + rank_row


def upright(line):
    n = line.shape[1]
    return jnp.sum(jnp.where(iota((n, n), 0) == iota((n, n), 1), line, 0), axis=1, keepdims=True)


def column_class(pixel):
    return 2 * (pixel >> 8) + jnp.where((pixel & (CHUNK - 1)) == CHUNK - 1, 1, 0)


def greet_all(n, me, row):
    barrier = pltpu.get_barrier_semaphore()
    for step in range(1, n):
        peer = (me + step) & (n - 1)
        pl.semaphore_signal(barrier, inc=1, device_id=(row, peer), device_id_type=MESH)
    return barrier


def exchange(n, me, row, source, target, send_sem, recv_sem, meanwhile):
    def copy(peer, source_slots, target_slots):
        return pltpu.make_async_remote_copy(
            src_ref=source.at[source_slots],
            dst_ref=target.at[target_slots],
            send_sem=send_sem,
            recv_sem=recv_sem,
            device_id=(row, peer),
            device_id_type=MESH,
        )

    for step in range(1, n):
        peer = (me + step) & (n - 1)
        copy(peer, peer, me).start()
    target[pl.ds(me, 1)] = source[pl.ds(me, 1)]
    meanwhile()
    every = copy((me + 1) & (n - 1), pl.ds(0, n - 1), pl.ds(0, n - 1))
    every.wait_recv()
    every.wait_send()


def make_bands(mid_high, mid_low, edge_high, edge_low, col_high, col_low):
    for kernel, sigma in enumerate(SIGMAS):
        shape = (2 * HALO, 4 * HALO)
        high, low = split(taps((iota(shape, 1) - iota(shape, 0) - HALO).astype(F32), sigma))
        for band, mid, edges in ((high, mid_high, edge_high), (low, mid_low, edge_low)):
            mid[kernel * 2 * HALO : (kernel + 1) * 2 * HALO] = band
            for e in range(2):
                edges[e, kernel * HALO : (kernel + 1) * HALO] = band[e * HALO : (e + 1) * HALO]
        shape = (2 * CHUNK, CHUNK)
        high, low = split(taps((iota(shape, 0) - iota(shape, 1) - SIDE).astype(F32), sigma))
        col_high[kernel] = high
        col_low[kernel] = low


BANDS = [
    jax.ShapeDtypeStruct(shape, BF16)
    for shape in ((6 * HALO, 4 * HALO), (2, 3 * HALO, 4 * HALO), (3, 2 * CHUNK, CHUNK))
    for _ in range(2)
]


def route_kernel(
    n, cols, dose, frac, pos, count, tile, recv, order, *rest
):
    bands, (parts, ordered, send, send_sem, recv_sem) = rest[:6], rest[6:]
    row, me = lax.axis_index("row"), lax.axis_index("col")
    barrier = greet_all(n, me, row)
    blocks = tile.shape[1]
    live = iota((blocks, LANES), 1) < upright(count[...])
    dead = 2 * (cols // CHUNK) - 1
    kind = jnp.where(live, column_class(jnp.minimum(pos[...] & (cols - 1), cols - 2)), dead)
    masks = [jnp.where(kind == j, 1.0, 0.0) for j in range(dead + 1)]
    before = jnp.where(iota((LANES, LANES), 0) < iota((LANES, LANES), 1), 1.0, 0.0).astype(BF16)
    prefix = dot(jnp.concatenate(masks, axis=0).astype(BF16), before)
    start = jnp.zeros((blocks, 1), F32)
    rank = jnp.zeros((blocks, LANES), F32)
    for j, mask in enumerate(masks):
        rank = rank + mask * (prefix[j * blocks : (j + 1) * blocks] + start)
        start = start + jnp.sum(mask, axis=1, keepdims=True)
    rank = rank.astype(I32)
    order[...] = rank
    fields = [
        jnp.where(live, dose[...], 0.0),
        frac[0],
        frac[1],
        jnp.where(live, pos[...] + 1, 0).astype(F32),
    ]
    for f, field in enumerate(fields):
        for part in range(3):
            piece = field.astype(BF16).astype(F32)
            parts[:, 4 * part + f] = piece
            field = field - piece
        parts[:, 12 + f] = jnp.zeros((blocks, LANES), F32)
    target = iota((LANES, LANES), 0)
    for b in range(blocks):
        moves = jnp.where(target == rank[b : b + 1], 1.0, 0.0).astype(BF16)
        ordered[b] = dot_nt(parts[b].astype(BF16), moves)
    width = 16 * blocks
    _, placed = slots_of(upright(tile[...]), width)
    out, col = iota((8 * n, width), 0), iota((8 * n, width), 1)
    chosen = (out // 4 == placed) & (out % 4 == col % 4) & (col % 16 < 12)
    onehot = jnp.where(chosen, 1.0, 0.0).astype(BF16)
    send[...] = dot(onehot, ordered[...].reshape(width, LANES).astype(BF16)).reshape(n, 8, LANES)
    pl.semaphore_wait(barrier, n - 1)
    exchange(n, me, row, send, recv, send_sem, recv_sem, lambda: make_bands(*bands))


def route(n, cols, dose, frac, pos, count, tile):
    vmem = pl.BlockSpec(memory_space=pltpu.VMEM)
    blocks = tile.shape[1]
    return pl.pallas_call(
        functools.partial(route_kernel, n, cols),
        out_shape=[
            jax.ShapeDtypeStruct((n, 8, LANES), F32),
            jax.ShapeDtypeStruct((blocks, LANES), I32),
            *BANDS,
        ],
        in_specs=[vmem] * 5,
        out_specs=[vmem] * 8,
        scratch_shapes=[
            pltpu.VMEM((blocks, 16, LANES), F32),
            pltpu.VMEM((blocks, 16, LANES), F32),
            pltpu.VMEM((n, 8, LANES), F32),
            pltpu.SemaphoreType.DMA,
            pltpu.SemaphoreType.DMA,
        ],
        compiler_params=pltpu.CompilerParams(
            collective_id=0, has_side_effects=True, vmem_limit_bytes=8 * 2**20
        ),
        cost_estimate=cost(10),
        name="route",
    )(*(far(x) for x in (dose, frac, pos, count, tile)))


def return_kernel(n, grads, tile, order, out, back, send_sem, recv_sem):
    row, me = lax.axis_index("row"), lax.axis_index("col")
    barrier = greet_all(n, me, row)
    blocks = tile.shape[1]
    placed, _ = slots_of(upright(tile[...]), blocks)
    onehot = jnp.where(placed == iota((blocks, 2 * n), 1), 1.0, 0.0).astype(BF16)
    pl.semaphore_wait(barrier, n - 1)
    exchange(n, me, row, grads, back, send_sem, recv_sem, lambda: None)
    found = pick(onehot, jnp.concatenate([back[i] for i in range(n)], axis=0))
    out[...] = jnp.take_along_axis(found, order[...], axis=1)


def give_back(n, grads, tile, order):
    vmem = pl.BlockSpec(memory_space=pltpu.VMEM)
    return pl.pallas_call(
        functools.partial(return_kernel, n),
        out_shape=jax.ShapeDtypeStruct((tile.shape[1], LANES), F32),
        in_specs=[vmem] * 3,
        out_specs=vmem,
        scratch_shapes=[
            pltpu.VMEM((n, 2, LANES), F32),
            pltpu.SemaphoreType.DMA,
            pltpu.SemaphoreType.DMA,
        ],
        compiler_params=pltpu.CompilerParams(
            collective_id=2, has_side_effects=True, vmem_limit_bytes=8 * 2**20
        ),
        cost_estimate=cost(10),
        name="give_back",
    )(grads, far(tile), order)


def shot_rows(buf, first, end):
    lane = iota((8, LANES), 1)
    tiles = [jnp.where(lane < end - i * LANES, buf[first + i], 0.0) for i in range(SHOTS // LANES)]
    line = lambda f: jnp.concatenate([tile[f : f + 1] for tile in tiles], axis=1)
    return line(0), line(1), line(2), line(3).astype(I32) - 1


def table(index, low, high, count):
    here = iota((count, index.shape[1]), 0).astype(F32).astype(BF16)
    first = index.astype(F32).astype(BF16)
    second = (index + 1).astype(F32).astype(BF16)
    at_first, at_second = here == first, here == second
    zero = jnp.zeros((), BF16)
    return [jnp.where(at_first, lo, jnp.where(at_second, hi, zero)) for lo, hi in zip(low, high)]


def col_table(place, frac, cols, window):
    pixel = jnp.minimum(place & (cols - 1), cols - 2)
    local = jnp.clip(pixel - window * CHUNK, -2, CHUNK)
    return table(local, split(1.0 - frac), split(frac), CHUNK)


def tiles_of_bin(n):
    return 2 * n + 2


def deposit_kernel(recv, dose, buf, spans, row_spans, sem):
    n = recv.shape[0]
    rows, cols = dose.shape
    bins = cols // CHUNK
    shift = int(math.log2(cols))
    lane = iota((8, LANES), 1)
    ends = []
    for half in range(2):
        place = recv[:, 4 * half + 3, :].astype(I32) - 1
        kind = column_class(jnp.minimum(place & (cols - 1), cols - 2))
        kind = jnp.where(place >= 0, kind, 2 * bins)
        ends.append([jnp.sum(jnp.where(kind <= j, 1, 0), axis=1, keepdims=True) for j in range(2 * bins)])
    which = iota((n, LANES), 1)
    chosen = (lax.rem(which, n) == iota((n, LANES), 0)) & (which < 2 * n)

    def to_lanes(first, second):
        spread = jnp.where(which < n, first, second)
        return jnp.sum(jnp.where(chosen, spread, 0), axis=0, keepdims=True)

    lines = []
    for q in range(bins):
        lines.append(to_lanes(*(e[2 * q - 2] if q else jnp.zeros((n, 1), I32) for e in ends)))
    for q in range(bins):
        lines.append(to_lanes(*(e[2 * q + 1] for e in ends)) - lines[q])
    row_spans[...] = jnp.concatenate(lines, axis=0)
    copy = pltpu.make_async_copy(row_spans, spans, sem)
    copy.start()
    dose[...] = jnp.zeros_like(dose)
    copy.wait()

    def append(block, begin, amount, carry):
        at, current = carry
        lane_at = at & (LANES - 1)
        moved = pltpu.roll(block, (at - begin) & (LANES - 1), axis=1)
        merged = jnp.where(lane < lane_at, current, moved)
        buf[at >> 7] = merged
        full = jnp.full((8, LANES), lane_at + amount, I32) >= LANES
        return at + amount, jnp.where(full, moved, merged)

    def gather(step, carry):
        for i in range(4):
            block = recv[4 * step + i]
            for half in range(2):
                index = half * n + 4 * step + i
                carry = [
                    append(block, spans[q, index], spans[bins + q, index], carry[q]) for q in range(bins)
                ]
                block = pltpu.roll(block, 4, axis=0)
        return carry

    starts = [q * tiles_of_bin(n) for q in range(bins)]
    empty = jnp.zeros((8, LANES), F32)
    found = lax.fori_loop(0, n // 4, gather, [(jnp.int32(s * LANES), empty) for s in starts])
    most = jnp.int32(0)
    for q, (at, last) in enumerate(found):
        buf[at >> 7] = jnp.where(lane < (at & (LANES - 1)), last, 0.0)
        buf[(at >> 7) + 1] = empty
        most = jnp.maximum(most, (at - starts[q] * LANES + SHOTS - 1) >> SHOTS.bit_length() - 1)
    spans[0, LANES - 1] = most

    def deposit(chunk, carry):
        for q in range(bins):
            first = starts[q] + SHOTS // LANES * chunk
            end = found[q][0] - first * LANES
            amount, frac_row, frac_col, place = shot_rows(buf, first, end)
            pixel_row = jnp.minimum(place >> shift, rows - 2)
            row_high, row_low = table(
                pixel_row, split(amount * (1.0 - frac_row)), split(amount * frac_row), rows
            )
            high, low = col_table(place, frac_col, cols, q)
            dose[:, q * CHUNK : (q + 1) * CHUNK] += (
                dot_nt(row_high, high) + dot_nt(row_low, high) + dot_nt(row_high, low)
            )
        return carry

    lax.fori_loop(0, most, deposit, 0)


def deposit(recv, rows, cols):
    vmem = pl.BlockSpec(memory_space=pltpu.VMEM)
    smem = pl.BlockSpec(memory_space=pltpu.SMEM)
    tiles = (cols // CHUNK) * tiles_of_bin(recv.shape[0])
    spans = (2 * (cols // CHUNK), LANES)
    return pl.pallas_call(
        deposit_kernel,
        out_shape=[
            jax.ShapeDtypeStruct((rows, cols), F32),
            jax.ShapeDtypeStruct((tiles, 8, LANES), F32),
            jax.ShapeDtypeStruct(spans, I32),
        ],
        in_specs=[vmem],
        out_specs=[vmem, vmem, smem],
        scratch_shapes=[pltpu.VMEM(spans, I32), pltpu.SemaphoreType.DMA],
        compiler_params=pltpu.CompilerParams(vmem_limit_bytes=16 * 2**20),
        cost_estimate=cost(8),
        name="deposit",
    )(recv)


def sample_kernel(grad_high, grad_low, buf, spans, exposure, out, exposure_out, values, sem):
    leave = pltpu.make_async_copy(exposure, exposure_out, sem)
    leave.start()
    n = out.shape[0]
    rows, cols = grad_high.shape
    bins = cols // CHUNK
    shift = int(math.log2(cols))
    starts = [q * tiles_of_bin(n) for q in range(bins)]

    def sample(chunk, carry):
        for q in range(bins):
            first = starts[q] + SHOTS // LANES * chunk
            _, frac_row, frac_col, place = shot_rows(buf, first, SHOTS)
            pixel_row = jnp.minimum(place >> shift, rows - 2)
            high, low = col_table(place, frac_col, cols, q)
            window = slice(q * CHUNK, (q + 1) * CHUNK)
            along = (
                dot(grad_high[:, window], high)
                + dot(grad_low[:, window], high)
                + dot(grad_high[:, window], low)
            )
            here = iota((rows, SHOTS), 0)
            weight = jnp.where(
                here == pixel_row, 1.0 - frac_row, jnp.where(here == pixel_row + 1, frac_row, 0.0)
            )
            got = jnp.sum(weight * along, axis=0, keepdims=True)
            for i in range(SHOTS // LANES):
                values[first + i, 0:1] = got[:, i * LANES : (i + 1) * LANES]
        return carry

    lax.fori_loop(0, spans[0, LANES - 1], sample, 0)

    lane = iota((1, LANES), 1)

    def take(begin, amount, at):
        lane_at, tile_at = at & (LANES - 1), at >> 7
        both = jnp.where(lane >= lane_at, values[tile_at, 0:1], values[tile_at + 1, 0:1])
        moved = pltpu.roll(both, (begin - at) & (LANES - 1), axis=1)
        return jnp.where((lane >= begin) & (lane < begin + amount), moved, 0.0)

    def spread(step, at):
        for i in range(8):
            at = spread_one(8 * step + i, at)
        return at

    def spread_one(i, at):
        at = list(at)
        both = []
        for half in range(2):
            total = jnp.zeros((1, LANES), F32)
            for q in range(bins):
                begin, amount = spans[q, half * n + i], spans[bins + q, half * n + i]
                total = total + take(begin, amount, at[q])
                at[q] = at[q] + amount
            both.append(total)
        out[i] = jnp.concatenate(both, axis=0)
        return at

    lax.fori_loop(0, n // 8, spread, [jnp.int32(s * LANES) for s in starts])
    leave.wait()


def sample(n, grad_high, grad_low, buf, spans, exposure):
    vmem = pl.BlockSpec(memory_space=pltpu.VMEM)
    smem = pl.BlockSpec(memory_space=pltpu.SMEM)
    return pl.pallas_call(
        sample_kernel,
        out_shape=[
            jax.ShapeDtypeStruct((n, 2, LANES), F32),
            jax.ShapeDtypeStruct(exposure.shape, F32),
        ],
        in_specs=[vmem, vmem, vmem, smem, pl.BlockSpec(memory_space=pl.ANY)],
        out_specs=[vmem, pl.BlockSpec(memory_space=pl.ANY)],
        scratch_shapes=[pltpu.VMEM(buf.shape, F32), pltpu.SemaphoreType.DMA],
        compiler_params=pltpu.CompilerParams(vmem_limit_bytes=16 * 2**20),
        cost_estimate=cost(8),
        name="sample",
    )(grad_high, grad_low, buf, spans, exposure)


SIDES = ((-1, 0), (1, 0), (0, -1), (0, 1), (-1, -1), (-1, 1), (1, -1), (1, 1))
PIECE_SIDE = (0, 0, 0, 0, 1, 1, 1, 1, 2, 3, 4, 5, 6, 7)
OPPOSITE = (4, 5, 6, 7, 0, 1, 2, 3, 9, 8, 13, 12, 11, 10)


def blur_kernel(
    dims, dose, target_far, zone, zone_weights,
    mid_high, mid_low, edge_high, edge_low, col_high, col_low,
    exposure, grad_high, grad_low,
    target, near_sem,
    zone_own, zone_in, halo_rows, halo_cols, halo_corners, dose_high, dose_low, part_high, part_low,
    mixed_high, mixed_low, error, weight, sends, recvs, zone_send, zone_recv,
):
    n_row, n_col = dims
    rows, cols = dose.shape
    wide = cols + 2 * SIDE
    steps = cols // CHUNK
    row, col = lax.axis_index("row"), lax.axis_index("col")

    def exists(side):
        down, right = SIDES[side]
        tests = []
        if down:
            tests.append(row > 0 if down < 0 else row < n_row - 1)
        if right:
            tests.append(col > 0 if right < 0 else col < n_col - 1)
        return functools.reduce(jnp.logical_and, tests)

    def neighbour(side):
        down, right = SIDES[side]
        return (row + down, col + right)

    def landing(turn, piece):
        if piece < 8:
            return halo_rows.at[turn, piece // 4, :, pl.ds(piece % 4 * CHUNK, CHUNK)]
        if piece < 10:
            return halo_cols.at[turn, piece - 8]
        return halo_corners.at[turn, piece - 10]

    def edge(field, piece):
        down, right = SIDES[PIECE_SIDE[piece]]
        high = pl.ds(0, rows) if not down else (pl.ds(0, HALO) if down < 0 else pl.ds(rows - HALO, HALO))
        if piece < 8:
            across = pl.ds(piece % 4 * CHUNK, CHUNK)
        else:
            across = pl.ds(0, SIDE) if right < 0 else pl.ds(cols - SIDE, SIDE)
        return field.at[high, across]

    def halo_copy(field, turn, piece):
        return pltpu.make_async_remote_copy(
            src_ref=edge(field, piece),
            dst_ref=landing(turn, OPPOSITE[piece]),
            send_sem=sends.at[turn, piece],
            recv_sem=recvs.at[turn, OPPOSITE[piece]],
            device_id=neighbour(PIECE_SIDE[piece]),
            device_id_type=MESH,
        )

    def zone_copy(side):
        down, right = SIDES[side]
        there = SIDES.index((-down, -right))
        return pltpu.make_async_remote_copy(
            src_ref=zone_own,
            dst_ref=zone_in.at[there],
            send_sem=zone_send.at[side],
            recv_sem=zone_recv.at[there],
            device_id=neighbour(side),
            device_id_type=MESH,
        )

    def by_side(pieces, act):
        for side in sorted({PIECE_SIDE[piece] for piece in pieces}, key=[PIECE_SIDE[p] for p in pieces].index):

            @pl.when(exists(side))
            def _(side=side):
                for piece in pieces:
                    if PIECE_SIDE[piece] == side:
                        act(piece)

    def send(field, turn, pieces):
        by_side(pieces, lambda piece: halo_copy(field, turn, piece).start())

    def await_halo(field, turn, pieces):
        by_side(pieces, lambda piece: halo_copy(field, turn, OPPOSITE[piece]).wait_recv())

    barrier = pltpu.get_barrier_semaphore()
    for side in range(8):

        @pl.when(exists(side))
        def _(side=side):
            pl.semaphore_signal(barrier, inc=1, device_id=neighbour(side), device_id_type=MESH)

    near = pltpu.make_async_copy(target_far, target, near_sem)
    near.start()
    zone_own[...] = jnp.zeros_like(zone_own)
    zone_own[0 : zone.shape[0], 0 : zone.shape[1]] = zone[...]
    for side in range(8):

        @pl.when(jnp.logical_not(exists(side)))
        def _(side=side):
            for turn in range(2):
                if side < 2:
                    halo_rows[turn, side] = jnp.zeros((HALO, cols), F32)
                elif side < 4:
                    halo_cols[turn, side - 2] = jnp.zeros((rows, SIDE), F32)
                else:
                    halo_corners[turn, side - 4] = jnp.zeros((HALO, SIDE), F32)
            zone_in[side] = jnp.zeros_like(zone_own)

    tall = 1 + jnp.where(row > 0, 1, 0) + jnp.where(row < n_row - 1, 1, 0)
    broad = 1 + jnp.where(col > 0, 1, 0) + jnp.where(col < n_col - 1, 1, 0)
    pl.semaphore_wait(barrier, tall * broad - 1)
    for side in range(8):

        @pl.when(exists(side))
        def _(side=side):
            zone_copy(side).start()

    send(dose, 0, (8, 9, 0, 1, 4, 5, 11, 13))
    send(dose, 0, (2, 3, 6, 7, 10, 12))

    def put_dose(value, first_row, first_col):
        high, low = split(value)
        here = pl.ds(first_row, value.shape[0]), pl.ds(first_col, value.shape[1])
        dose_high[here] = high
        dose_low[here] = low

    def put_part(value, square, first_col):
        across = pl.ds(first_col, value.shape[1])
        here = pl.ds(square * HALO, HALO)
        for kernel in range(3):
            factor = weight[8 * kernel + square : 8 * kernel + square + 1, across]
            high, low = split(factor * value)
            part_high[kernel, here, across] = high
            part_low[kernel, here, across] = low

    def tile_forward(edges, j):
        tile = pl.ds(j * CHUNK, CHUNK)

        def keep(band_high, band_low, first_row, first_out, count):
            here = pl.ds(first_row, 4 * HALO)
            in_high, in_low = dose_high[here, tile], dose_low[here, tile]
            field = dot(band_high, in_high) + dot(band_low, in_high) + dot(band_high, in_low)
            high, low = split(field)
            for kernel in range(3):
                part = slice(kernel * count, (kernel + 1) * count)
                mixed_high[edges, kernel, first_out : first_out + count, tile] = high[part]
                mixed_low[edges, kernel, first_out : first_out + count, tile] = low[part]

        if edges:
            keep(edge_high[0], edge_low[0], 0, 0, HALO)
            keep(edge_high[1], edge_low[1], 2 * HALO, HALO, HALO)
        else:
            keep(mid_high[...], mid_low[...], HALO, 0, 2 * HALO)

    def along_cols(edges, u, kernel):
        take = pl.ds(u * CHUNK, 2 * CHUNK)
        high, low = mixed_high[edges, kernel, :, take], mixed_low[edges, kernel, :, take]
        both = dot(jnp.concatenate([high, low], axis=0), col_high[kernel])
        return both[: 2 * HALO] + both[2 * HALO :] + dot(high, col_low[kernel])

    def window_forward(edges, u):
        squares = (1, rows // HALO) if edges else (2, 3)
        total = [jnp.zeros((HALO, CHUNK), F32) for _ in range(2)]
        for kernel in range(3):
            field = along_cols(edges, u, kernel)
            for half, square in enumerate(squares):
                line = 8 * kernel + square
                factor = weight[line : line + 1, SIDE + u * CHUNK : SIDE + (u + 1) * CHUNK]
                total[half] = total[half] + factor * field[half * HALO : (half + 1) * HALO]
        for half, square in enumerate(squares):
            here = pl.ds((square - 1) * HALO, HALO), pl.ds(u * CHUNK, CHUNK)
            exposure[here] = total[half]
            wrong = total[half] - target[here]
            error[here] = wrong
            put_part(wrong, square, SIDE + u * CHUNK)

    def tile_backward(edges, j):
        tile = pl.ds(j * CHUNK, CHUNK)

        def keep(kernel, band_high, band_low, first_row, first_out, count):
            here = pl.ds(first_row, 4 * HALO)
            in_high, in_low = part_high[kernel, here, tile], part_low[kernel, here, tile]
            field = dot(band_high, in_high) + dot(band_low, in_high) + dot(band_high, in_low)
            high, low = split(field)
            mixed_high[edges, kernel, first_out : first_out + count, tile] = high
            mixed_low[edges, kernel, first_out : first_out + count, tile] = low

        for kernel in range(3):
            if edges:
                part = pl.ds(kernel * HALO, HALO)
                keep(kernel, edge_high[0, part], edge_low[0, part], 0, 0, HALO)
                keep(kernel, edge_high[1, part], edge_low[1, part], 2 * HALO, HALO, HALO)
            else:
                part = pl.ds(kernel * 2 * HALO, 2 * HALO)
                keep(kernel, mid_high[part], mid_low[part], HALO, 0, 2 * HALO)

    def window_backward(edges, u):
        squares = (1, rows // HALO) if edges else (2, 3)
        high, low = split(sum(along_cols(edges, u, kernel) for kernel in range(3)))
        for half, square in enumerate(squares):
            here = pl.ds((square - 1) * HALO, HALO), pl.ds(u * CHUNK, CHUNK)
            grad_high[here] = high[half * HALO : (half + 1) * HALO]
            grad_low[here] = low[half * HALO : (half + 1) * HALO]

    def zone_table():
        sub, lane = iota((8, LANES), 0), iota((8, LANES), 1)
        high, across = zone.shape
        table = pltpu.roll(pltpu.roll(zone_own[...], 1, axis=0), 2, axis=1)
        for side in range(8):
            down, right = SIDES[side]
            got = pltpu.roll(zone_in[side], (1 + down * high) % 8, axis=0)
            got = pltpu.roll(got, (2 + right * across) % LANES, axis=1)
            row_ok = (sub == 0) if down < 0 else (sub == high + 1) if down > 0 else (sub >= 1) & (sub <= high)
            col_ok = (
                (lane == 1) if right < 0 else (lane == across + 2) if right > 0 else (lane >= 2) & (lane < across + 2)
            )
            table = jnp.where(row_ok & col_ok, got, table)
        picked = []
        for kernel in range(3):
            value = jnp.zeros((8, LANES), F32)
            for z in range(ZONES):
                value = jnp.where(table == z, zone_weights[kernel, z], value)
            picked.append(value)
        return jnp.concatenate(picked, axis=0)

    put_dose(dose[...], HALO, SIDE)
    for side in range(8):

        @pl.when(exists(side))
        def _(side=side):
            down, right = SIDES[side]
            zone_copy(SIDES.index((-down, -right))).wait_recv()

    spread = jnp.where(iota((LANES, wide), 0) == iota((LANES, wide), 1) // HALO, 1.0, 0.0).astype(BF16)
    table = zone_table()
    for _ in range(3):
        piece = table.astype(BF16)
        weight[...] = dot(piece, spread) if _ == 0 else weight[...] + dot(piece, spread)
        table = table - piece.astype(F32)

    def sweep(tile, window, edges, before, after, ahead=2):
        done = 0
        for u in range(steps):
            before(u)
            while done <= min(u + ahead, steps):
                tile(edges, done)
                done += 1
            window(edges, u)
            after(u)

    def nothing(u):
        return None

    await_halo(dose, 0, (8, 9))
    put_dose(halo_cols[0, 0], HALO, 0)
    put_dose(halo_cols[0, 1], HALO, SIDE + cols)
    sweep(tile_forward, window_forward, 0, lambda u: near.wait() if u == 0 else None, nothing)

    def arrive(turn, field, put, ahead, u):
        chunks = tuple(range(ahead + 1)) if u == 0 else (u + ahead,) if u + ahead < steps else ()
        corners = (10, 12) if u == 0 else (11, 13) if u == steps - ahead else ()
        await_halo(field, turn, (*chunks, *(4 + c for c in chunks), *corners))
        for side, square in ((0, 0), (1, rows // HALO + 1)):
            for c in chunks:
                put(halo_rows[turn, side, :, c * CHUNK : (c + 1) * CHUNK], square, SIDE + c * CHUNK)
            if u == 0:
                put(halo_corners[turn, 2 * side], square, 0)
            if u == steps - ahead:
                put(halo_corners[turn, 2 * side + 1], square, SIDE + cols)

    def send_error(u):
        sides = (8, 10, 12) if u == 0 else (9, 11, 13) if u == steps - 1 else ()
        send(error, 1, (u, 4 + u, *sides))

    sweep(
        tile_forward,
        window_forward,
        1,
        lambda u: arrive(0, dose, lambda value, square, at: put_dose(value, square * HALO, at), 1, u),
        send_error,
        ahead=1,
    )
    await_halo(error, 1, (8, 9))
    for side, at in ((0, 0), (1, SIDE + cols)):
        for square in range(rows // HALO):
            put_part(halo_cols[1, side, square * HALO : (square + 1) * HALO], 1 + square, at)
    sweep(tile_backward, window_backward, 0, nothing, nothing)
    sweep(tile_backward, window_backward, 1, lambda u: arrive(1, error, put_part, 2, u), nothing)
    by_side(range(14), lambda piece: halo_copy(dose, 0, piece).wait_send())
    by_side(range(14), lambda piece: halo_copy(error, 1, piece).wait_send())
    for side in range(8):

        @pl.when(exists(side))
        def _(side=side):
            zone_copy(side).wait_send()


def blur(dims, dose, target, zone, zone_weights, bands):
    rows, cols = dose.shape
    wide, high = cols + 2 * SIDE, rows + 2 * HALO
    vmem = pl.BlockSpec(memory_space=pltpu.VMEM)
    smem = pl.BlockSpec(memory_space=pltpu.SMEM)
    dma = pltpu.SemaphoreType.DMA
    return pl.pallas_call(
        functools.partial(blur_kernel, dims),
        out_shape=[
            jax.ShapeDtypeStruct((rows, cols), F32),
            jax.ShapeDtypeStruct((rows, cols), BF16),
            jax.ShapeDtypeStruct((rows, cols), BF16),
        ],
        in_specs=[vmem, pl.BlockSpec(memory_space=pl.ANY), vmem, smem, *[vmem] * 6],
        out_specs=[vmem] * 3,
        scratch_shapes=[
            pltpu.VMEM((rows, cols), F32),
            dma,
            pltpu.VMEM((8, LANES), I32),
            pltpu.VMEM((8, 8, LANES), I32),
            pltpu.VMEM((2, 2, HALO, cols), F32),
            pltpu.VMEM((2, 2, rows, SIDE), F32),
            pltpu.VMEM((2, 4, HALO, SIDE), F32),
            pltpu.VMEM((high, wide), BF16),
            pltpu.VMEM((high, wide), BF16),
            pltpu.VMEM((3, high, wide), BF16),
            pltpu.VMEM((3, high, wide), BF16),
            pltpu.VMEM((2, 3, 2 * HALO, wide), BF16),
            pltpu.VMEM((2, 3, 2 * HALO, wide), BF16),
            pltpu.VMEM((rows, cols), F32),
            pltpu.VMEM((24, wide), F32),
            dma((2, 14)), dma((2, 14)), dma((8,)), dma((8,)),
        ],
        compiler_params=pltpu.CompilerParams(
            collective_id=1, has_side_effects=True, vmem_limit_bytes=40 * 2**20
        ),
        cost_estimate=cost(25),
        name="blur",
    )(dose, far(target), far(zone), far(zone_weights), *bands)


def per_device(dims, shot_dose, shot_frac, shot_pos, block_count, shot_tile, zone, zone_weights, target):
    n = dims[1]
    rows, cols = target.shape
    count, tile = block_count.reshape(1, -1), shot_tile.reshape(1, -1)
    recv, order, *bands = route(n, cols, shot_dose, shot_frac, shot_pos, count, tile)
    dose, buf, spans = deposit(recv, rows, cols)
    exposure, grad_high, grad_low = blur(dims, dose, target, zone, zone_weights.T, bands)
    slot_grad, exposure = sample(n, grad_high, grad_low, buf, spans, exposure)
    return exposure, give_back(n, slot_grad, tile, order)


def solution(mesh):
    dims = (mesh.shape["row"], mesh.shape["col"])
    return jax.shard_map(
        functools.partial(per_device, dims),
        mesh=mesh,
        in_specs=(
            P(("row", "col"), None),
            P(None, ("row", "col"), None),
            P(("row", "col"), None),
            P(("row", "col")),
            P(("row", "col"), None),
            P("row", "col"),
            P(),
            P("row", "col"),
        ),
        out_specs=(P("row", "col"), P(("row", "col"), None)),
        check_vma=False,
    )
```

```python
import functools
import math

import jax
import jax.numpy as jnp
import numpy as np
from jax import lax
from jax.experimental import pallas as pl
from jax.experimental.pallas import tpu as pltpu
from jax.sharding import PartitionSpec as P

HALO = 64
ZONES = 8
LANES = 128
CHUNK = 256
SHOTS = 512
SIDE = 128
SIGMAS = (0.125 * HALO, 0.25 * HALO, 0.5 * HALO)
MESH = pl.DeviceIdType.MESH
F32, BF16, I32 = jnp.float32, jnp.bfloat16, jnp.int32


def cost(us):
    return pl.CostEstimate(flops=0, bytes_accessed=int(us * 3.0e6), transcendentals=0)


def iota(shape, dim):
    return lax.broadcasted_iota(I32, shape, dim)


def split(x):
    high = x.astype(BF16)
    return high, (x - high.astype(F32)).astype(BF16)


def dot(a, b):
    return jnp.dot(a, b, preferred_element_type=F32)


def dot_nt(a, b):
    return lax.dot_general(a, b, (((1,), (1,)), ((), ())), preferred_element_type=F32)


def pick(onehot, x):
    first = x.astype(BF16)
    rest = x - first.astype(F32)
    second = rest.astype(BF16)
    third = (rest - second.astype(F32)).astype(BF16)
    return dot(onehot, first) + dot(onehot, second) + dot(onehot, third)


def taps(offset, sigma):
    reach = np.arange(-HALO, HALO + 1).astype(np.float64)
    total = float(np.exp(-reach * reach / (2.0 * sigma * sigma)).sum())
    value = jnp.exp(offset * offset * (-1.0 / (2.0 * sigma * sigma))) * (1.0 / total)
    return jnp.where(jnp.abs(offset) <= float(HALO), value, 0.0)


def far(x):
    return pltpu.with_memory_space_constraint(x, pltpu.HBM)


def slots_of(tile, width):
    n = tile.shape[0]
    times = width // n
    own, lane = iota((n, width), 0), iota((n, width), 1)
    other = lane // times
    tile_row = jnp.sum(jnp.where(own == other, tile, 0), axis=0, keepdims=True)
    same = tile == tile_row
    rank_row = jnp.sum(jnp.where(same & (own < other), 1, 0), axis=0, keepdims=True)
    once = lane % times == 0
    rank_col = jnp.sum(jnp.where(same & (other < own) & once, 1, 0), axis=1, keepdims=True)
    return tile * 2 + rank_col, tile_row * 2 + rank_row


def upright(line):
    n = line.shape[1]
    return jnp.sum(jnp.where(iota((n, n), 0) == iota((n, n), 1), line, 0), axis=1, keepdims=True)


def column_class(pixel):
    return 2 * (pixel >> 8) + jnp.where((pixel & (CHUNK - 1)) == CHUNK - 1, 1, 0)


def greet_all(n, me, row):
    barrier = pltpu.get_barrier_semaphore()
    for step in range(1, n):
        peer = (me + step) & (n - 1)
        pl.semaphore_signal(barrier, inc=1, device_id=(row, peer), device_id_type=MESH)
    return barrier


def exchange(n, me, row, source, target, send_sem, recv_sem, meanwhile):
    def copy(peer, source_slots, target_slots):
        return pltpu.make_async_remote_copy(
            src_ref=source.at[source_slots],
            dst_ref=target.at[target_slots],
            send_sem=send_sem,
            recv_sem=recv_sem,
            device_id=(row, peer),
            device_id_type=MESH,
        )

    for step in range(1, n):
        peer = (me + step) & (n - 1)
        copy(peer, peer, me).start()
    target[pl.ds(me, 1)] = source[pl.ds(me, 1)]
    meanwhile()
    every = copy((me + 1) & (n - 1), pl.ds(0, n - 1), pl.ds(0, n - 1))
    every.wait_recv()
    every.wait_send()


def make_bands(mid_high, mid_low, edge_high, edge_low, col_high, col_low):
    for kernel, sigma in enumerate(SIGMAS):
        shape = (2 * HALO, 4 * HALO)
        high, low = split(taps((iota(shape, 1) - iota(shape, 0) - HALO).astype(F32), sigma))
        for band, mid, edges in ((high, mid_high, edge_high), (low, mid_low, edge_low)):
            mid[kernel * 2 * HALO : (kernel + 1) * 2 * HALO] = band
            for e in range(2):
                edges[e, kernel * HALO : (kernel + 1) * HALO] = band[e * HALO : (e + 1) * HALO]
        shape = (2 * CHUNK, CHUNK)
        high, low = split(taps((iota(shape, 0) - iota(shape, 1) - SIDE).astype(F32), sigma))
        col_high[kernel] = high
        col_low[kernel] = low


BANDS = [
    jax.ShapeDtypeStruct(shape, BF16)
    for shape in ((6 * HALO, 4 * HALO), (2, 3 * HALO, 4 * HALO), (3, 2 * CHUNK, CHUNK))
    for _ in range(2)
]


def route_kernel(
    n, cols, dose, frac, pos, count, tile, recv, order, *rest
):
    bands, (parts, ordered, send, send_sem, recv_sem) = rest[:6], rest[6:]
    row, me = lax.axis_index("row"), lax.axis_index("col")
    barrier = greet_all(n, me, row)
    blocks = tile.shape[1]
    live = iota((blocks, LANES), 1) < upright(count[...])
    dead = 2 * (cols // CHUNK) - 1
    kind = jnp.where(live, column_class(jnp.minimum(pos[...] & (cols - 1), cols - 2)), dead)
    masks = [jnp.where(kind == j, 1.0, 0.0) for j in range(dead + 1)]
    before = jnp.where(iota((LANES, LANES), 0) < iota((LANES, LANES), 1), 1.0, 0.0).astype(BF16)
    prefix = dot(jnp.concatenate(masks, axis=0).astype(BF16), before)
    start = jnp.zeros((blocks, 1), F32)
    rank = jnp.zeros((blocks, LANES), F32)
    for j, mask in enumerate(masks):
        rank = rank + mask * (prefix[j * blocks : (j + 1) * blocks] + start)
        start = start + jnp.sum(mask, axis=1, keepdims=True)
    rank = rank.astype(I32)
    order[...] = rank
    fields = [
        jnp.where(live, dose[...], 0.0),
        frac[0],
        frac[1],
        jnp.where(live, pos[...] + 1, 0).astype(F32),
    ]
    for f, field in enumerate(fields):
        for part in range(3):
            piece = field.astype(BF16).astype(F32)
            parts[:, 4 * part + f] = piece
            field = field - piece
        parts[:, 12 + f] = jnp.zeros((blocks, LANES), F32)
    target = iota((LANES, LANES), 0)
    for b in range(blocks):
        moves = jnp.where(target == rank[b : b + 1], 1.0, 0.0).astype(BF16)
        ordered[b] = dot_nt(parts[b].astype(BF16), moves)
    width = 16 * blocks
    _, placed = slots_of(upright(tile[...]), width)
    out, col = iota((8 * n, width), 0), iota((8 * n, width), 1)
    chosen = (out // 4 == placed) & (out % 4 == col % 4) & (col % 16 < 12)
    onehot = jnp.where(chosen, 1.0, 0.0).astype(BF16)
    send[...] = dot(onehot, ordered[...].reshape(width, LANES).astype(BF16)).reshape(n, 8, LANES)
    pl.semaphore_wait(barrier, n - 1)
    exchange(n, me, row, send, recv, send_sem, recv_sem, lambda: make_bands(*bands))


def route(n, cols, dose, frac, pos, count, tile):
    vmem = pl.BlockSpec(memory_space=pltpu.VMEM)
    blocks = tile.shape[1]
    return pl.pallas_call(
        functools.partial(route_kernel, n, cols),
        out_shape=[
            jax.ShapeDtypeStruct((n, 8, LANES), F32),
            jax.ShapeDtypeStruct((blocks, LANES), I32),
            *BANDS,
        ],
        in_specs=[vmem] * 5,
        out_specs=[vmem] * 8,
        scratch_shapes=[
            pltpu.VMEM((blocks, 16, LANES), F32),
            pltpu.VMEM((blocks, 16, LANES), F32),
            pltpu.VMEM((n, 8, LANES), F32),
            pltpu.SemaphoreType.DMA,
            pltpu.SemaphoreType.DMA,
        ],
        compiler_params=pltpu.CompilerParams(
            collective_id=0, has_side_effects=True, vmem_limit_bytes=8 * 2**20
        ),
        cost_estimate=cost(10),
        name="route",
    )(*(far(x) for x in (dose, frac, pos, count, tile)))


def return_kernel(n, grads, tile, order, out, back, send_sem, recv_sem):
    row, me = lax.axis_index("row"), lax.axis_index("col")
    barrier = greet_all(n, me, row)
    blocks = tile.shape[1]
    placed, _ = slots_of(upright(tile[...]), blocks)
    onehot = jnp.where(placed == iota((blocks, 2 * n), 1), 1.0, 0.0).astype(BF16)
    pl.semaphore_wait(barrier, n - 1)
    exchange(n, me, row, grads, back, send_sem, recv_sem, lambda: None)
    found = pick(onehot, jnp.concatenate([back[i] for i in range(n)], axis=0))
    out[...] = jnp.take_along_axis(found, order[...], axis=1)


def give_back(n, grads, tile, order):
    vmem = pl.BlockSpec(memory_space=pltpu.VMEM)
    return pl.pallas_call(
        functools.partial(return_kernel, n),
        out_shape=jax.ShapeDtypeStruct((tile.shape[1], LANES), F32),
        in_specs=[vmem] * 3,
        out_specs=vmem,
        scratch_shapes=[
            pltpu.VMEM((n, 2, LANES), F32),
            pltpu.SemaphoreType.DMA,
            pltpu.SemaphoreType.DMA,
        ],
        compiler_params=pltpu.CompilerParams(
            collective_id=2, has_side_effects=True, vmem_limit_bytes=8 * 2**20
        ),
        cost_estimate=cost(10),
        name="give_back",
    )(grads, far(tile), order)


def shot_rows(buf, first, end):
    lane = iota((8, LANES), 1)
    tiles = [jnp.where(lane < end - i * LANES, buf[first + i], 0.0) for i in range(SHOTS // LANES)]
    line = lambda f: jnp.concatenate([tile[f : f + 1] for tile in tiles], axis=1)
    return line(0), line(1), line(2), line(3).astype(I32) - 1


def table(index, low, high, count):
    here = iota((count, index.shape[1]), 0).astype(F32).astype(BF16)
    first = index.astype(F32).astype(BF16)
    second = (index + 1).astype(F32).astype(BF16)
    at_first, at_second = here == first, here == second
    zero = jnp.zeros((), BF16)
    return [jnp.where(at_first, lo, jnp.where(at_second, hi, zero)) for lo, hi in zip(low, high)]


def col_table(place, frac, cols, window):
    pixel = jnp.minimum(place & (cols - 1), cols - 2)
    local = jnp.clip(pixel - window * CHUNK, -2, CHUNK)
    return table(local, split(1.0 - frac), split(frac), CHUNK)


def tiles_of_bin(n):
    return 2 * n + 2


def deposit_kernel(recv, dose, buf, spans, row_spans, sem):
    n = recv.shape[0]
    rows, cols = dose.shape
    bins = cols // CHUNK
    shift = int(math.log2(cols))
    lane = iota((8, LANES), 1)
    ends = []
    for half in range(2):
        place = recv[:, 4 * half + 3, :].astype(I32) - 1
        kind = column_class(jnp.minimum(place & (cols - 1), cols - 2))
        kind = jnp.where(place >= 0, kind, 2 * bins)
        ends.append([jnp.sum(jnp.where(kind <= j, 1, 0), axis=1, keepdims=True) for j in range(2 * bins)])
    which = iota((n, LANES), 1)
    chosen = (lax.rem(which, n) == iota((n, LANES), 0)) & (which < 2 * n)

    def to_lanes(first, second):
        spread = jnp.where(which < n, first, second)
        return jnp.sum(jnp.where(chosen, spread, 0), axis=0, keepdims=True)

    lines = []
    for q in range(bins):
        lines.append(to_lanes(*(e[2 * q - 2] if q else jnp.zeros((n, 1), I32) for e in ends)))
    for q in range(bins):
        lines.append(to_lanes(*(e[2 * q + 1] for e in ends)) - lines[q])
    row_spans[...] = jnp.concatenate(lines, axis=0)
    copy = pltpu.make_async_copy(row_spans, spans, sem)
    copy.start()
    dose[...] = jnp.zeros_like(dose)
    copy.wait()

    def append(block, begin, amount, carry):
        at, current = carry
        lane_at = at & (LANES - 1)
        moved = pltpu.roll(block, (at - begin) & (LANES - 1), axis=1)
        merged = jnp.where(lane < lane_at, current, moved)
        buf[at >> 7] = merged
        full = jnp.full((8, LANES), lane_at + amount, I32) >= LANES
        return at + amount, jnp.where(full, moved, merged)

    def gather(step, carry):
        for i in range(4):
            block = recv[4 * step + i]
            for half in range(2):
                index = half * n + 4 * step + i
                carry = [
                    append(block, spans[q, index], spans[bins + q, index], carry[q]) for q in range(bins)
                ]
                block = pltpu.roll(block, 4, axis=0)
        return carry

    starts = [q * tiles_of_bin(n) for q in range(bins)]
    empty = jnp.zeros((8, LANES), F32)
    found = lax.fori_loop(0, n // 4, gather, [(jnp.int32(s * LANES), empty) for s in starts])
    most = jnp.int32(0)
    for q, (at, last) in enumerate(found):
        buf[at >> 7] = jnp.where(lane < (at & (LANES - 1)), last, 0.0)
        buf[(at >> 7) + 1] = empty
        most = jnp.maximum(most, (at - starts[q] * LANES + SHOTS - 1) >> SHOTS.bit_length() - 1)
    spans[0, LANES - 1] = most

    def deposit(chunk, carry):
        for q in range(bins):
            first = starts[q] + SHOTS // LANES * chunk
            end = found[q][0] - first * LANES
            amount, frac_row, frac_col, place = shot_rows(buf, first, end)
            pixel_row = jnp.minimum(place >> shift, rows - 2)
            row_high, row_low = table(
                pixel_row, split(amount * (1.0 - frac_row)), split(amount * frac_row), rows
            )
            high, low = col_table(place, frac_col, cols, q)
            dose[:, q * CHUNK : (q + 1) * CHUNK] += (
                dot_nt(row_high, high) + dot_nt(row_low, high) + dot_nt(row_high, low)
            )
        return carry

    lax.fori_loop(0, most, deposit, 0)


def deposit(recv, rows, cols):
    vmem = pl.BlockSpec(memory_space=pltpu.VMEM)
    smem = pl.BlockSpec(memory_space=pltpu.SMEM)
    tiles = (cols // CHUNK) * tiles_of_bin(recv.shape[0])
    spans = (2 * (cols // CHUNK), LANES)
    return pl.pallas_call(
        deposit_kernel,
        out_shape=[
            jax.ShapeDtypeStruct((rows, cols), F32),
            jax.ShapeDtypeStruct((tiles, 8, LANES), F32),
            jax.ShapeDtypeStruct(spans, I32),
        ],
        in_specs=[vmem],
        out_specs=[vmem, vmem, smem],
        scratch_shapes=[pltpu.VMEM(spans, I32), pltpu.SemaphoreType.DMA],
        compiler_params=pltpu.CompilerParams(vmem_limit_bytes=16 * 2**20),
        cost_estimate=cost(8),
        name="deposit",
    )(recv)


def sample_kernel(grad_high, grad_low, buf, spans, exposure, out, exposure_out, values, sem):
    leave = pltpu.make_async_copy(exposure, exposure_out, sem)
    leave.start()
    n = out.shape[0]
    rows, cols = grad_high.shape
    bins = cols // CHUNK
    shift = int(math.log2(cols))
    starts = [q * tiles_of_bin(n) for q in range(bins)]

    def sample(chunk, carry):
        for q in range(bins):
            first = starts[q] + SHOTS // LANES * chunk
            _, frac_row, frac_col, place = shot_rows(buf, first, SHOTS)
            pixel_row = jnp.minimum(place >> shift, rows - 2)
            high, low = col_table(place, frac_col, cols, q)
            window = slice(q * CHUNK, (q + 1) * CHUNK)
            along = (
                dot(grad_high[:, window], high)
                + dot(grad_low[:, window], high)
                + dot(grad_high[:, window], low)
            )
            here = iota((rows, SHOTS), 0)
            weight = jnp.where(
                here == pixel_row, 1.0 - frac_row, jnp.where(here == pixel_row + 1, frac_row, 0.0)
            )
            got = jnp.sum(weight * along, axis=0, keepdims=True)
            for i in range(SHOTS // LANES):
                values[first + i, 0:1] = got[:, i * LANES : (i + 1) * LANES]
        return carry

    lax.fori_loop(0, spans[0, LANES - 1], sample, 0)

    lane = iota((1, LANES), 1)

    def take(begin, amount, at):
        lane_at, tile_at = at & (LANES - 1), at >> 7
        both = jnp.where(lane >= lane_at, values[tile_at, 0:1], values[tile_at + 1, 0:1])
        moved = pltpu.roll(both, (begin - at) & (LANES - 1), axis=1)
        return jnp.where((lane >= begin) & (lane < begin + amount), moved, 0.0)

    def spread(step, at):
        for i in range(8):
            at = spread_one(8 * step + i, at)
        return at

    def spread_one(i, at):
        at = list(at)
        both = []
        for half in range(2):
            total = jnp.zeros((1, LANES), F32)
            for q in range(bins):
                begin, amount = spans[q, half * n + i], spans[bins + q, half * n + i]
                total = total + take(begin, amount, at[q])
                at[q] = at[q] + amount
            both.append(total)
        out[i] = jnp.concatenate(both, axis=0)
        return at

    lax.fori_loop(0, n // 8, spread, [jnp.int32(s * LANES) for s in starts])
    leave.wait()


def sample(n, grad_high, grad_low, buf, spans, exposure):
    vmem = pl.BlockSpec(memory_space=pltpu.VMEM)
    smem = pl.BlockSpec(memory_space=pltpu.SMEM)
    return pl.pallas_call(
        sample_kernel,
        out_shape=[
            jax.ShapeDtypeStruct((n, 2, LANES), F32),
            jax.ShapeDtypeStruct(exposure.shape, F32),
        ],
        in_specs=[vmem, vmem, vmem, smem, pl.BlockSpec(memory_space=pl.ANY)],
        out_specs=[vmem, pl.BlockSpec(memory_space=pl.ANY)],
        scratch_shapes=[pltpu.VMEM(buf.shape, F32), pltpu.SemaphoreType.DMA],
        compiler_params=pltpu.CompilerParams(vmem_limit_bytes=16 * 2**20),
        cost_estimate=cost(8),
        name="sample",
    )(grad_high, grad_low, buf, spans, exposure)


SIDES = ((-1, 0), (1, 0), (0, -1), (0, 1), (-1, -1), (-1, 1), (1, -1), (1, 1))
PIECE_SIDE = (0, 0, 0, 0, 1, 1, 1, 1, 2, 3, 4, 5, 6, 7)
OPPOSITE = (4, 5, 6, 7, 0, 1, 2, 3, 9, 8, 13, 12, 11, 10)


def blur_kernel(
    dims, dose, target_far, zone, zone_weights,
    mid_high, mid_low, edge_high, edge_low, col_high, col_low,
    exposure, grad_high, grad_low,
    target, near_sem,
    zone_own, zone_in, halo_rows, halo_cols, halo_corners, dose_high, dose_low, part_high, part_low,
    mixed_high, mixed_low, error, weight, sends, recvs, zone_send, zone_recv,
):
    n_row, n_col = dims
    rows, cols = dose.shape
    wide = cols + 2 * SIDE
    steps = cols // CHUNK
    row, col = lax.axis_index("row"), lax.axis_index("col")

    def exists(side):
        down, right = SIDES[side]
        tests = []
        if down:
            tests.append(row > 0 if down < 0 else row < n_row - 1)
        if right:
            tests.append(col > 0 if right < 0 else col < n_col - 1)
        return functools.reduce(jnp.logical_and, tests)

    def neighbour(side):
        down, right = SIDES[side]
        return (row + down, col + right)

    def landing(turn, piece):
        if piece < 8:
            return halo_rows.at[turn, piece // 4, :, pl.ds(piece % 4 * CHUNK, CHUNK)]
        if piece < 10:
            return halo_cols.at[turn, piece - 8]
        return halo_corners.at[turn, piece - 10]

    def edge(field, piece):
        down, right = SIDES[PIECE_SIDE[piece]]
        high = pl.ds(0, rows) if not down else (pl.ds(0, HALO) if down < 0 else pl.ds(rows - HALO, HALO))
        if piece < 8:
            across = pl.ds(piece % 4 * CHUNK, CHUNK)
        else:
            across = pl.ds(0, SIDE) if right < 0 else pl.ds(cols - SIDE, SIDE)
        return field.at[high, across]

    def halo_copy(field, turn, piece):
        return pltpu.make_async_remote_copy(
            src_ref=edge(field, piece),
            dst_ref=landing(turn, OPPOSITE[piece]),
            send_sem=sends.at[turn, piece],
            recv_sem=recvs.at[turn, OPPOSITE[piece]],
            device_id=neighbour(PIECE_SIDE[piece]),
            device_id_type=MESH,
        )

    def zone_copy(side):
        down, right = SIDES[side]
        there = SIDES.index((-down, -right))
        return pltpu.make_async_remote_copy(
            src_ref=zone_own,
            dst_ref=zone_in.at[there],
            send_sem=zone_send.at[side],
            recv_sem=zone_recv.at[there],
            device_id=neighbour(side),
            device_id_type=MESH,
        )

    def by_side(pieces, act):
        for side in sorted({PIECE_SIDE[piece] for piece in pieces}, key=[PIECE_SIDE[p] for p in pieces].index):

            @pl.when(exists(side))
            def _(side=side):
                for piece in pieces:
                    if PIECE_SIDE[piece] == side:
                        act(piece)

    def send(field, turn, pieces):
        by_side(pieces, lambda piece: halo_copy(field, turn, piece).start())

    def await_halo(field, turn, pieces):
        by_side(pieces, lambda piece: halo_copy(field, turn, OPPOSITE[piece]).wait_recv())

    barrier = pltpu.get_barrier_semaphore()
    for side in range(8):

        @pl.when(exists(side))
        def _(side=side):
            pl.semaphore_signal(barrier, inc=1, device_id=neighbour(side), device_id_type=MESH)

    near = pltpu.make_async_copy(target_far, target, near_sem)
    near.start()
    zone_own[...] = jnp.zeros_like(zone_own)
    zone_own[0 : zone.shape[0], 0 : zone.shape[1]] = zone[...]
    for side in range(8):

        @pl.when(jnp.logical_not(exists(side)))
        def _(side=side):
            for turn in range(2):
                if side < 2:
                    halo_rows[turn, side] = jnp.zeros((HALO, cols), F32)
                elif side < 4:
                    halo_cols[turn, side - 2] = jnp.zeros((rows, SIDE), F32)
                else:
                    halo_corners[turn, side - 4] = jnp.zeros((HALO, SIDE), F32)
            zone_in[side] = jnp.zeros_like(zone_own)

    tall = 1 + jnp.where(row > 0, 1, 0) + jnp.where(row < n_row - 1, 1, 0)
    broad = 1 + jnp.where(col > 0, 1, 0) + jnp.where(col < n_col - 1, 1, 0)
    pl.semaphore_wait(barrier, tall * broad - 1)
    for side in range(8):

        @pl.when(exists(side))
        def _(side=side):
            zone_copy(side).start()

    send(dose, 0, (8, 9, 0, 1, 4, 5, 11, 13))
    send(dose, 0, (2, 3, 6, 7, 10, 12))

    def put_dose(value, first_row, first_col):
        high, low = split(value)
        here = pl.ds(first_row, value.shape[0]), pl.ds(first_col, value.shape[1])
        dose_high[here] = high
        dose_low[here] = low

    def put_part(value, square, first_col):
        across = pl.ds(first_col, value.shape[1])
        here = pl.ds(square * HALO, HALO)
        for kernel in range(3):
            factor = weight[8 * kernel + square : 8 * kernel + square + 1, across]
            high, low = split(factor * value)
            part_high[kernel, here, across] = high
            part_low[kernel, here, across] = low

    def tile_forward(edges, j):
        tile = pl.ds(j * CHUNK, CHUNK)

        def keep(band_high, band_low, first_row, first_out, count):
            here = pl.ds(first_row, 4 * HALO)
            in_high, in_low = dose_high[here, tile], dose_low[here, tile]
            field = dot(band_high, in_high) + dot(band_low, in_high) + dot(band_high, in_low)
            high, low = split(field)
            for kernel in range(3):
                part = slice(kernel * count, (kernel + 1) * count)
                mixed_high[edges, kernel, first_out : first_out + count, tile] = high[part]
                mixed_low[edges, kernel, first_out : first_out + count, tile] = low[part]

        if edges:
            keep(edge_high[0], edge_low[0], 0, 0, HALO)
            keep(edge_high[1], edge_low[1], 2 * HALO, HALO, HALO)
        else:
            keep(mid_high[...], mid_low[...], HALO, 0, 2 * HALO)

    def along_cols(edges, u, kernel):
        take = pl.ds(u * CHUNK, 2 * CHUNK)
        high, low = mixed_high[edges, kernel, :, take], mixed_low[edges, kernel, :, take]
        both = dot(jnp.concatenate([high, low], axis=0), col_high[kernel])
        return both[: 2 * HALO] + both[2 * HALO :] + dot(high, col_low[kernel])

    def window_forward(edges, u):
        squares = (1, rows // HALO) if edges else (2, 3)
        total = [jnp.zeros((HALO, CHUNK), F32) for _ in range(2)]
        for kernel in range(3):
            field = along_cols(edges, u, kernel)
            for half, square in enumerate(squares):
                line = 8 * kernel + square
                factor = weight[line : line + 1, SIDE + u * CHUNK : SIDE + (u + 1) * CHUNK]
                total[half] = total[half] + factor * field[half * HALO : (half + 1) * HALO]
        for half, square in enumerate(squares):
            here = pl.ds((square - 1) * HALO, HALO), pl.ds(u * CHUNK, CHUNK)
            exposure[here] = total[half]
            wrong = total[half] - target[here]
            error[here] = wrong
            put_part(wrong, square, SIDE + u * CHUNK)

    def tile_backward(edges, j):
        tile = pl.ds(j * CHUNK, CHUNK)

        def keep(kernel, band_high, band_low, first_row, first_out, count):
            here = pl.ds(first_row, 4 * HALO)
            in_high, in_low = part_high[kernel, here, tile], part_low[kernel, here, tile]
            field = dot(band_high, in_high) + dot(band_low, in_high) + dot(band_high, in_low)
            high, low = split(field)
            mixed_high[edges, kernel, first_out : first_out + count, tile] = high
            mixed_low[edges, kernel, first_out : first_out + count, tile] = low

        for kernel in range(3):
            if edges:
                part = pl.ds(kernel * HALO, HALO)
                keep(kernel, edge_high[0, part], edge_low[0, part], 0, 0, HALO)
                keep(kernel, edge_high[1, part], edge_low[1, part], 2 * HALO, HALO, HALO)
            else:
                part = pl.ds(kernel * 2 * HALO, 2 * HALO)
                keep(kernel, mid_high[part], mid_low[part], HALO, 0, 2 * HALO)

    def window_backward(edges, u):
        squares = (1, rows // HALO) if edges else (2, 3)
        high, low = split(sum(along_cols(edges, u, kernel) for kernel in range(3)))
        for half, square in enumerate(squares):
            here = pl.ds((square - 1) * HALO, HALO), pl.ds(u * CHUNK, CHUNK)
            grad_high[here] = high[half * HALO : (half + 1) * HALO]
            grad_low[here] = low[half * HALO : (half + 1) * HALO]

    def zone_table():
        sub, lane = iota((8, LANES), 0), iota((8, LANES), 1)
        high, across = zone.shape
        table = pltpu.roll(pltpu.roll(zone_own[...], 1, axis=0), 2, axis=1)
        for side in range(8):
            down, right = SIDES[side]
            got = pltpu.roll(zone_in[side], (1 + down * high) % 8, axis=0)
            got = pltpu.roll(got, (2 + right * across) % LANES, axis=1)
            row_ok = (sub == 0) if down < 0 else (sub == high + 1) if down > 0 else (sub >= 1) & (sub <= high)
            col_ok = (
                (lane == 1) if right < 0 else (lane == across + 2) if right > 0 else (lane >= 2) & (lane < across + 2)
            )
            table = jnp.where(row_ok & col_ok, got, table)
        picked = []
        for kernel in range(3):
            value = jnp.zeros((8, LANES), F32)
            for z in range(ZONES):
                value = jnp.where(table == z, zone_weights[kernel, z], value)
            picked.append(value)
        return jnp.concatenate(picked, axis=0)

    put_dose(dose[...], HALO, SIDE)
    for side in range(8):

        @pl.when(exists(side))
        def _(side=side):
            down, right = SIDES[side]
            zone_copy(SIDES.index((-down, -right))).wait_recv()

    spread = jnp.where(iota((LANES, wide), 0) == iota((LANES, wide), 1) // HALO, 1.0, 0.0).astype(BF16)
    table = zone_table()
    for _ in range(3):
        piece = table.astype(BF16)
        weight[...] = dot(piece, spread) if _ == 0 else weight[...] + dot(piece, spread)
        table = table - piece.astype(F32)

    def sweep(tile, window, edges, before, after, ahead=2):
        done = 0
        for u in range(steps):
            before(u)
            while done <= min(u + ahead, steps):
                tile(edges, done)
                done += 1
            window(edges, u)
            after(u)

    def nothing(u):
        return None

    await_halo(dose, 0, (8, 9))
    put_dose(halo_cols[0, 0], HALO, 0)
    put_dose(halo_cols[0, 1], HALO, SIDE + cols)
    sweep(tile_forward, window_forward, 0, lambda u: near.wait() if u == 0 else None, nothing)

    def arrive(turn, field, put, ahead, u):
        chunks = tuple(range(ahead + 1)) if u == 0 else (u + ahead,) if u + ahead < steps else ()
        corners = (10, 12) if u == 0 else (11, 13) if u == steps - ahead else ()
        await_halo(field, turn, (*chunks, *(4 + c for c in chunks), *corners))
        for side, square in ((0, 0), (1, rows // HALO + 1)):
            for c in chunks:
                put(halo_rows[turn, side, :, c * CHUNK : (c + 1) * CHUNK], square, SIDE + c * CHUNK)
            if u == 0:
                put(halo_corners[turn, 2 * side], square, 0)
            if u == steps - ahead:
                put(halo_corners[turn, 2 * side + 1], square, SIDE + cols)

    def send_error(u):
        sides = (8, 10, 12) if u == 0 else (9, 11, 13) if u == steps - 1 else ()
        send(error, 1, (u, 4 + u, *sides))

    sweep(
        tile_forward,
        window_forward,
        1,
        lambda u: arrive(0, dose, lambda value, square, at: put_dose(value, square * HALO, at), 1, u),
        send_error,
        ahead=1,
    )
    await_halo(error, 1, (8, 9))
    for side, at in ((0, 0), (1, SIDE + cols)):
        for square in range(rows // HALO):
            put_part(halo_cols[1, side, square * HALO : (square + 1) * HALO], 1 + square, at)
    sweep(tile_backward, window_backward, 0, nothing, nothing)
    sweep(tile_backward, window_backward, 1, lambda u: arrive(1, error, put_part, 1, u), nothing, 1)
    by_side(range(14), lambda piece: halo_copy(dose, 0, piece).wait_send())
    by_side(range(14), lambda piece: halo_copy(error, 1, piece).wait_send())
    for side in range(8):

        @pl.when(exists(side))
        def _(side=side):
            zone_copy(side).wait_send()


def blur(dims, dose, target, zone, zone_weights, bands):
    rows, cols = dose.shape
    wide, high = cols + 2 * SIDE, rows + 2 * HALO
    vmem = pl.BlockSpec(memory_space=pltpu.VMEM)
    smem = pl.BlockSpec(memory_space=pltpu.SMEM)
    dma = pltpu.SemaphoreType.DMA
    return pl.pallas_call(
        functools.partial(blur_kernel, dims),
        out_shape=[
            jax.ShapeDtypeStruct((rows, cols), F32),
            jax.ShapeDtypeStruct((rows, cols), BF16),
            jax.ShapeDtypeStruct((rows, cols), BF16),
        ],
        in_specs=[vmem, pl.BlockSpec(memory_space=pl.ANY), vmem, smem, *[vmem] * 6],
        out_specs=[vmem] * 3,
        scratch_shapes=[
            pltpu.VMEM((rows, cols), F32),
            dma,
            pltpu.VMEM((8, LANES), I32),
            pltpu.VMEM((8, 8, LANES), I32),
            pltpu.VMEM((2, 2, HALO, cols), F32),
            pltpu.VMEM((2, 2, rows, SIDE), F32),
            pltpu.VMEM((2, 4, HALO, SIDE), F32),
            pltpu.VMEM((high, wide), BF16),
            pltpu.VMEM((high, wide), BF16),
            pltpu.VMEM((3, high, wide), BF16),
            pltpu.VMEM((3, high, wide), BF16),
            pltpu.VMEM((2, 3, 2 * HALO, wide), BF16),
            pltpu.VMEM((2, 3, 2 * HALO, wide), BF16),
            pltpu.VMEM((rows, cols), F32),
            pltpu.VMEM((24, wide), F32),
            dma((2, 14)), dma((2, 14)), dma((8,)), dma((8,)),
        ],
        compiler_params=pltpu.CompilerParams(
            collective_id=1, has_side_effects=True, vmem_limit_bytes=40 * 2**20
        ),
        cost_estimate=cost(25),
        name="blur",
    )(dose, far(target), far(zone), far(zone_weights), *bands)


def per_device(dims, shot_dose, shot_frac, shot_pos, block_count, shot_tile, zone, zone_weights, target):
    n = dims[1]
    rows, cols = target.shape
    count, tile = block_count.reshape(1, -1), shot_tile.reshape(1, -1)
    recv, order, *bands = route(n, cols, shot_dose, shot_frac, shot_pos, count, tile)
    dose, buf, spans = deposit(recv, rows, cols)
    exposure, grad_high, grad_low = blur(dims, dose, target, zone, zone_weights.T, bands)
    slot_grad, exposure = sample(n, grad_high, grad_low, buf, spans, exposure)
    return exposure, give_back(n, slot_grad, tile, order)


def solution(mesh):
    dims = (mesh.shape["row"], mesh.shape["col"])
    return jax.shard_map(
        functools.partial(per_device, dims),
        mesh=mesh,
        in_specs=(
            P(("row", "col"), None),
            P(None, ("row", "col"), None),
            P(("row", "col"), None),
            P(("row", "col")),
            P(("row", "col"), None),
            P("row", "col"),
            P(),
            P("row", "col"),
        ),
        out_specs=(P("row", "col"), P(("row", "col"), None)),
        check_vma=False,
    )
```
